32 devices in a mesh: dp: 8 (over y, x, core), tensor: 4 (over z).
Axes of the slice: x: 2, y: 2, z: 4, core: 2. Of those that a mesh axis runs over, the one named last changes fastest.
Arguments:
- text_input: bfloat16 [12288, 768], P('dp'), may hold values from -6 to 6
- layout_input: bfloat16 [12288, 192], P('dp'), may hold values from -6 to 6
- block_starts: int32 [24], P('dp'), may hold values from 0 to 1920
- intersection_flags: int32 [24, 512], P('dp'), may hold values from 0 to 1, as said below
- text_cotangent: bfloat16 [12288, 768], P(('dp', 'tensor')), may hold values from -6 to 6
- layout_cotangent: bfloat16 [12288, 192], P(('dp', 'tensor')), may hold values from -6 to 6
- text_project: bfloat16 [768, 2304], replicated, may hold values from -0.21875 to 0.21875
- text_biases: float32 [4, 768], replicated, may hold values from -4 to 4
- text_dense: bfloat16 [768, 768], replicated, may hold values from -1.75 to 1.75
- text_gains: float32 [2, 768], replicated, may hold values from 0.5 to 1.5
- text_shifts: float32 [2, 768], replicated, may hold values from -4 to 4
- text_widen: bfloat16 [768, 3072], P(None, 'tensor'), may hold values from -0.21875 to 0.21875
- text_hidden_bias: float32 [3072], P('tensor'), may hold values from -4 to 4
- text_narrow: bfloat16 [3072, 768], P('tensor'), may hold values from -0.109375 to 0.109375
- layout_project: bfloat16 [192, 576], replicated, may hold values from -0.4375 to 0.4375
- layout_biases: float32 [4, 192], replicated, may hold values from -4 to 4
- layout_dense: bfloat16 [192, 192], replicated, may hold values from -2.5 to 2.5
- layout_gains: float32 [2, 192], replicated, may hold values from 0.5 to 1.5
- layout_shifts: float32 [2, 192], replicated, may hold values from -4 to 4
- layout_widen: bfloat16 [192, 768], P(None, 'tensor'), may hold values from -0.4375 to 0.4375
- layout_hidden_bias: float32 [768], P('tensor'), may hold values from -4 to 4
- layout_narrow: bfloat16 [768, 192], P('tensor'), may hold values from -0.21875 to 0.21875
Outputs:
- text_result: bfloat16 [12288, 768], P(('dp', 'tensor'))
- layout_result: bfloat16 [12288, 192], P(('dp', 'tensor'))
- text_input_grad: float32 [12288, 768], P('dp')
- layout_input_grad: float32 [12288, 192], P('dp')
- grad_text_project: float32 [768, 2304], replicated
- grad_text_biases: float32 [4, 768], replicated
- grad_text_dense: float32 [768, 768], replicated
- grad_text_gains: float32 [2, 768], replicated
- grad_text_shifts: float32 [2, 768], replicated
- grad_text_widen: float32 [768, 3072], P(None, 'tensor')
- grad_text_hidden_bias: float32 [3072], P('tensor')
- grad_text_narrow: float32 [3072, 768], P('tensor')
- grad_layout_project: float32 [192, 576], replicated
- grad_layout_biases: float32 [4, 192], replicated
- grad_layout_dense: float32 [192, 192], replicated
- grad_layout_gains: float32 [2, 192], replicated
- grad_layout_shifts: float32 [2, 192], replicated
- grad_layout_widen: float32 [192, 768], P(None, 'tensor')
- grad_layout_hidden_bias: float32 [768], P('tensor')
- grad_layout_narrow: float32 [768, 192], P('tensor')
The draws below stay inside these ranges and needn't reach their ends.
Inputs may be any that keep to these rules, and one draw needn't show every extreme that they name: `intersection_flags`: in every block the flagged rows form a leading run.
All inputs are finite; a program needn't handle non-finite values.
Results may differ from the reference program's by a relative error of at most 0.013.
The reference program's roundings to bfloat16 on the way count: a program that leaves them out, or rounds other values in their place, can miss the bound.
Values may be sent and summed in bfloat16 or wider, within the bound.
No kernel may reach another device: no remote copies, remote signals or barrier semaphores. Data moves between devices by JAX's collectives and lax.ppermute only.
A program may use at most 192 MiB of HBM per device.

```python
import math
import jax
import jax.numpy as jnp
from jax import lax

D = 768
L = 192
HEADS = 12
FF = 3072
FFL = 768
BLOCK = 512
DOC = 2048
BLOCKS = 24
TOKENS = 12288


def draw_intersection_flags(key, part):
    key = jax.random.fold_in(key, 7)
    repeated = jax.random.randint(key, (BLOCKS, 1), 0, BLOCK // 2 + 1)
    position = jnp.arange(BLOCK, dtype=jnp.int32)[None, :]
    return (position < repeated).astype(jnp.int32)


def set_ends(values, rng, smallest, largest):
    dims = values.shape
    place = [jax.random.randint(jax.random.fold_in(rng, axis), (), 0, dims[axis]) for axis in range(len(dims))]
    values = values.at[tuple(place)].set(smallest)
    longest = dims.index(max(dims))
    place[longest] = (place[longest] + 1) % dims[longest]
    return values.at[tuple(place)].set(largest)


def steps_of(own_key, extent, pieces, low, high):
    def one(axis_at, parts):
        draws = jax.random.uniform(jax.random.fold_in(jax.random.fold_in(own_key, 6), axis_at), (parts,), jnp.float32, low / len(pieces), high / len(pieces))
        return jnp.repeat(jnp.exp(draws), extent[axis_at] // parts).reshape((-1,) + (1,) * (len(extent) - axis_at - 1))

    level = one(*pieces[0])
    for cut in pieces[1:]:
        level = level * one(*cut)
    return level


def bell_draw(rng, extent, scale, most, cuts=(), held_as=jnp.bfloat16):
    drawn = scale * jax.random.normal(rng, extent, jnp.float32)
    if cuts:
        drawn = drawn * steps_of(rng, extent, cuts, -0.22, 0.18)
    return jnp.clip(drawn, -most, most).astype(held_as)


def setup_inputs(seed: int = 0) -> dict:
    key_list = jax.random.split(jax.random.key(seed), 23)
    return {
        "text_input": bell_draw(key_list[0], (TOKENS, D), 1.0, 6.0, ((0, 8),)),
        "layout_input": bell_draw(key_list[1], (TOKENS, L), 1.0, 6.0, ((0, 8),)),
        "block_starts": set_ends(jax.random.randint(key_list[2], (BLOCKS,), 0, DOC - BLOCK // 4 + 1), jax.random.fold_in(key_list[2], 1), 0, (DOC - BLOCK // 4 + 1) - 1).astype(jnp.int32),
        "intersection_flags": draw_intersection_flags(jax.random.fold_in(key_list[22], 71), 0),
        "text_cotangent": bell_draw(key_list[4], (TOKENS, D), 1.0, 6.0, ((0, 32),)),
        "layout_cotangent": bell_draw(key_list[5], (TOKENS, L), 1.0, 6.0, ((0, 32),)),
        "text_project": bell_draw(key_list[6], (D, 3 * D), D ** -0.5, 0.21875),
        "text_biases": bell_draw(key_list[7], (4, D), 0.3, 4.0, (), jnp.float32),
        "text_dense": bell_draw(key_list[8], (D, D), (D // 64) ** -0.5, 1.75),
        "text_gains": jnp.clip(1.0 + 0.1 * jax.random.normal(key_list[9], (2, D), jnp.float32), 0.5, 1.5),
        "text_shifts": bell_draw(key_list[10], (2, D), 0.3, 4.0, (), jnp.float32),
        "text_widen": bell_draw(key_list[11], (D, FF), D ** -0.5, 0.21875, ((1, 4),)),
        "text_hidden_bias": bell_draw(key_list[12], (FF,), 0.3, 4.0, ((0, 4),), jnp.float32),
        "text_narrow": bell_draw(key_list[13], (FF, D), FF ** -0.5, 0.109375, ((0, 4),)),
        "layout_project": bell_draw(key_list[14], (L, 3 * L), L ** -0.5, 0.4375),
        "layout_biases": bell_draw(key_list[15], (4, L), 0.3, 4.0, (), jnp.float32),
        "layout_dense": bell_draw(key_list[16], (L, L), (L // 32) ** -0.5, 2.5),
        "layout_gains": jnp.clip(1.0 + 0.1 * jax.random.normal(key_list[17], (2, L), jnp.float32), 0.5, 1.5),
        "layout_shifts": bell_draw(key_list[18], (2, L), 0.3, 4.0, (), jnp.float32),
        "layout_widen": bell_draw(key_list[19], (L, FFL), L ** -0.5, 0.4375, ((1, 4),)),
        "layout_hidden_bias": bell_draw(key_list[20], (FFL,), 0.3, 4.0, ((0, 4),), jnp.float32),
        "layout_narrow": bell_draw(key_list[21], (FFL, L), FFL ** -0.5, 0.21875, ((0, 4),)),
    }


@jax.custom_vjp
def low(v):
    return lax.optimization_barrier(v.astype(jnp.bfloat16)).astype(jnp.float32)

@jax.custom_vjp
def low_back(v):
    return v

def low_keep(v):
    return (low(v), None)

def low_pass(kept, grad):
    return (grad,)

def back_keep(v):
    return (v, None)

def back_low(kept, grad):
    return (low(grad),)
low.defvjp(low_keep, low_pass)
low_back.defvjp(back_keep, back_low)
epsilon = 1e-05
highest = lax.Precision.HIGHEST

def layer_norm(values, gain_row, shift_row):
    centre = values - lax.optimization_barrier(jnp.mean(values, axis=-1, keepdims=True))
    spread = lax.optimization_barrier(jnp.mean(centre * centre, axis=-1, keepdims=True))
    return centre * lax.rsqrt(spread + epsilon) * gain_row + shift_row

def attend(block_items):
    text_query, text_key, text_value, layout_query, layout_key, layout_value, valid_keys = block_items
    text_scale = 1.0 / math.sqrt(text_query.shape[-1])
    layout_scale = 1.0 / math.sqrt(layout_query.shape[-1])
    joined = jnp.einsum('qhd,khd->hqk', text_query, text_key, precision=highest) * text_scale
    joined = joined + jnp.einsum('qhd,khd->hqk', layout_query, layout_key, precision=highest) * layout_scale
    joined = low_back(joined)
    masked = jnp.where(valid_keys[None, None, :], joined, -1e+30)
    attention = low(jax.nn.softmax(masked, axis=-1))
    text_context = jnp.einsum('hqk,khd->qhd', attention, text_value, precision=highest)
    layout_context = jnp.einsum('hqk,khd->qhd', attention, layout_value, precision=highest)
    return (text_context, layout_context)

def stream_heads(source, project, biases):
    features = source.shape[1]
    joint_bias = jnp.concatenate([biases[0], jnp.zeros_like(biases[0]), biases[1]])
    projected = low_back(low(jnp.dot(source, project, precision=highest) + joint_bias))
    return projected.reshape(BLOCKS, BLOCK, 3, HEADS, features // HEADS)

def stream_rest(source, context, param_set):
    project, biases, dense, gains, shifts, widen, hidden_bias, narrow = param_set
    features = source.shape[1]
    context = low_back(low(context.reshape(TOKENS, features)))
    branch = low_back(jnp.dot(context, dense, precision=highest) + biases[2])
    first_sum = source + branch
    normed = layer_norm(first_sum, gains[0], shifts[0])
    hidden = low_back(jnp.dot(low(normed), widen, precision=highest) + hidden_bias)
    active = low(jax.nn.gelu(hidden, approximate=False))
    second_sum = normed + low_back(jnp.dot(active, narrow, precision=highest) + biases[3])
    return layer_norm(second_sum, gains[1], shifts[1])

def reference(text_input, layout_input, block_starts, intersection_flags, text_cotangent, layout_cotangent, text_project, text_biases, text_dense, text_gains, text_shifts, text_widen, text_hidden_bias, text_narrow, layout_project, layout_biases, layout_dense, layout_gains, layout_shifts, layout_widen, layout_hidden_bias, layout_narrow):
    position = jnp.arange(BLOCK, dtype=jnp.int32)
    valid_keys = block_starts[:, None] + position[None, :] < DOC
    kept_rows = jnp.logical_and(valid_keys, intersection_flags == 0).reshape(TOKENS).astype(jnp.float32)
    text_set = tuple((member.astype(jnp.float32) for member in (text_project, text_biases, text_dense, text_gains, text_shifts, text_widen, text_hidden_bias, text_narrow)))
    layout_set = tuple((member.astype(jnp.float32) for member in (layout_project, layout_biases, layout_dense, layout_gains, layout_shifts, layout_widen, layout_hidden_bias, layout_narrow)))

    def forward(text_source, layout_source, text_params, layout_params):
        text_heads = stream_heads(text_source, text_params[0], text_params[1])
        layout_heads = stream_heads(layout_source, layout_params[0], layout_params[1])
        block_items = (text_heads[:, :, 0], text_heads[:, :, 1], text_heads[:, :, 2], layout_heads[:, :, 0], layout_heads[:, :, 1], layout_heads[:, :, 2], valid_keys)
        text_context, layout_context = lax.map(jax.checkpoint(attend), block_items)
        return (stream_rest(text_source, text_context, text_params), stream_rest(layout_source, layout_context, layout_params))
    outputs, pullback = jax.vjp(forward, text_input.astype(jnp.float32), layout_input.astype(jnp.float32), text_set, layout_set)
    text_upstream = text_cotangent.astype(jnp.float32) * kept_rows[:, None]
    layout_upstream = layout_cotangent.astype(jnp.float32) * kept_rows[:, None]
    text_dinput, layout_dinput, text_grads, layout_grads = pullback((text_upstream, layout_upstream))
    return (outputs[0].astype(jnp.bfloat16), outputs[1].astype(jnp.bfloat16), text_dinput, layout_dinput, text_grads[0], text_grads[1], text_grads[2], text_grads[3], text_grads[4], text_grads[5], text_grads[6], text_grads[7], layout_grads[0], layout_grads[1], layout_grads[2], layout_grads[3], layout_grads[4], layout_grads[5], layout_grads[6], layout_grads[7])
```

```python
import functools
import math

import jax
import jax.numpy as jnp
from jax import lax
from jax.experimental import pallas as pl
from jax.experimental.pallas import tpu as pltpu
from jax.sharding import PartitionSpec as P

HEADS = 12
DOC = 2048
LANES = 128
epsilon = 1e-05
masked_score = -1e30
F32 = jnp.float32
BF = jnp.bfloat16

OWN, WINDOW, SHIFT, LOCAL, LIMIT, FLAGGED, PLACE = 0, 1, 2, 3, 6, 9, 12
SCALARS = 16


def nn(a, b):
    return lax.dot_general(a, b, (((1,), (0,)), ((), ())), preferred_element_type=F32)


def nt(a, b):
    return lax.dot_general(a, b, (((1,), (1,)), ((), ())), preferred_element_type=F32)


def tn(a, b):
    return lax.dot_general(a, b, (((0,), (0,)), ((), ())), preferred_element_type=F32)


def mean(values):
    return jnp.mean(values, axis=-1, keepdims=True)


def column_sum(values):
    return jnp.sum(values.astype(F32), axis=0, keepdims=True)


def normalised(values):
    centre = values - mean(values)
    scale = lax.rsqrt(mean(centre * centre) + epsilon)
    return centre * scale, scale


def norm_back(upstream, normal, scale, gain_row):
    u = upstream * gain_row
    return scale * (u - mean(u) - normal * mean(u * normal))


def lanes_of(start):
    return pl.ds(pl.multiple_of(start, LANES), LANES)


def head_masks(pair, text_scale, layout_scale):
    lane = lax.broadcasted_iota(jnp.int32, (1, LANES), 1)
    first = 32 * pair - LANES * (pair // 4)
    text_a = jnp.where(lane < 64, text_scale, 0.0)
    text_b = jnp.where(lane < 64, 0.0, text_scale)
    layout_a = jnp.where((lane >= first) & (lane < first + 16), layout_scale, 0.0)
    layout_b = jnp.where((lane >= first + 16) & (lane < first + 32), layout_scale, 0.0)
    return text_a, layout_a, text_b, layout_b


def stack_heads(text, layout, masks):
    text_a, layout_a, text_b, layout_b = (m.astype(BF) for m in masks)
    upper = jnp.concatenate([text * text_a, layout * layout_a], axis=1)
    lower = jnp.concatenate([text * text_b, layout * layout_b], axis=1)
    return jnp.concatenate([upper, lower], axis=0)


def unstack_heads(stacked, masks):
    text_a, layout_a, text_b, layout_b = masks
    upper, lower = stacked[:LANES], stacked[LANES:]
    text = upper[:, :LANES] * text_a + lower[:, :LANES] * text_b
    layout = upper[:, LANES:] * layout_a + lower[:, LANES:] * layout_b
    return text, layout


def pair_scores(stacked, keys, limit):
    scores = nt(stacked, keys)
    key = lax.broadcasted_iota(jnp.int32, (1, scores.shape[1]), 1)
    return jnp.where(key < limit, scores, masked_score)


def attend_kernel(
    info, xt, xl, wt, wl, bt, bl, dense_t, dense_l, gt, st, gl, sl,
    qt, kt, vt, ql, kl, vl, ct, cl, first_t, first_l, low_t, low_l, lse,
    q_scr, k_scr, v_scr, ql_scr, kl_scr, vl_scr, cl_scr,
):
    own_rows, width = first_t.shape
    layout_width = first_l.shape[1]
    wide = ql.shape[1]
    window = kt.shape[0]
    block = window // 2
    own = pl.multiple_of(info[OWN], LANES)
    start = pl.multiple_of(info[WINDOW], LANES)

    for i in range(own_rows // LANES):
        rows = pl.ds(i * LANES, LANES)
        from_rows = pl.ds(pl.multiple_of(own + i * LANES, LANES), LANES)
        q = (nn(xt[from_rows, :], wt[:, :width]) + bt[0:1, :]).astype(BF)
        q_scr[rows, :] = q
        qt[rows, :] = q
        q = (nn(xl[from_rows, :], wl[:, :wide]) + bl[0:1, :]).astype(BF)
        ql_scr[rows, :] = q
        ql[rows, :] = q

    def project(i, carry):
        rows = pl.ds(pl.multiple_of(i * 256, 256), 256)
        from_rows = pl.ds(pl.multiple_of(start + i * 256, 256), 256)
        x = xt[from_rows, :]
        k = nn(x, wt[:, width : 2 * width]).astype(BF)
        k_scr[rows, :] = k
        kt[rows, :] = k
        v = (nn(x, wt[:, 2 * width :]) + bt[1:2, :]).astype(BF)
        v_scr[rows, :] = v
        vt[rows, :] = v
        x = xl[from_rows, :]
        k = nn(x, wl[:, wide : 2 * wide]).astype(BF)
        kl_scr[rows, :] = k
        kl[rows, :] = k
        v = (nn(x, wl[:, 2 * wide :]) + bl[1:2, :]).astype(BF)
        vl_scr[rows, :] = v
        vl[rows, :] = v
        return carry

    lax.fori_loop(0, window // 256, project, 0)
    cl_scr[...] = jnp.zeros_like(cl_scr)
    lse[...] = jnp.zeros_like(lse)
    lane = lax.broadcasted_iota(jnp.int32, (1, LANES), 1)

    def one_pair(pair, carry):
        text_lanes = lanes_of(pair * LANES)
        group_lanes = lanes_of((pair // 4) * LANES)
        scaled = head_masks(pair, 0.125, 0.25)
        plain = head_masks(pair, 1.0, 1.0)
        for j in range(own_rows // LANES):
            rows = pl.ds(j * LANES, LANES)
            keys_at = pl.ds(pl.multiple_of(info[LOCAL + j] * block, block), block)
            stacked = stack_heads(q_scr[rows, text_lanes], ql_scr[rows, group_lanes], scaled)
            keys = jnp.concatenate([k_scr[keys_at, text_lanes], kl_scr[keys_at, group_lanes]], axis=1)
            values = jnp.concatenate([v_scr[keys_at, text_lanes], vl_scr[keys_at, group_lanes]], axis=1)
            scores = pair_scores(stacked, keys, info[LIMIT + j])
            highest = jnp.max(scores, axis=-1, keepdims=True)
            exponent = jnp.exp(scores - highest)
            totals = jnp.sum(exponent, axis=-1, keepdims=True)
            probs = (exponent * (1.0 / totals)).astype(BF)
            text, layout = unstack_heads(nn(probs, values), plain)
            ct[rows, text_lanes] = text.astype(BF)
            cl_scr[rows, group_lanes] += layout
            log_total = highest + jnp.log(totals)
            lse[rows, :] = (
                lse[rows, :]
                + jnp.where(lane == 2 * pair, log_total[:LANES], 0.0)
                + jnp.where(lane == 2 * pair + 1, log_total[LANES:], 0.0)
            )
        return carry

    lax.fori_loop(0, HEADS // 2, one_pair, 0)

    for i in range(own_rows // LANES):
        rows = pl.ds(i * LANES, LANES)
        from_rows = pl.ds(pl.multiple_of(own + i * LANES, LANES), LANES)
        first = xt[from_rows, :].astype(F32) + (nn(ct[rows, :], dense_t[...]) + bt[2:3, :])
        first_t[rows, :] = first
        low_t[rows, :] = (normalised(first)[0] * gt[0:1, :] + st[0:1, :]).astype(BF)
        context = cl_scr[rows, :layout_width].astype(BF)
        cl[rows, :] = context
        first = xl[from_rows, :].astype(F32) + (nn(context, dense_l[...]) + bl[2:3, :layout_width])
        first_l[rows, :] = first
        low_l[rows, :] = (normalised(first)[0] * gl[0:1, :] + sl[0:1, :]).astype(BF)


def gelu_both(hidden):
    below = 0.5 * (1.0 + lax.erf(hidden * math.sqrt(0.5)))
    density = jnp.exp(-0.5 * hidden * hidden) * (1.0 / math.sqrt(2.0 * math.pi))
    return hidden * below, below + hidden * density


def ffn_stream(first, low, widen, hidden_bias, narrow, out_bias, gain, shift, cot, keep, dense, scratch, outs):
    gprime, second = scratch
    result, dout_ref, active, dhid, dfirst, dbranch, dcontext, sums, hidden_sums = outs
    shards = widen.shape[0]
    hid = widen.shape[2]
    wide = dcontext.shape[1]
    width = first.shape[1]
    step = 256 if hid % 256 == 0 else hid
    xh_one, scale_one = normalised(first[...])
    second[...] = xh_one * gain[0:1, :] + shift[0:1, :] + out_bias

    def forward(i, carry):
        for n in range(hid // step):
            cols = pl.ds(n * step, step)
            hidden = nn(low[...], widen[i, :, cols]) + hidden_bias[i, :, cols]
            value, slope = gelu_both(hidden)
            active[i, :, cols] = value.astype(BF)
            gprime[i, :, cols] = slope
        second[...] += nn(active[i], narrow[i])
        return carry

    lax.fori_loop(0, shards, forward, 0)
    xh_two, scale_two = normalised(second[...])
    result[...] = (xh_two * gain[1:2, :] + shift[1:2, :]).astype(BF)
    upstream = cot[...].astype(F32) * keep
    dsecond = norm_back(upstream, xh_two, scale_two, gain[1:2, :])
    dout_ref[...] = dsecond.astype(BF)
    sums[0:1, :] = column_sum(upstream * xh_two)
    sums[1:2, :] = column_sum(upstream)
    sums[2:3, :] = column_sum(dout_ref[...])
    second[...] = dsecond

    def backward(i, carry):
        for n in range(hid // step):
            cols = pl.ds(n * step, step)
            dactive = nt(dout_ref[...], narrow[i, cols, :])
            dhidden = (dactive * gprime[i, :, cols]).astype(BF)
            dhid[i, :, cols] = dhidden
            hidden_sums[i, :, cols] = column_sum(dhidden)
        second[...] += nt(dhid[i], widen[i])
        return carry

    lax.fori_loop(0, shards, backward, 0)
    dnormed = second[...]
    xh_one, scale_one = normalised(first[...])
    back = norm_back(dnormed, xh_one, scale_one, gain[0:1, :])
    sums[3:4, :] = column_sum(dnormed * xh_one)
    sums[4:5, :] = column_sum(dnormed)
    dfirst[...] = back
    dbranch[...] = back.astype(BF)
    sums[5:6, :] = column_sum(dbranch[...])
    sums[6:8, :] = jnp.zeros((2, width), F32)
    dc = nt(dbranch[...], dense[...]).astype(BF)
    dcontext[:, :width] = dc
    if wide > width:
        dcontext[:, width:] = jnp.zeros((dc.shape[0], wide - width), BF)


def ffn_kernel(info, *refs):
    (first_t, low_t, widen_t, hb_t, narrow_t, bt, gt, st, cot_t, dense_t) = refs[:10]
    (first_l, low_l, widen_l, hb_l, narrow_l, bl, gl, sl, cot_l, dense_l) = refs[10:20]
    outs_t, outs_l = refs[20:29], refs[29:38]
    gp_t, sec_t, gp_l, sec_l = refs[38:]
    row = lax.broadcasted_iota(jnp.int32, (LANES, 1), 0)
    keep = []
    for j in range(first_t.shape[0] // LANES):
        place = row + info[PLACE + j]
        keep.append(jnp.where((place >= info[FLAGGED + j]) & (place < info[LIMIT + j]), 1.0, 0.0))
    keep = jnp.concatenate(keep, axis=0)
    ffn_stream(first_t, low_t, widen_t, hb_t, narrow_t, bt[3:4, :], gt, st, cot_t, keep, dense_t, (gp_t, sec_t), outs_t)
    ffn_stream(first_l, low_l, widen_l, hb_l, narrow_l, bl[3:4, :], gl, sl, cot_l, keep, dense_l, (gp_l, sec_l), outs_l)


def weight_grads_kernel(active, dout, low, dhid, active_l, dout_l, low_l, dhid_l, gn, gw, gn_l, gw_l):
    gn[0] = tn(active[0], dout[...]).astype(BF)
    gw[0] = tn(low[...], dhid[0]).astype(BF)
    gn_l[0] = tn(active_l[0], dout_l[...])
    gw_l[0] = tn(low_l[...], dhid_l[0])


def attend_back_kernel(
    info, qt, kt, vt, ql, kl, vl, dct, dcl, lse,
    dq, dk, dv, dq_l, dk_l, dv_l,
    k_acc, v_acc, kl_acc, vl_acc, ql_acc,
):
    own_rows = qt.shape[0]
    window = kt.shape[0]
    block = window // 2
    pad = (dk.shape[0] - window) // 2
    for acc in (k_acc, v_acc, kl_acc, vl_acc, ql_acc):
        acc[...] = jnp.zeros_like(acc)
    for out in (dk, dv, dk_l, dv_l):
        edge = jnp.zeros((pad, out.shape[1]), BF)
        out[:pad, :] = edge
        out[pad + window :, :] = edge
    lane = lax.broadcasted_iota(jnp.int32, (1, LANES), 1)

    def one_pair(pair, carry):
        text_lanes = lanes_of(pair * LANES)
        group_lanes = lanes_of((pair // 4) * LANES)
        scaled = head_masks(pair, 0.125, 0.25)
        plain = head_masks(pair, 1.0, 1.0)
        for j in range(own_rows // LANES):
            rows = pl.ds(j * LANES, LANES)
            keys_at = pl.ds(pl.multiple_of(info[LOCAL + j] * block, block), block)
            stacked = stack_heads(qt[rows, text_lanes], ql[rows, group_lanes], scaled)
            keys = jnp.concatenate([kt[keys_at, text_lanes], kl[keys_at, group_lanes]], axis=1)
            values = jnp.concatenate([vt[keys_at, text_lanes], vl[keys_at, group_lanes]], axis=1)
            dcs = stack_heads(dct[rows, text_lanes], dcl[rows, group_lanes], plain)
            logs = lse[rows, :]
            log_total = jnp.concatenate(
                [
                    jnp.sum(jnp.where(lane == 2 * pair, logs, 0.0), axis=1, keepdims=True),
                    jnp.sum(jnp.where(lane == 2 * pair + 1, logs, 0.0), axis=1, keepdims=True),
                ],
                axis=0,
            )
            probs = jnp.exp(pair_scores(stacked, keys, info[LIMIT + j]) - log_total)
            dprobs = nt(dcs, values)
            inner = jnp.sum(probs * dprobs, axis=1, keepdims=True)
            dscores = (probs * (dprobs - inner)).astype(BF)
            text, layout = unstack_heads(nn(dscores, keys), scaled)
            dq[rows, text_lanes] = text.astype(BF)
            ql_acc[rows, group_lanes] += layout
            both = tn(dscores, stacked)
            k_acc[keys_at, text_lanes] += both[:, :LANES]
            kl_acc[keys_at, group_lanes] += both[:, LANES:]
            both = tn(probs.astype(BF), dcs)
            v_acc[keys_at, text_lanes] += both[:, :LANES]
            vl_acc[keys_at, group_lanes] += both[:, LANES:]
        return carry

    lax.fori_loop(0, HEADS // 2, one_pair, 0)
    middle = pl.ds(pad, window)
    dk[middle, :] = k_acc[...].astype(BF)
    dv[middle, :] = v_acc[...].astype(BF)
    dk_l[middle, :] = kl_acc[...].astype(BF)
    dv_l[middle, :] = vl_acc[...].astype(BF)
    dq_l[...] = ql_acc[...].astype(BF)


def project_back_kernel(
    info, xt, xl, wt, wl, dq, dk, dv, dq_l, dk_l, dv_l, dfirst_t, dfirst_l, ct, cl, db_t, db_l,
    side, own_grad, gp, gd, gp_l, gd_l, sums, sums_l,
):
    own_rows, width = dq.shape
    wide = dq_l.shape[1]
    layout_width = xl.shape[1]
    pad = own_rows
    window = dk.shape[0] - 2 * pad
    own = pl.multiple_of(info[OWN], LANES)
    start = pl.multiple_of(info[WINDOW], LANES)
    shift = pl.multiple_of(info[SHIFT], LANES)

    def rows_grad(at):
        rows = pl.ds(pl.multiple_of(shift + at, LANES), LANES)
        text = nt(dk[rows, :], wt[:, width : 2 * width]) + nt(dv[rows, :], wt[:, 2 * width :])
        layout = nt(dk_l[rows, :], wl[:, wide : 2 * wide]) + nt(dv_l[rows, :], wl[:, 2 * wide :])
        return text, layout

    def part(i, carry):
        at = i * LANES
        to = pl.ds(pl.multiple_of(at, LANES), LANES)
        text, layout = rows_grad(at)
        side[0, to, :width] = text.astype(BF)
        side[0, to, width:] = layout.astype(BF)
        text, layout = rows_grad(at + 2 * own_rows)
        side[1, to, :width] = text.astype(BF)
        side[1, to, width:] = layout.astype(BF)
        text, layout = rows_grad(at + own_rows)
        own_grad[to, :width] = dfirst_t[to, :] + text + nt(dq[to, :], wt[:, :width])
        own_grad[to, width:] = dfirst_l[to, :] + layout + nt(dq_l[to, :], wl[:, :wide])
        return carry

    lax.fori_loop(0, own_rows // LANES, part, 0)
    x_own = xt[pl.ds(own, own_rows), :]
    x_win = xt[pl.ds(start, window), :]
    middle = pl.ds(pad, window)
    gp[0] = tn(x_own, dq[...]).astype(BF)
    gp[1] = tn(x_win, dk[middle, :]).astype(BF)
    gp[2] = tn(x_win, dv[middle, :]).astype(BF)
    gd[...] = tn(ct[...], db_t[...]).astype(BF)
    x_own = xl[pl.ds(own, own_rows), :]
    x_win = xl[pl.ds(start, window), :]
    gp_l[0] = tn(x_own, dq_l[...])
    gp_l[1] = tn(x_win, dk_l[middle, :])
    gp_l[2] = tn(x_win, dv_l[middle, :])
    gd_l[...] = tn(cl[...], db_l[...])
    sums[0:1, :] = column_sum(dq[...])
    sums[1:2, :] = column_sum(dv[middle, :])
    sums_l[0:1, :] = column_sum(dq_l[...])
    sums_l[1:2, :] = column_sum(dv_l[middle, :])


def call(kernel, operands, outs, scratch=(), grid=None, in_specs=None, out_specs=None, flops=0, name=None):
    operands = tuple(operands)
    if in_specs is None:
        in_specs = [pl.BlockSpec(memory_space=pltpu.SMEM)]
        in_specs += [pl.BlockSpec(memory_space=pltpu.VMEM)] * (len(operands) - 1)
    if out_specs is None:
        out_specs = [pl.BlockSpec(memory_space=pltpu.VMEM)] * len(outs)
    moved = sum(math.prod(o.shape) * o.dtype.itemsize for o in tuple(operands) + tuple(outs))
    extra = {} if grid is None else {"grid": grid}
    return pl.pallas_call(
        kernel,
        out_shape=outs,
        in_specs=in_specs,
        out_specs=out_specs,
        scratch_shapes=list(scratch),
        cost_estimate=pl.CostEstimate(flops=flops, bytes_accessed=moved, transcendentals=0),
        compiler_params=pltpu.CompilerParams(vmem_limit_bytes=56 << 20),
        name=name,
        **extra,
    )(*operands)


def shape(dims, dtype=BF):
    return jax.ShapeDtypeStruct(dims, dtype)


def per_device(
    text_input, layout_input, block_starts, intersection_flags, text_cotangent, layout_cotangent,
    text_project, text_biases, text_dense, text_gains, text_shifts, text_widen, text_hidden_bias, text_narrow,
    layout_project, layout_biases, layout_dense, layout_gains, layout_shifts, layout_widen, layout_hidden_bias,
    layout_narrow,
):
    blocks, length = intersection_flags.shape
    total = blocks * length
    groups = lax.axis_size("tensor")
    planes = lax.axis_size("dp")
    own = total // groups
    tiles = own // LANES
    width = text_input.shape[1]
    layout_width = layout_input.shape[1]
    wide = 2 * LANES
    window = 2 * length
    t = lax.axis_index("tensor").astype(jnp.int32)
    me = lax.axis_index("dp").astype(jnp.int32)

    flagged = jnp.sum(intersection_flags, axis=1, dtype=jnp.int32)
    base = jnp.minimum((t * own) // length, blocks - 2)
    tile_rows = t * own + LANES * jnp.arange(tiles, dtype=jnp.int32)
    tile_block = tile_rows // length
    pick = tile_block[:, None] == jnp.arange(blocks, dtype=jnp.int32)[None, :]
    limit = DOC - jnp.sum(jnp.where(pick, block_starts[None, :], 0), axis=1)
    flags_of = jnp.sum(jnp.where(pick, flagged[None, :], 0), axis=1)
    info = jnp.concatenate(
        [
            jnp.stack([t * own, base * length, t * own - base * length]),
            tile_block - base,
            limit,
            flags_of,
            tile_rows - tile_block * length,
            jnp.zeros((1,), jnp.int32),
        ]
    ).astype(jnp.int32)

    piece = text_widen.shape[0] // planes
    mine = jnp.concatenate(
        [
            lax.dynamic_slice_in_dim(text_widen, me * piece, piece, 0),
            lax.dynamic_slice_in_dim(text_narrow, me * piece, piece, 0),
        ],
        axis=0,
    )
    gathered = lax.all_gather(mine, ("tensor", "dp"), axis=0, tiled=False)
    gathered = gathered.reshape(groups, planes, 2, piece, width)
    widen_t = gathered[:, :, 0].reshape(groups, width, -1)
    narrow_t = gathered[:, :, 1].reshape(groups, -1, width)
    small = lax.all_gather(jnp.concatenate([layout_widen, layout_narrow], axis=0), "tensor", axis=0, tiled=False)
    widen_l, narrow_l = small[:, :layout_width], small[:, layout_width:]
    hidden_bias = lax.all_gather(
        jnp.concatenate([text_hidden_bias, layout_hidden_bias])[None, :], "tensor", axis=0, tiled=False
    )
    split = text_hidden_bias.shape[0]
    hb_t, hb_l = hidden_bias[:, :, :split], hidden_bias[:, :, split:]

    def pad_parts(values):
        rows = values.shape[0]
        parts = values.reshape(rows, -1, layout_width)
        return jnp.pad(parts, ((0, 0), (0, 0), (0, wide - layout_width))).reshape(rows, -1)

    wl = pad_parts(layout_project)
    bl = pad_parts(layout_biases)

    qkv_macs = (own + 2 * window) * width * width
    unit = 2 * 36 // groups * length * length * 256
    (qt, kt, vt, ql, kl, vl, ct, cl, first_t, first_l, low_t, low_l, lse) = call(
        attend_kernel,
        (info, text_input, layout_input, text_project, wl, text_biases, bl, text_dense, layout_dense,
         text_gains, text_shifts, layout_gains, layout_shifts),
        (
            shape((own, width)), shape((window, width)), shape((window, width)),
            shape((own, wide)), shape((window, wide)), shape((window, wide)),
            shape((own, width)), shape((own, layout_width)),
            shape((own, width), F32), shape((own, layout_width), F32),
            shape((own, width)), shape((own, layout_width)), shape((own, LANES), F32),
        ),
        scratch=(
            pltpu.VMEM((own, width), BF), pltpu.VMEM((window, width), BF), pltpu.VMEM((window, width), BF),
            pltpu.VMEM((own, wide), BF), pltpu.VMEM((window, wide), BF), pltpu.VMEM((window, wide), BF),
            pltpu.VMEM((own, wide), F32),
        ),
        flops=2 * (qkv_macs + 2 * unit), name="attend",
    )

    hid = text_narrow.shape[0]
    hid_l = layout_narrow.shape[0]
    stream_outs = lambda w, h, pw: (
        shape((own, w)), shape((own, w)), shape((groups, own, h)), shape((groups, own, h)),
        shape((own, w), F32), shape((own, w)), shape((own, pw)), shape((8, w), F32), shape((groups, 1, h), F32),
    )
    outs = call(
        ffn_kernel,
        (info,
         first_t, low_t, widen_t, hb_t, narrow_t, text_biases, text_gains, text_shifts, text_cotangent, text_dense,
         first_l, low_l, widen_l, hb_l, narrow_l, layout_biases, layout_gains, layout_shifts, layout_cotangent,
         layout_dense),
        stream_outs(width, hid, width) + stream_outs(layout_width, hid_l, wide),
        scratch=(
            pltpu.VMEM((groups, own, hid), F32), pltpu.VMEM((own, width), F32),
            pltpu.VMEM((groups, own, hid_l), F32), pltpu.VMEM((own, layout_width), F32),
        ),
        flops=2 * 4 * groups * own * width * hid, name="feed_forward",
    )
    result_t, dout_t, active_t, dhid_t, dfirst_t, db_t, dc_t, sums_t, hsum_t = outs[:9]
    result_l, dout_l, active_l, dhid_l, dfirst_l, db_l, dc_l, sums_l, hsum_l = outs[9:]

    vm = lambda block, index: pl.BlockSpec(block, index)
    whole = lambda w: vm((own, w), lambda k: (0, 0))
    shard = lambda *dims: vm((1, *dims), lambda k: (k, 0, 0))
    gn, gw, gn_l, gw_l = call(
        weight_grads_kernel,
        (active_t, dout_t, low_t, dhid_t, active_l, dout_l, low_l, dhid_l),
        (shape((groups, hid, width)), shape((groups, width, hid)),
         shape((groups, hid_l, layout_width), F32), shape((groups, layout_width, hid_l), F32)),
        grid=(groups,),
        in_specs=[shard(own, hid), whole(width), whole(width), shard(own, hid),
                  shard(own, hid_l), whole(layout_width), whole(layout_width), shard(own, hid_l)],
        out_specs=[shard(hid, width), shard(width, hid), shard(hid_l, layout_width), shard(layout_width, hid_l)],
        flops=2 * 2 * groups * own * width * hid, name="weight_grads",
    )

    padded = window + 2 * own
    dq, dk, dv, dq_l, dk_l, dv_l = call(
        attend_back_kernel,
        (info, qt, kt, vt, ql, kl, vl, dc_t, dc_l, lse),
        (shape((own, width)), shape((padded, width)), shape((padded, width)),
         shape((own, wide)), shape((padded, wide)), shape((padded, wide))),
        scratch=(pltpu.VMEM((window, width), F32), pltpu.VMEM((window, width), F32),
                 pltpu.VMEM((window, wide), F32), pltpu.VMEM((window, wide), F32), pltpu.VMEM((own, wide), F32)),
        flops=2 * 5 * unit, name="attend_back",
    )
    side, own_grad, gp, gd, gp_l, gd_l, psums_t, psums_l = call(
        project_back_kernel,
        (info, text_input, layout_input, text_project, wl, dq, dk, dv, dq_l, dk_l, dv_l, dfirst_t, dfirst_l,
         ct, cl, db_t, db_l),
        (shape((2, own, width + layout_width)), shape((own, width + layout_width), F32),
         shape((3, width, width)), shape((width, width)),
         shape((3, layout_width, wide), F32), shape((layout_width, layout_width), F32),
         shape((2, width), F32), shape((2, wide), F32)),
        flops=2 * 2 * qkv_macs, name="project_back",
    )

    to_left = [(i + 1, i) for i in range(groups - 1)]
    to_right = [(i, i + 1) for i in range(groups - 1)]
    from_right = lax.ppermute(side[0], "tensor", to_left)
    from_left = lax.ppermute(side[1], "tensor", to_right)
    own_sum = (own_grad + from_right.astype(F32) + from_left.astype(F32)).astype(BF)
    all_rows = lax.all_gather(own_sum, "tensor", axis=0, tiled=True).astype(F32)
    text_grad, layout_grad = all_rows[:, :width], all_rows[:, width:]

    both = ("tensor", "dp")
    sharded = jnp.concatenate([gn, gw], axis=1).reshape(-1, width)
    sharded = lax.psum_scatter(sharded, both, scatter_dimension=0, tiled=True)
    sharded = lax.all_gather(sharded, "dp", axis=0, tiled=True).astype(F32)
    g_narrow, g_widen = sharded[:hid], sharded[hid:]
    copied = jnp.concatenate([gp.reshape(-1, width), gd], axis=0)
    copied = lax.psum(copied, both).astype(F32)
    g_project = jnp.concatenate([copied[i * width : (i + 1) * width] for i in range(3)], axis=1)
    g_dense = copied[3 * width :]

    w = layout_width
    small = lax.psum((gn_l, gw_l, gp_l[:, :, :w], gd_l, sums_t, hsum_t, sums_l, hsum_l, psums_t, psums_l[:, :w]), both)
    gn_l, gw_l, gp_l, gd_l, sums_t, hsum_t, sums_l, hsum_l, psums_t, psums_l = small
    at = lambda v: lax.dynamic_index_in_dim(v, t, 0, keepdims=False)
    g_project_l = jnp.concatenate([gp_l[0], gp_l[1], gp_l[2]], axis=1)

    def vectors(sums, psums):
        biases = jnp.stack([psums[0], psums[1], sums[5], sums[2]])
        return biases, jnp.stack([sums[3], sums[0]]), jnp.stack([sums[4], sums[1]])

    bias_t, gain_t, shift_t = vectors(sums_t, psums_t)
    bias_l, gain_l, shift_l = vectors(sums_l, psums_l)
    return (
        result_t, result_l, text_grad, layout_grad,
        g_project, bias_t, g_dense, gain_t, shift_t, g_widen, at(hsum_t)[0], g_narrow,
        g_project_l, bias_l, gd_l, gain_l, shift_l, at(gw_l), at(hsum_l)[0], at(gn_l),
    )


def solution(mesh):
    rows = P(("dp", "tensor"), None)
    weights = (P(), P(), P(), P(), P(), P(None, "tensor"), P("tensor"), P("tensor", None))
    return jax.shard_map(
        per_device,
        mesh=mesh,
        in_specs=(P("dp", None), P("dp", None), P("dp"), P("dp", None), rows, rows) + weights + weights,
        out_specs=(rows, rows, P("dp", None), P("dp", None)) + weights + weights,
        check_vma=False,
    )
```

```python
import functools
import math

import jax
import jax.numpy as jnp
from jax import lax
from jax.experimental import pallas as pl
from jax.experimental.pallas import tpu as pltpu
from jax.sharding import PartitionSpec as P

HEADS = 12
DOC = 2048
LANES = 128
epsilon = 1e-05
masked_score = -1e30
F32 = jnp.float32
BF = jnp.bfloat16

OWN, WINDOW, SHIFT, LOCAL, LIMIT, FLAGGED, PLACE, GROUP, HALF, PIECE, SLOT = 0, 1, 2, 3, 6, 9, 12, 15, 16, 18, 22
PIECES = 8
VMEM_LIMIT = 56 << 20
PER_MICROSECOND = 1e9
MICROSECONDS = {
    "pack": 2, "project": 9, "attend": 11, "first_norm": 7, "shard": 6, "turn": 24, "lower": 5, "ffn_keep": 9,
    "attend_back": 20, "sides": 7, "copied_send": 11, "own": 7, "copied_keep": 9, "input_final": 3,
    "ffn_spread": 3, "ffn_final": 4, "copied_spread": 2, "copied_final": 8,
}


def nn(a, b):
    return lax.dot_general(a, b, (((1,), (0,)), ((), ())), preferred_element_type=F32)


def nt(a, b):
    return lax.dot_general(a, b, (((1,), (1,)), ((), ())), preferred_element_type=F32)


def tn(a, b):
    return lax.dot_general(a, b, (((0,), (0,)), ((), ())), preferred_element_type=F32)


def mean(values):
    return jnp.mean(values, axis=-1, keepdims=True)


def column_sum(values):
    return jnp.sum(values.astype(F32), axis=0, keepdims=True)


def normalised(values):
    centre = values - mean(values)
    scale = lax.rsqrt(mean(centre * centre) + epsilon)
    return centre * scale, scale


def norm_back(upstream, normal, scale, gain_row):
    u = upstream * gain_row
    return scale * (u - mean(u) - normal * mean(u * normal))


def lanes_of(start):
    return pl.ds(pl.multiple_of(start, LANES), LANES)


def head_masks(pair, text_scale, layout_scale):
    lane = lax.broadcasted_iota(jnp.int32, (1, LANES), 1)
    first = 32 * pair - LANES * (pair // 4)
    text_a = jnp.where(lane < 64, text_scale, 0.0)
    text_b = jnp.where(lane < 64, 0.0, text_scale)
    layout_a = jnp.where((lane >= first) & (lane < first + 16), layout_scale, 0.0)
    layout_b = jnp.where((lane >= first + 16) & (lane < first + 32), layout_scale, 0.0)
    return text_a, layout_a, text_b, layout_b


def stack_heads(text, layout, masks):
    text_a, layout_a, text_b, layout_b = (m.astype(BF) for m in masks)
    upper = jnp.concatenate([text * text_a, layout * layout_a], axis=1)
    lower = jnp.concatenate([text * text_b, layout * layout_b], axis=1)
    return jnp.concatenate([upper, lower], axis=0)


def unstack_heads(stacked, masks):
    text_a, layout_a, text_b, layout_b = masks
    upper, lower = stacked[:LANES], stacked[LANES:]
    text = upper[:, :LANES] * text_a + lower[:, :LANES] * text_b
    layout = upper[:, LANES:] * layout_a + lower[:, LANES:] * layout_b
    return text, layout


def pair_scores(stacked, keys, limit):
    scores = nt(stacked, keys)
    key = lax.broadcasted_iota(jnp.int32, (1, scores.shape[1]), 1)
    return jnp.where(key < limit, scores, masked_score)


def pack_kernel(info, widen, narrow, widen_l, narrow_l, bias, mine, small, hidden):
    rows = piece_rows(info, 0)
    mine[0] = widen[rows, :]
    mine[1] = narrow[rows, :]
    width_l = widen_l.shape[0]
    small[:, width_l:] = jnp.zeros((small.shape[0], small.shape[1] - width_l), BF)
    small[:width_l, :width_l] = widen_l[...]
    small[width_l:, :width_l] = narrow_l[...]
    high = bias[...].astype(BF).astype(F32)
    middle = (bias[...] - high).astype(BF).astype(F32)
    low = bias[...] - high - middle
    upper = jnp.concatenate([high, middle], axis=0)
    hidden[...] = jnp.concatenate([upper, jnp.concatenate([low, jnp.zeros_like(low)], axis=0)], axis=1).astype(BF)


def biases_of(hidden):
    split = hidden[...].astype(F32)
    rows = split[:8, :LANES] + split[8:, :LANES] + split[:8, LANES:]
    text = jnp.concatenate([rows[i : i + 1] for i in range(6)], axis=1)
    layout = jnp.concatenate([rows[i : i + 1] for i in (6, 7)], axis=1)
    return text, layout


def identity(size):
    row = lax.broadcasted_iota(jnp.int32, (size, size), 0)
    column = lax.broadcasted_iota(jnp.int32, (size, size), 1)
    return jnp.where(row == column, 1.0, 0.0).astype(BF)


def project_kernel(info, xt, xlt, wt, wl, bt, bl, qt, kt, vt, ql, kl, vl, xl_own, wide_l):
    own_rows, width = qt.shape
    wide = ql.shape[1]
    width_l = wl.shape[0]
    own = pl.multiple_of(info[OWN], LANES)
    start = pl.multiple_of(info[WINDOW], LANES)
    rows = pl.ds(own, own_rows)
    for i in range(3):
        wide_l[:, i * wide : i * wide + width_l] = wl[:, i * width_l : (i + 1) * width_l]
        wide_l[:, i * wide + width_l : (i + 1) * wide] = jnp.zeros((width_l, wide - width_l), BF)
    edge = jnp.zeros((1, wide - width_l), F32)
    bias = [jnp.concatenate([bl[i : i + 1, :], edge], axis=1) for i in (0, 1)]
    qt[...] = (nn(xt[rows, :], wt[:, :width]) + bt[0:1, :]).astype(BF)
    ql[...] = (tn(xlt[:, rows], wide_l[:, :wide]) + bias[0]).astype(BF)
    xl_own[...] = tn(xlt[:, rows], identity(width_l)).astype(BF)

    def part(i, carry):
        rows = pl.ds(pl.multiple_of(i * 256, 256), 256)
        from_rows = pl.ds(pl.multiple_of(start + i * 256, 256), 256)
        x = xt[from_rows, :]
        kt[rows, :] = nn(x, wt[:, width : 2 * width]).astype(BF)
        vt[rows, :] = (nn(x, wt[:, 2 * width :]) + bt[1:2, :]).astype(BF)
        x = xlt[:, from_rows]
        kl[rows, :] = tn(x, wide_l[:, wide : 2 * wide]).astype(BF)
        vl[rows, :] = (tn(x, wide_l[:, 2 * wide :]) + bias[1]).astype(BF)
        return carry

    lax.fori_loop(0, kt.shape[0] // 256, part, 0)


def attend_kernel(info, qt, kt, vt, ql, kl, vl, ct, cl, lse, cl_acc):
    own_rows, layout_width = cl.shape
    block = kt.shape[0] // 2
    cl_acc[...] = jnp.zeros_like(cl_acc)
    lse[...] = jnp.zeros_like(lse)
    lane = lax.broadcasted_iota(jnp.int32, (1, LANES), 1)

    def one_pair(pair, carry):
        text_lanes = lanes_of(pair * LANES)
        group_lanes = lanes_of((pair // 4) * LANES)
        scaled = head_masks(pair, 0.125, 0.25)
        plain = head_masks(pair, 1.0, 1.0)
        for j in range(own_rows // LANES):
            rows = pl.ds(j * LANES, LANES)
            keys_at = pl.ds(pl.multiple_of(info[LOCAL + j] * block, block), block)
            stacked = stack_heads(qt[rows, text_lanes], ql[rows, group_lanes], scaled)
            keys = jnp.concatenate([kt[keys_at, text_lanes], kl[keys_at, group_lanes]], axis=1)
            values = jnp.concatenate([vt[keys_at, text_lanes], vl[keys_at, group_lanes]], axis=1)
            scores = pair_scores(stacked, keys, info[LIMIT + j])
            highest = jnp.max(scores, axis=-1, keepdims=True)
            exponent = jnp.exp(scores - highest)
            totals = jnp.sum(exponent, axis=-1, keepdims=True)
            probs = (exponent * (1.0 / totals)).astype(BF)
            text, layout = unstack_heads(nn(probs, values), plain)
            ct[rows, text_lanes] = text.astype(BF)
            cl_acc[rows, group_lanes] += layout
            log_total = highest + jnp.log(totals)
            lse[rows, :] = (
                lse[rows, :]
                + jnp.where(lane == 2 * pair, log_total[:LANES], 0.0)
                + jnp.where(lane == 2 * pair + 1, log_total[LANES:], 0.0)
            )
        return carry

    lax.fori_loop(0, HEADS // 2, one_pair, 0)
    cl[...] = cl_acc[:, :layout_width].astype(BF)


def gelu_both(hidden):
    below = 0.5 * (1.0 + lax.erf(hidden * math.sqrt(0.5)))
    density = jnp.exp(-0.5 * hidden * hidden) * (1.0 / math.sqrt(2.0 * math.pi))
    return hidden * below, below + hidden * density


def shard_forward(low, widen, bias, narrow, active, slope, total):
    hid = widen.shape[1]
    step = 256 if hid % 256 == 0 else hid
    for n in range(hid // step):
        cols = slice(n * step, (n + 1) * step)
        value, gradient = gelu_both(nn(low[...], widen[:, cols]) + bias[:, cols])
        active[:, cols] = value.astype(BF)
        slope[:, cols] = gradient
    total[...] += nn(active[...], narrow[...])


def shard_backward(dout, narrow, slope, widen, dhid, sums, total):
    hid = widen.shape[1]
    step = 256 if hid % 256 == 0 else hid
    for n in range(hid // step):
        cols = slice(n * step, (n + 1) * step)
        dhidden = (nt(dout[...], narrow[cols, :]) * slope[:, cols]).astype(BF)
        dhid[:, cols] = dhidden
        sums[:, cols] = column_sum(dhidden)
    total[...] += nt(dhid[...], widen[...])


def first_norm_kernel(
    info, xt, xl_own, ct, cl, dense_t, dense_l, bt, bl, gt, st, gl, sl, widen, hidden, narrow,
    first_t, first_l, low_t, low_l, normed_l, active, slope, total,
):
    own_rows, width = first_t.shape
    rows = pl.ds(pl.multiple_of(info[OWN], LANES), own_rows)
    first = xt[rows, :].astype(F32) + (nn(ct[...], dense_t[...]) + bt[2:3, :])
    first_t[...] = first
    normed = normalised(first)[0] * gt[0:1, :] + st[0:1, :]
    low_t[...] = normed.astype(BF)
    total[...] = normed + bt[3:4, :]
    first = xl_own[...].astype(F32) + (nn(cl[...], dense_l[...]) + bl[2:3, :])
    first_l[...] = first
    normed = normalised(first)[0] * gl[0:1, :] + sl[0:1, :]
    low_l[...] = normed.astype(BF)
    normed_l[...] = normed + bl[3:4, :]
    shard_forward(low_t, widen, biases_of(hidden)[0], narrow, active, slope, total)


def piece_rows(info, rel):
    return pl.ds(pl.multiple_of(info[HALF + rel // 4] + info[PIECE + rel % 4], 32), 96)


def load_shard(info, plan, refs, weights, sems, at):
    copies = []
    for i, (rel, low, high) in enumerate(plan):
        copy = pltpu.make_async_copy(
            refs[i], weights.at[at, pl.ds(low, high - low), piece_rows(info, rel), :], sems.at[at, i]
        )
        copy.start()
        copies.append(copy)
    return copies


def shard_kernel(plan, info, low, total_in, hidden, *refs):
    pieces = refs[: len(plan)]
    active, slope, total, weights, sems = refs[len(plan) :]
    copies = load_shard(info, plan, pieces, weights, sems, 0)
    total[...] = total_in[...]
    for copy in copies:
        copy.wait()
    shard_forward(low, weights.at[0, 0], biases_of(hidden)[0], weights.at[0, 1], active, slope, total)


def upper_back(total, gain, shift, cot, keep, result, dout, sums):
    normal, scale = normalised(total[...])
    result[...] = (normal * gain[1:2, :] + shift[1:2, :]).astype(BF)
    upstream = cot.astype(F32) * keep
    dsecond = norm_back(upstream, normal, scale, gain[1:2, :])
    dout[...] = dsecond.astype(BF)
    sums[0:1, :] = column_sum(upstream * normal)
    sums[1:2, :] = column_sum(upstream)
    sums[2:3, :] = column_sum(dout[...])
    sums[3:4, :] = jnp.zeros_like(sums[3:4, :])
    total[...] = dsecond


def turn_kernel(plans, info, *refs):
    refs = list(refs)
    take = lambda n: [refs.pop(0) for _ in range(n)]
    low, total_in, gain, shift, cot, widen_own, narrow_own = take(7)
    slopes_in, actives = take(3), take(3)
    low_l, normed_l, gain_l, shift_l, cot_lt = take(5)
    small, hidden = take(4), take(4)
    pieces = [take(len(plan)) for plan in plans]
    result, dout, dhid, dnormed, sums, hsums, active = take(7)
    result_lt, dnormed_l, sums_l, hsums_l = take(4)
    send_a, send_b, pack = take(3)
    weights, slope, slope_l, active_l, dhid_l, dout_l, result_l, grad, sems = take(9)
    shards = dhid.shape[0]
    copies = [load_shard(info, plan, piece, weights, sems, s) for s, (plan, piece) in enumerate(zip(plans, pieces))]
    dnormed[...] = total_in[...]
    dnormed_l[...] = normed_l[...]
    row = lax.broadcasted_iota(jnp.int32, (LANES, 1), 0)
    keep = []
    for j in range(low.shape[0] // LANES):
        place = row + info[PLACE + j]
        keep.append(jnp.where((place >= info[FLAGGED + j]) & (place < info[LIMIT + j]), 1.0, 0.0))
    keep = jnp.concatenate(keep, axis=0)

    width_l = low_l.shape[1]
    for s in range(shards):
        widen, narrow = (small[s][i * width_l : (i + 1) * width_l, :width_l] for i in (0, 1))
        shard_forward(low_l, widen, biases_of(hidden[s])[1][:, :width_l], narrow, active_l.at[s], slope_l.at[s], dnormed_l)
    cot_l = tn(cot_lt[...], identity(width_l))
    upper_back(dnormed_l, gain_l, shift_l, cot_l, keep, result_l, dout_l, sums_l)
    result_lt[...] = nt(identity(width_l), result_l[...]).astype(BF)
    for s in range(shards):
        widen, narrow = (small[s][i * width_l : (i + 1) * width_l, :width_l] for i in (0, 1))
        shard_backward(dout_l, narrow, slope_l.at[s], widen, dhid_l.at[s], hsums_l.at[s], dnormed_l)
    for s in range(shards):
        pack[s] = jnp.zeros_like(pack[s])
        g = tn(active_l[s], dout_l[...]).astype(BF)
        pack[s, :128, :width_l] = g[:128]
        pack[s, :64, 512 : 512 + width_l] = g[128:]
        g = tn(low_l[...], dhid_l[s]).astype(BF)
        pack[s, :128, 256 : 256 + width_l] = g[:128]
        pack[s, 64:, 512 : 512 + width_l] = g[128:]

    for copy in copies[1]:
        copy.wait()
    shard_forward(low, weights.at[1, 0], biases_of(hidden[2])[0], weights.at[1, 1], active, slope, dnormed)
    upper_back(dnormed, gain, shift, cot[...], keep, result, dout, sums)
    shard_backward(dout, narrow_own, slopes_in[0], widen_own, dhid.at[0], hsums.at[0], dnormed)
    for copy in copies[0] + copies[2]:
        copy.wait()
    shard_backward(dout, weights.at[0, 1], slopes_in[1], weights.at[0, 0], dhid.at[1], hsums.at[1], dnormed)
    shard_backward(dout, weights.at[1, 1], slope, weights.at[1, 0], dhid.at[2], hsums.at[2], dnormed)
    shard_backward(dout, weights.at[2, 1], slopes_in[2], weights.at[2, 0], dhid.at[3], hsums.at[3], dnormed)

    half = pl.ds(pl.multiple_of(info[HALF + 1], LANES), grad.shape[0])
    for s, act in enumerate((actives[0], actives[1], active, actives[2])):
        grad[...] = tn(act[:, half], dout[...])

        def store_a(rel, rows, s=s):
            send_a[s, rel % 2, rel // 2, :96] = rows.astype(BF)
            send_a[s, rel % 2, rel // 2, 96:] = pack[s, extra_rows(info, 1, rel), :]

        pieces_of(info, grad, store_a)
        grad[...] = tn(low[:, half], dhid[s])

        def store_b(rel, rows, s=s):
            send_b[s, rel // 2, rel % 2] = rows.astype(BF)

        pieces_of(info, grad, store_b)


def lower_back(first, dnormed, gain, dense, dfirst, dbranch, dcontext, sums):
    width = first.shape[1]
    wide = dcontext.shape[1]
    normal, scale = normalised(first[...])
    back = norm_back(dnormed[...], normal, scale, gain[0:1, :])
    sums[0:1, :] = column_sum(dnormed[...] * normal)
    sums[1:2, :] = column_sum(dnormed[...])
    dfirst[...] = back
    dbranch[...] = back.astype(BF)
    sums[2:3, :] = column_sum(dbranch[...])
    sums[3:4, :] = jnp.zeros_like(sums[3:4, :])
    dc = nt(dbranch[...], dense[...]).astype(BF)
    dcontext[:, :width] = dc
    if wide > width:
        dcontext[:, width:] = jnp.zeros((dc.shape[0], wide - width), BF)


def lower_kernel(
    info, first, dnormed, gain, dense, first_l, dnormed_l, gain_l, dense_l,
    dfirst, dbranch, dcontext, sums, dfirst_lt, dbranch_l, dcontext_l, sums_l, dfirst_l,
):
    lower_back(first, dnormed, gain, dense, dfirst, dbranch, dcontext, sums)
    lower_back(first_l, dnormed_l, gain_l, dense_l, dfirst_l, dbranch_l, dcontext_l, sums_l)
    dfirst_lt[...] = jnp.transpose(dfirst_l[...])


EXTRA = 16


def extra_rows(info, half, rel):
    return pl.ds(pl.multiple_of((info[HALF + half] + info[PIECE + rel]) // 6, EXTRA), EXTRA)


def pieces_of(info, grad, store):
    for rel in range(4):
        store(rel, grad[pl.ds(pl.multiple_of(info[PIECE + rel], 32), 96), :])


def ffn_keep_kernel(
    info, a0, a1, a2, a3, dout, low, dhid, recv_a, recv_b, pack, next_a, keep_a, next_b, keep_b, grad,
):
    half = pl.ds(pl.multiple_of(info[HALF], LANES), grad.shape[0])
    for s, active in enumerate((a0, a1, a2, a3)):
        grad[...] = tn(active[:, half], dout[...])

        def store_a(rel, rows, s=s):
            to = next_a if rel % 2 else keep_a
            recv = recv_a[s, rel % 2, rel // 2].astype(F32)
            to[rel // 2, s, :96] = (rows + recv[:96]).astype(BF)
            to[rel // 2, s, 96:] = (pack[s, extra_rows(info, 0, rel), :].astype(F32) + recv[96:]).astype(BF)

        pieces_of(info, grad, store_a)
        grad[...] = tn(low[:, half], dhid[s])

        def store_b(rel, rows, s=s):
            to = next_b if rel // 2 else keep_b
            to[rel % 2, s] = (rows + recv_b[s, rel // 2, rel % 2].astype(F32)).astype(BF)

        pieces_of(info, grad, store_b)


def add(a, b, *more):
    total = a.astype(F32) + b.astype(F32)
    for value in more:
        total = total + value.astype(F32)
    return total.astype(BF)


def add_split(keep, recv):
    return add(keep[1], recv[1]), add(keep[0], recv[0])


def ffn_spread_kernel(info, keep_a, recv_a, keep_b, recv_b, *outs):
    rows = keep_a.shape[1]
    for k, out in enumerate(outs):
        out[:rows] = (keep_a[k].astype(F32) + recv_a[k].astype(F32)).astype(out.dtype)
        out[rows:] = (keep_b[k].astype(F32) + recv_b[k].astype(F32)).astype(out.dtype)


def copied_spread_kernel(info, keep_a, recv_a, keep_b, recv_b, *outs):
    for k, out in enumerate(outs):
        keep, recv = (keep_a, recv_a) if k < 2 else (keep_b, recv_b)
        out[...] = (keep[k % 2].astype(F32) + recv[k % 2].astype(F32)).astype(out.dtype)


def ffn_final_kernel(plan, info, *refs):
    pieces, (narrow, widen, narrow_l, widen_l, pack) = refs[: len(plan)], refs[len(plan) :]
    for piece, (rel, low, high) in zip(pieces, plan):
        rows = piece_rows(info, rel)
        if low == 0:
            narrow[rows, :] = piece[:96].astype(F32)
            pack[extra_rows(info, rel // 4, rel % 4), :] = piece[96:112].astype(F32)
        if high > 112:
            widen[rows, :] = piece[112 - low :].astype(F32)
    width_l = narrow_l.shape[0]
    narrow_l[:128] = pack[:, :width_l]
    narrow_l[128:] = pack[:64, 512 : 512 + width_l]
    widen_l[:128] = pack[:, 256 : 256 + width_l]
    widen_l[128:] = pack[64:, 512 : 512 + width_l]


def copied_final_kernel(plan, info, *refs):
    pieces, refs = refs[: len(plan)], refs[len(plan) :]
    project, dense, project_l, dense_l = refs[:4]
    vectors, vectors_l, (extra,) = refs[4:8], refs[8:12], refs[12:]
    width = dense.shape[1]
    for piece, (rel, low, high) in zip(pieces, plan):
        rows = piece_rows(info, rel)
        for part in range(low, high):
            block = lax.rem(info[GROUP] + part, 4)
            at = pl.ds(pl.multiple_of(128 * block + (info[HALF + rel // 4] + info[PIECE + rel % 4]) // 6, EXTRA), EXTRA)
            extra[at, :] = piece[part - low, 96:].astype(F32)

            @pl.when(block < 3)
            def _():
                project[rows, pl.ds(pl.multiple_of(block * width, LANES), width)] = piece[part - low, :96].astype(F32)

            @pl.when(block == 3)
            def _():
                dense[rows, :] = piece[part - low, :96].astype(F32)

    width_l = dense_l.shape[0]
    for i in range(3):
        project_l[:, i * width_l : (i + 1) * width_l] = extra[:width_l, i * 256 : i * 256 + width_l]
    dense_l[...] = extra[width_l : 2 * width_l, :width_l]
    for at, (biases, gains, shifts, hidden), lanes in ((2 * width_l, vectors, width), (2 * width_l + 16, vectors_l, width_l)):
        rows = extra[at : at + 16, :lanes]
        for i, row in enumerate((8, 9, 6, 2)):
            biases[i : i + 1, :] = rows[row : row + 1]
        gains[0:1, :] = rows[4:5]
        gains[1:2, :] = rows[0:1]
        shifts[0:1, :] = rows[5:6]
        shifts[1:2, :] = rows[1:2]
        hidden[...] = extra[pl.ds(at + 12 + info[GROUP], 1), :lanes]


def attend_back_kernel(
    info, qt, kt, vt, ql, kl, vl, dct, dcl, lse,
    dq, dk, dv, dq_l, dk_l, dv_l,
    k_acc, v_acc, kl_acc, vl_acc, ql_acc,
):
    own_rows = qt.shape[0]
    window = kt.shape[0]
    block = window // 2
    pad = (dk.shape[0] - window) // 2
    for acc in (k_acc, v_acc, kl_acc, vl_acc, ql_acc):
        acc[...] = jnp.zeros_like(acc)
    for out in (dk, dv, dk_l, dv_l):
        edge = jnp.zeros((pad, out.shape[1]), BF)
        out[:pad, :] = edge
        out[pad + window :, :] = edge
    lane = lax.broadcasted_iota(jnp.int32, (1, LANES), 1)

    def one_pair(pair, carry):
        text_lanes = lanes_of(pair * LANES)
        group_lanes = lanes_of((pair // 4) * LANES)
        scaled = head_masks(pair, 0.125, 0.25)
        plain = head_masks(pair, 1.0, 1.0)
        for j in range(own_rows // LANES):
            rows = pl.ds(j * LANES, LANES)
            keys_at = pl.ds(pl.multiple_of(info[LOCAL + j] * block, block), block)
            stacked = stack_heads(qt[rows, text_lanes], ql[rows, group_lanes], scaled)
            keys = jnp.concatenate([kt[keys_at, text_lanes], kl[keys_at, group_lanes]], axis=1)
            values = jnp.concatenate([vt[keys_at, text_lanes], vl[keys_at, group_lanes]], axis=1)
            dcs = stack_heads(dct[rows, text_lanes], dcl[rows, group_lanes], plain)
            logs = lse[rows, :]
            log_total = jnp.concatenate(
                [
                    jnp.sum(jnp.where(lane == 2 * pair, logs, 0.0), axis=1, keepdims=True),
                    jnp.sum(jnp.where(lane == 2 * pair + 1, logs, 0.0), axis=1, keepdims=True),
                ],
                axis=0,
            )
            probs = jnp.exp(pair_scores(stacked, keys, info[LIMIT + j]) - log_total)
            dprobs = nt(dcs, values)
            inner = jnp.sum(probs * dprobs, axis=1, keepdims=True)
            dscores = (probs * (dprobs - inner)).astype(BF)
            text, layout = unstack_heads(nn(dscores, keys), scaled)
            dq[rows, text_lanes] = text.astype(BF)
            ql_acc[rows, group_lanes] += layout
            both = tn(dscores, stacked)
            k_acc[keys_at, text_lanes] += both[:, :LANES]
            kl_acc[keys_at, group_lanes] += both[:, LANES:]
            both = tn(probs.astype(BF), dcs)
            v_acc[keys_at, text_lanes] += both[:, :LANES]
            vl_acc[keys_at, group_lanes] += both[:, LANES:]
        return carry

    lax.fori_loop(0, HEADS // 2, one_pair, 0)
    middle = pl.ds(pad, window)
    dk[middle, :] = k_acc[...].astype(BF)
    dv[middle, :] = v_acc[...].astype(BF)
    dk_l[middle, :] = kl_acc[...].astype(BF)
    dv_l[middle, :] = vl_acc[...].astype(BF)
    dq_l[...] = ql_acc[...].astype(BF)


def key_value_grad(info, at, rows_out, wt, wl, dk, dv, dk_l, dv_l):
    width, wide = dk.shape[1], dk_l.shape[1]
    rows = pl.ds(pl.multiple_of(info[SHIFT] + at, LANES), rows_out)
    text = nt(dk[rows, :], wt[:, width : 2 * width]) + nt(dv[rows, :], wt[:, 2 * width :])
    layout = nt(wl[:, wide : 2 * wide], dk_l[rows, :]) + nt(wl[:, 2 * wide :], dv_l[rows, :])
    return text, layout


def store_packed(out, text, layout):
    own_rows = text.shape[0]
    half = layout.shape[0] // 2
    out[:own_rows, :] = text.astype(BF)
    out[own_rows:, :own_rows] = layout[:half].astype(BF)
    out[own_rows:, own_rows:] = layout[half:].astype(BF)


def sides_kernel(info, wt, wl, dk, dv, dk_l, dv_l, left, right):
    own_rows = left.shape[0] * 4 // 5
    for side, shift in ((left, 0), (right, 2 * own_rows)):
        store_packed(side, *key_value_grad(info, shift, own_rows, wt, wl, dk, dv, dk_l, dv_l))


def own_kernel(info, wt, wl, dq, dk, dv, dq_l, dk_l, dv_l, dfirst_t, dfirst_lt, left, right, out):
    own_rows, width = dq.shape
    wide = dq_l.shape[1]
    half = dfirst_lt.shape[0] // 2
    text, layout = key_value_grad(info, own_rows, own_rows, wt, wl, dk, dv, dk_l, dv_l)
    text = dfirst_t[...] + text + nt(dq[...], wt[:, :width])
    layout = dfirst_lt[...] + layout + nt(wl[:, :wide], dq_l[...])
    got = left[...].astype(F32) + right[...].astype(F32)
    text = text + got[:own_rows]
    layout = layout + jnp.concatenate([got[own_rows:, :own_rows], got[own_rows:, own_rows:]], axis=0)
    store_packed(out, text, layout)


def input_final_kernel(info, rows, text, layout):
    own_rows = rows.shape[1] * 4 // 5
    half = layout.shape[0] // 2
    for t in range(rows.shape[0]):
        at = pl.ds(t * own_rows, own_rows)
        text[at, :] = rows[t, :own_rows, :].astype(F32)
        layout[:half, at] = rows[t, own_rows:, :own_rows].astype(F32)
        layout[half:, at] = rows[t, own_rows:, own_rows:].astype(F32)


def extras(
    info, xlt, dq, dv, dq_l, dk_l, dv_l, cl, db_l, sums_a, sums_b, hsums, sums_al, sums_bl, hsums_l, extra, small,
):
    own_rows = dq.shape[0]
    wide = dq_l.shape[1]
    width_l = xlt.shape[0]
    window = dk_l.shape[0] - 2 * own_rows
    own = pl.ds(pl.multiple_of(info[OWN], LANES), own_rows)
    seen = pl.ds(pl.multiple_of(info[WINDOW], LANES), window)
    middle = pl.ds(own_rows, window)
    extra[width_l:, :] = jnp.zeros((extra.shape[0] - width_l, extra.shape[1]), BF)
    extra[:width_l, :wide] = nn(xlt[:, own], dq_l[...]).astype(BF)
    extra[:width_l, wide : 2 * wide] = nn(xlt[:, seen], dk_l[middle, :]).astype(BF)
    extra[:width_l, 2 * wide : 3 * wide] = nn(xlt[:, seen], dv_l[middle, :]).astype(BF)
    extra[width_l : 2 * width_l, :width_l] = tn(cl[...], db_l[...]).astype(BF)
    small[...] = jnp.zeros_like(small)
    small[0:4, :] = sums_a[...]
    small[4:8, :] = sums_b[...]
    small[8:9, :] = column_sum(dq[...])
    small[9:10, :] = column_sum(dv[middle, :])
    small[16:20, :width_l] = sums_al[...]
    small[20:24, :width_l] = sums_bl[...]
    small[24:25, :wide] = column_sum(dq_l[...])
    small[25:26, :wide] = column_sum(dv_l[middle, :])
    for s in range(4):
        group = lax.rem(info[GROUP] + s, 4)
        small[pl.ds(12 + group, 1), :] = hsums[s]
        small[pl.ds(28 + group, 1), :width_l] = hsums_l[s]
    extra[2 * width_l : 2 * width_l + 32, :] = small[...].astype(BF)


def copied_grads(info, xt, dq, dk, dv, ct, db, half, grad, store):
    own_rows = dq.shape[0]
    window = dk.shape[0] - 2 * own_rows
    own = pl.ds(pl.multiple_of(info[OWN], LANES), own_rows)
    seen = pl.ds(pl.multiple_of(info[WINDOW], LANES), window)
    middle = pl.ds(own_rows, window)
    for block in range(4):
        if block == 0:
            grad[...] = tn(xt[own, half], dq[...])
        elif block == 1:
            grad[...] = tn(xt[seen, half], dk[middle, :])
        elif block == 2:
            grad[...] = tn(xt[seen, half], dv[middle, :])
        else:
            grad[...] = tn(ct[:, half], db[...])
        slot = info[SLOT + block]
        for p in range(2):
            for q in range(2):
                row = jnp.where(slot < 2, info[PIECE + p + 2 * q], info[PIECE + q + 2 * p])
                store(block, slot, p, q, row, grad[pl.ds(pl.multiple_of(row, 32), 96), :])


def copied_send_kernel(
    info, xt, dq, dk, dv, ct, db, xlt, dq_l, dk_l, dv_l, cl, db_l, sums_a, sums_b, hsums, sums_al, sums_bl, hsums_l,
    send, extra, grad, small,
):
    half = pl.ds(pl.multiple_of(info[HALF + 1], LANES), grad.shape[0])
    extras(info, xlt, dq, dv, dq_l, dk_l, dv_l, cl, db_l, sums_a, sums_b, hsums, sums_al, sums_bl, hsums_l, extra, small)

    def store(block, slot, p, q, row, rows):
        at = pl.multiple_of(128 * block + (info[HALF + 1] + row) // 6, EXTRA)
        send[slot, p, q, :96] = rows.astype(BF)
        send[slot, p, q, 96:] = extra[pl.ds(at, EXTRA), :]

    copied_grads(info, xt, dq, dk, dv, ct, db, half, grad, store)


def copied_keep_kernel(info, xt, dq, dk, dv, ct, db, extra, recv, next_a, keep_a, next_b, keep_b, grad):
    half = pl.ds(pl.multiple_of(info[HALF], LANES), grad.shape[0])

    def store(block, slot, p, q, row, rows):
        at = pl.multiple_of(128 * block + (info[HALF] + row) // 6, EXTRA)
        got = recv[slot, p, q].astype(F32)
        text = (rows + got[:96]).astype(BF)
        rest = (extra[pl.ds(at, EXTRA), :].astype(F32) + got[96:]).astype(BF)

        @pl.when(slot < 2)
        def _():
            (next_a if p else keep_a)[q, slot, :96] = text
            (next_a if p else keep_a)[q, slot, 96:] = rest

        @pl.when(slot >= 2)
        def _():
            (next_b if p else keep_b)[q, slot - 2, :96] = text
            (next_b if p else keep_b)[q, slot - 2, 96:] = rest

    copied_grads(info, xt, dq, dk, dv, ct, db, half, grad, store)


SM = pl.BlockSpec(memory_space=pltpu.SMEM)
VM = pl.BlockSpec(memory_space=pltpu.VMEM)
HB = pl.BlockSpec(memory_space=pl.ANY)


def call(name, kernel, operands, outs, scratch=(), after=(), in_hbm=0):
    operands = tuple(operands)
    outs = tuple(outs) + (shape((8, LANES), F32),)
    specs = [HB] * len(after) + [SM] + [VM] * (len(operands) - 1 - in_hbm) + [HB] * in_hbm
    operands = tuple(after) + operands
    at = len(operands) + len(outs) - 1

    def with_token(*refs):
        kernel(*refs[len(after) : at], *refs[at + 1 :])
        refs[at][...] = jnp.zeros_like(refs[at])

    return pl.pallas_call(
        with_token,
        out_shape=outs,
        in_specs=specs,
        out_specs=[VM] * len(outs),
        scratch_shapes=list(scratch),
        cost_estimate=pl.CostEstimate(flops=int(MICROSECONDS[name] * PER_MICROSECOND), bytes_accessed=0, transcendentals=0),
        compiler_params=pltpu.CompilerParams(vmem_limit_bytes=VMEM_LIMIT),
        name=name,
    )(*operands)


def shape(dims, dtype=BF):
    return jax.ShapeDtypeStruct(dims, dtype)


def flip(planes, bit):
    return [(i, i ^ bit) for i in range(planes)]


def tie(value, *tokens):
    return lax.optimization_barrier((value, tokens))[0]


def spread(piece, planes, split, mid=None, second=(), third=()):
    parts = piece.shape[0]
    core, x, y = 1, 2, 4
    send = lambda v, bit: lax.ppermute(v, "dp", flip(planes, bit))
    later = lambda v, tokens: tie(v, *tokens) if tokens else v
    by_x, by_y = send(piece, x), send(piece, y)
    held = [(later(v, second), rel, 0, parts) for rel, v in enumerate((piece, by_x, by_y))]
    by_x, by_y = held[1][0], held[2][0]
    if split == "x":
        forwarded = [(send(by_x, y), 3, 0, parts)]
    elif split == "y":
        forwarded = [(send(by_y, x), 3, 0, parts)]
    else:
        mid = mid or parts // 2
        forwarded = [(send(by_x[:mid], y), 3, 0, mid), (send(by_y[mid:], x), 3, mid, parts)]
    held += [(later(v, third), rel, low, high) for v, rel, low, high in forwarded]
    held += [(send(v, core), rel + 4, low, high) for v, rel, low, high in held]
    return [h[0] for h in held], tuple(h[1:] for h in held)


def per_device(
    text_input, layout_input, block_starts, intersection_flags, text_cotangent, layout_cotangent,
    text_project, text_biases, text_dense, text_gains, text_shifts, text_widen, text_hidden_bias, text_narrow,
    layout_project, layout_biases, layout_dense, layout_gains, layout_shifts, layout_widen, layout_hidden_bias,
    layout_narrow,
):
    blocks, length = intersection_flags.shape
    total = blocks * length
    groups = lax.axis_size("tensor")
    planes = lax.axis_size("dp")
    own = total // groups
    tiles = own // LANES
    width = text_input.shape[1]
    width_l = layout_input.shape[1]
    wide = 2 * LANES
    window = 2 * length
    padded = window + 2 * own
    hid = text_narrow.shape[0]
    hid_l = layout_narrow.shape[0]
    piece = width // PIECES
    t = lax.axis_index("tensor").astype(jnp.int32)
    me = lax.axis_index("dp").astype(jnp.int32)
    core, x_bit, y_bit = me & 1, (me >> 1) & 1, (me >> 2) & 1

    def row_of(rc, rx, ry):
        return 4 * piece * (core ^ rc) + piece * ((x_bit ^ rx) + 2 * (y_bit ^ ry))

    flagged = jnp.sum(intersection_flags, axis=1, dtype=jnp.int32)
    base = jnp.minimum((t * own) // length, blocks - 2)
    tile_rows = t * own + LANES * jnp.arange(tiles, dtype=jnp.int32)
    tile_block = tile_rows // length
    pick = tile_block[:, None] == jnp.arange(blocks, dtype=jnp.int32)[None, :]
    limit = DOC - jnp.sum(jnp.where(pick, block_starts[None, :], 0), axis=1)
    flags_of = jnp.sum(jnp.where(pick, flagged[None, :], 0), axis=1)
    info = jnp.concatenate(
        [
            jnp.stack([t * own, base * length, t * own - base * length]),
            tile_block - base,
            limit,
            flags_of,
            tile_rows - tile_block * length,
            jnp.stack(
                [t, 4 * piece * core, 4 * piece * (1 - core)]
                + [row_of(0, rx, ry) - 4 * piece * core for ry in (0, 1) for rx in (0, 1)]
                + [(b - t) % groups for b in range(4)]
            ),
        ]
    ).astype(jnp.int32)

    shift_from = lambda k: [(i, (i - k) % groups) for i in range(groups)]
    shift_to = lambda k: [(i, (i + k) % groups) for i in range(groups)]
    bias = jnp.concatenate([text_hidden_bias, layout_hidden_bias, jnp.zeros((8 * LANES - hid - hid_l,), F32)])
    mine, small, hidden, packed_up = call(
        "pack", pack_kernel,
        (info, text_widen, text_narrow, layout_widen, layout_narrow, bias.reshape(8, LANES)),
        (shape((2, piece, width)), shape((2 * width_l, wide)), shape((16, wide))),
    )
    come = {k: lax.ppermute(mine, "tensor", shift_from(k)) for k in (1, 3)}
    hiddens = [hidden] + [lax.ppermute(hidden, "tensor", shift_from(k)) for k in (1, 2, 3)]

    xlt = layout_input.T
    qt, kt, vt, ql, kl, vl, xl_own, wl, projected = call(
        "project", project_kernel,
        (info, text_input, xlt, text_project, layout_project, text_biases, layout_biases),
        (shape((own, width)), shape((window, width)), shape((window, width)),
         shape((own, wide)), shape((window, wide)), shape((window, wide)),
         shape((own, width_l)), shape((width_l, 3 * wide))),
        after=(packed_up,),
    )
    come[2] = lax.ppermute(tie(mine, projected), "tensor", shift_from(2))
    ct, cl, lse, attended = call(
        "attend", attend_kernel,
        (info, qt, kt, vt, ql, kl, vl),
        (shape((own, width)), shape((own, width_l)), shape((own, LANES), F32)),
        scratch=(pltpu.VMEM((own, wide), F32),),
    )
    first_t, first_l, low_t, low_l, normed_l, active0, slope0, total_t, first_done = call(
        "first_norm", first_norm_kernel,
        (info, text_input, xl_own, ct, cl, text_dense, layout_dense, text_biases, layout_biases,
         text_gains, text_shifts, layout_gains, layout_shifts, text_widen, hidden, text_narrow),
        (shape((own, width), F32), shape((own, width_l), F32), shape((own, width)), shape((own, width_l)),
         shape((own, width_l), F32), shape((own, hid)), shape((own, hid), F32), shape((own, width), F32)),
    )
    shards = {
        k: spread(tie(come[k], projected), planes, {1: "x", 3: "y"}[k], second=(attended,), third=(first_done,)) for k in (1, 3)
    }
    smalls = [small] + [lax.ppermute(tie(small, first_done), "tensor", shift_from(k)) for k in (1, 2, 3)]
    actives, slopes, shard_done = {0: active0}, {0: slope0}, {}
    for k in (1, 3):
        arrays, plan = shards[k]
        actives[k], slopes[k], total_t, shard_done[k] = call(
            "shard", functools.partial(shard_kernel, plan),
            (info, low_t, total_t, hiddens[k], *arrays),
            (shape((own, hid)), shape((own, hid), F32), shape((own, width), F32)),
            scratch=(pltpu.VMEM((1, 2, width, hid), BF), pltpu.SemaphoreType.DMA((1, len(plan)))),
            in_hbm=len(plan),
        )
    shards[2] = spread(tie(come[2], first_done), planes, "half", second=(shard_done[1],), third=(shard_done[3],))
    plans = tuple(shards[k][1] for k in (1, 2, 3))
    arrays = sum((shards[k][0] for k in (1, 2, 3)), [])
    rows_a = piece + EXTRA
    outs = call(
        "turn", functools.partial(turn_kernel, plans),
        (info, low_t, total_t, text_gains, text_shifts, text_cotangent, text_widen, text_narrow,
         slopes[0], slopes[1], slopes[3], actives[0], actives[1], actives[3],
         low_l, normed_l, layout_gains, layout_shifts, layout_cotangent.T, *smalls, *hiddens, *arrays),
        (shape((own, width)), shape((own, width)), shape((groups, own, hid)), shape((own, width), F32),
         shape((4, width), F32), shape((groups, 1, hid), F32), shape((own, hid)),
         shape((width_l, own)), shape((own, width_l), F32), shape((4, width_l), F32), shape((groups, 1, hid_l), F32),
         shape((groups, 2, 2, rows_a, width)), shape((groups, 2, 2, piece, width)), shape((groups, 128, width))),
        scratch=(pltpu.VMEM((3, 2, width, hid), BF), pltpu.VMEM((own, hid), F32),
                 pltpu.VMEM((groups, own, hid_l), F32), pltpu.VMEM((groups, own, hid_l), BF),
                 pltpu.VMEM((groups, own, hid_l), BF), pltpu.VMEM((own, width_l), BF), pltpu.VMEM((own, width_l), BF),
                 pltpu.VMEM((4 * piece, width), F32), pltpu.SemaphoreType.DMA((3, max(map(len, plans))))),
        in_hbm=len(arrays),
    )
    result_t, dout_t, dhid_t, dnormed_t, sums_t, hsums_t, actives[2] = outs[:7]
    result_lt, dnormed_l, sums_l, hsums_l, send_a, send_b, pack, turned = outs[7:]

    in_order = [actives[k] for k in range(4)]
    across = lambda v, bit: lax.ppermute(v, "dp", flip(planes, bit))
    recv_a, recv_b = across(send_a, 1), across(send_b, 1)
    dfirst_t, db_t, dc_t, low_sums_t, dfirst_lt, db_l, dc_l, low_sums_l, lowered = call(
        "lower", lower_kernel,
        (info, first_t, dnormed_t, text_gains, text_dense, first_l, dnormed_l, layout_gains, layout_dense),
        (shape((own, width), F32), shape((own, width)), shape((own, width)), shape((4, width), F32),
         shape((width_l, own), F32), shape((own, width_l)), shape((own, wide)), shape((4, width_l), F32)),
        scratch=(pltpu.VMEM((own, width_l), F32),),
    )
    next_a, keep_a, next_b, keep_b, kept = call(
        "ffn_keep", ffn_keep_kernel,
        (info, *in_order, dout_t, low_t, dhid_t, recv_a, recv_b, pack),
        (shape((2, groups, rows_a, width)),) * 2 + (shape((2, groups, piece, width)),) * 2,
        scratch=(pltpu.VMEM((4 * piece, width), F32),), after=(lowered,),
    )
    recv_a, recv_b = across(next_a, 2), across(next_b, 4)

    dq, dk, dv, dq_l, dk_l, dv_l, attended_back = call(
        "attend_back", attend_back_kernel,
        (info, qt, kt, vt, ql, kl, vl, dc_t, dc_l, lse),
        (shape((own, width)), shape((padded, width)), shape((padded, width)),
         shape((own, wide)), shape((padded, wide)), shape((padded, wide))),
        scratch=(pltpu.VMEM((window, width), F32), pltpu.VMEM((window, width), F32),
                 pltpu.VMEM((window, wide), F32), pltpu.VMEM((window, wide), F32), pltpu.VMEM((own, wide), F32)),
        after=(kept,),
    )
    packed = shape((own + own // 4, width))
    left, right, sided = call("sides", sides_kernel, (info, text_project, wl, dk, dv, dk_l, dv_l), (packed, packed))
    from_right = lax.ppermute(left, "tensor", [(i + 1, i) for i in range(groups - 1)])
    from_left = lax.ppermute(right, "tensor", [(i, i + 1) for i in range(groups - 1)])

    next_a, keep_a = add_split(keep_a, recv_a)
    next_b, keep_b = add_split(keep_b, recv_b)
    copied_in = (text_input, dq, dk, dv, ct, db_t)
    send, extra, sent = call(
        "copied_send", copied_send_kernel,
        (info,) + copied_in + (xlt, dq_l, dk_l, dv_l, cl, db_l, sums_t, low_sums_t, hsums_t, sums_l, low_sums_l, hsums_l),
        (shape((groups, 2, 2, rows_a, width)), shape((4 * 128, width))),
        scratch=(pltpu.VMEM((4 * piece, width), F32), pltpu.VMEM((32, width), F32)), after=(sided, next_a, next_b),
    )
    recv = across(send, 1)
    recv_a, recv_b = across(next_a, 4), across(next_b, 2)
    copied_next_a, copied_keep_a, copied_next_b, copied_keep_b, copied_kept = call(
        "copied_keep", copied_keep_kernel, (info,) + copied_in + (extra, recv),
        (shape((2, 2, rows_a, width)),) * 4,
        scratch=(pltpu.VMEM((4 * piece, width), F32),),
    )
    own_sum, owned = call(
        "own", own_kernel,
        (info, text_project, wl, dq, dk, dv, dq_l, dk_l, dv_l, dfirst_t, dfirst_lt, from_right, from_left),
        (packed,), after=(copied_kept,),
    )
    all_rows = lax.all_gather(own_sum, "tensor", axis=0, tiled=False)
    copied_recv_a, copied_recv_b = across(copied_next_a, 2), across(copied_next_b, 4)
    *ffn_parts, ffn_spreaded = call(
        "ffn_spread", ffn_spread_kernel, (info, keep_a, recv_a, keep_b, recv_b),
        (shape((rows_a + piece, width)),) * 4, after=(owned,),
    )
    ffn_parts = [ffn_parts[0]] + [lax.ppermute(ffn_parts[k], "tensor", shift_to(k)) for k in (1, 2, 3)]

    def across_planes(value):
        bit = PIECES
        while bit < planes:
            value = add(value, across(value, bit))
            bit *= 2
        return value

    next_a, keep_a = add_split(copied_keep_a, tie(copied_recv_a, ffn_spreaded))
    next_b, keep_b = add_split(copied_keep_b, tie(copied_recv_b, ffn_spreaded))
    recv_a, recv_b = across(next_a, 4), across(next_b, 2)
    ffn_arrays, ffn_plan = spread(across_planes(add(*ffn_parts)), planes, "half", rows_a)
    *parts, _ = call(
        "copied_spread", copied_spread_kernel, (info, keep_a, recv_a, keep_b, recv_b), (shape((rows_a, width)),) * 4,
    )
    parts = [parts[0]] + [lax.ppermute(parts[k], "tensor", shift_to(k)) for k in (1, 2, 3)]
    summed = across_planes(add(*parts))
    g_narrow, g_widen, g_narrow_l, g_widen_l, _ = call(
        "ffn_final", functools.partial(ffn_final_kernel, ffn_plan), (info, *ffn_arrays),
        (shape((hid, width), F32), shape((width, hid), F32), shape((hid_l, width_l), F32), shape((width_l, hid_l), F32)),
        scratch=(pltpu.VMEM((128, width), F32),),
    )
    every = jnp.stack([summed] + [lax.ppermute(summed, "tensor", shift_from(k)) for k in (1, 2, 3)])
    text_grad, layout_grad_t, given = call(
        "input_final", input_final_kernel, (info, all_rows),
        (shape((total, width), F32), shape((width_l, total), F32)),
    )
    arrays, plan = spread(tie(every, given), planes, "half")
    vectors = lambda w, h: (shape((4, w), F32), shape((2, w), F32), shape((2, w), F32), shape((1, h), F32))
    outs = call(
        "copied_final", functools.partial(copied_final_kernel, plan), (info, *arrays),
        (shape((width, 3 * width), F32), shape((width, width), F32),
         shape((width_l, 3 * width_l), F32), shape((width_l, width_l), F32)) + vectors(width, hid) + vectors(width_l, hid_l),
        scratch=(pltpu.VMEM((4 * 128, width), F32),),
    )
    g_project, g_dense, g_project_l, g_dense_l = outs[:4]
    bias_t, gain_t, shift_t, hb_t, bias_l, gain_l, shift_l, hb_l = outs[4:12]
    return (
        result_t, result_lt.T, text_grad, layout_grad_t.T,
        g_project, bias_t, g_dense, gain_t, shift_t, g_widen, hb_t[0], g_narrow,
        g_project_l, bias_l, g_dense_l, gain_l, shift_l, g_widen_l, hb_l[0], g_narrow_l,
    )


def solution(mesh):
    rows = P(("dp", "tensor"), None)
    weights = (P(), P(), P(), P(), P(), P(None, "tensor"), P("tensor"), P("tensor", None))
    return jax.shard_map(
        per_device,
        mesh=mesh,
        in_specs=(P("dp", None), P("dp", None), P("dp"), P("dp", None), rows, rows) + weights + weights,
        out_specs=(rows, rows, P("dp", None), P("dp", None)) + weights + weights,
        check_vma=False,
    )
```

```python
import functools
import math

import jax
import jax.numpy as jnp
from jax import lax
from jax.experimental import pallas as pl
from jax.experimental.pallas import tpu as pltpu
from jax.sharding import PartitionSpec as P

HEADS = 12
DOC = 2048
LANES = 128
epsilon = 1e-05
masked_score = -1e30
F32 = jnp.float32
BF = jnp.bfloat16

OWN, WINDOW, SHIFT, LOCAL, LIMIT, FLAGGED, PLACE, GROUP, HALF, PIECE, SLOT = 0, 1, 2, 3, 6, 9, 12, 15, 16, 18, 22
PIECES = 8
CORE, X, Y = 1, 2, 4
PER_MICROSECOND = 1e9
MICROSECONDS = {
    "pack": 1, "project": 5, "attend": 9, "first_norm": 4, "shard": 3, "turn": 21, "lower": 2, "ffn_keep": 4,
    "attend_back": 15, "sides": 3, "copied_send": 4, "own": 3, "copied_keep": 5, "input_final": 3,
    "ffn_spread": 1, "ffn_final": 3, "copied_spread": 1, "copied_final": 6,
}


def nn(a, b):
    return lax.dot_general(a, b, (((1,), (0,)), ((), ())), preferred_element_type=F32)


def nt(a, b):
    return lax.dot_general(a, b, (((1,), (1,)), ((), ())), preferred_element_type=F32)


def tn(a, b):
    return lax.dot_general(a, b, (((0,), (0,)), ((), ())), preferred_element_type=F32)


def mean(values):
    return jnp.mean(values, axis=-1, keepdims=True)


def column_sum(values):
    return jnp.sum(values.astype(F32), axis=0, keepdims=True)


def normalised(values):
    centre = values - mean(values)
    scale = lax.rsqrt(mean(centre * centre) + epsilon)
    return centre * scale, scale


def norm_back(upstream, normal, scale, gain_row):
    u = upstream * gain_row
    return scale * (u - mean(u) - normal * mean(u * normal))


def lanes_of(start):
    return pl.ds(pl.multiple_of(start, LANES), LANES)


def head_masks(pair, text_scale, layout_scale):
    lane = lax.broadcasted_iota(jnp.int32, (1, LANES), 1)
    first = 32 * pair - LANES * (pair // 4)
    text_a = jnp.where(lane < 64, text_scale, 0.0)
    text_b = jnp.where(lane < 64, 0.0, text_scale)
    layout_a = jnp.where((lane >= first) & (lane < first + 16), layout_scale, 0.0)
    layout_b = jnp.where((lane >= first + 16) & (lane < first + 32), layout_scale, 0.0)
    return text_a, layout_a, text_b, layout_b


def stack_heads(text, layout, masks):
    text_a, layout_a, text_b, layout_b = (m.astype(BF) for m in masks)
    upper = jnp.concatenate([text * text_a, layout * layout_a], axis=1)
    lower = jnp.concatenate([text * text_b, layout * layout_b], axis=1)
    return jnp.concatenate([upper, lower], axis=0)


def unstack_heads(stacked, masks):
    text_a, layout_a, text_b, layout_b = masks
    upper, lower = stacked[:LANES], stacked[LANES:]
    text = upper[:, :LANES] * text_a + lower[:, :LANES] * text_b
    layout = upper[:, LANES:] * layout_a + lower[:, LANES:] * layout_b
    return text, layout


def pair_scores(stacked, keys, limit):
    scores = nt(stacked, keys)
    key = lax.broadcasted_iota(jnp.int32, (1, scores.shape[1]), 1)
    return jnp.where(key < limit, scores, masked_score)


def pack_kernel(place, weights, layout, bias, mine):
    mine[:192] = weights[...]
    width_l = layout.shape[1]
    high = bias[...].astype(BF).astype(F32)
    middle = (bias[...] - high).astype(BF).astype(F32)
    low = bias[...] - high - middle
    biases = jnp.concatenate([high, middle, low, jnp.zeros_like(low)], axis=0)
    mine[192:, :] = jnp.zeros((32, mine.shape[1]), BF)
    empty = jnp.zeros((8, width_l), F32)
    both = layout[...].astype(F32)
    mine[192:, :width_l] = jnp.concatenate([both[:24], empty], axis=0).astype(BF)
    mine[192:, 256 : 256 + width_l] = jnp.concatenate([both[24:], empty], axis=0).astype(BF)
    mine[192:, 512:640] = biases.astype(BF)


def biases_of(rest):
    split = rest[:, 512:640].astype(F32)
    rows = split[:8] + split[8:16] + split[16:24]
    text = jnp.concatenate([rows[i : i + 1] for i in range(6)], axis=1)
    layout = jnp.concatenate([rows[i : i + 1] for i in (6, 7)], axis=1)
    return text, layout


def identity(size):
    row = lax.broadcasted_iota(jnp.int32, (size, size), 0)
    column = lax.broadcasted_iota(jnp.int32, (size, size), 1)
    return jnp.where(row == column, 1.0, 0.0).astype(BF)


def project_kernel(info, xt, xlt, wt, wl, bt, bl, qt, kt, vt, ql, kl, vl, xl_own, wide_l):
    own_rows, width = qt.shape
    wide = ql.shape[1]
    width_l = wl.shape[0]
    own = pl.multiple_of(info[OWN], LANES)
    start = pl.multiple_of(info[WINDOW], LANES)
    rows = pl.ds(own, own_rows)
    for i in range(3):
        wide_l[:, i * wide : i * wide + width_l] = wl[:, i * width_l : (i + 1) * width_l]
        wide_l[:, i * wide + width_l : (i + 1) * wide] = jnp.zeros((width_l, wide - width_l), BF)
    edge = jnp.zeros((1, wide - width_l), F32)
    bias = [jnp.concatenate([bl[i : i + 1, :], edge], axis=1) for i in (0, 1)]
    qt[...] = (nn(xt[rows, :], wt[:, :width]) + bt[0:1, :]).astype(BF)
    ql[...] = (tn(xlt[:, rows], wide_l[:, :wide]) + bias[0]).astype(BF)
    xl_own[...] = tn(xlt[:, rows], identity(width_l)).astype(BF)

    def part(i, carry):
        rows = pl.ds(pl.multiple_of(i * 256, 256), 256)
        from_rows = pl.ds(pl.multiple_of(start + i * 256, 256), 256)
        x = xt[from_rows, :]
        kt[rows, :] = nn(x, wt[:, width : 2 * width]).astype(BF)
        vt[rows, :] = (nn(x, wt[:, 2 * width :]) + bt[1:2, :]).astype(BF)
        x = xlt[:, from_rows]
        kl[rows, :] = tn(x, wide_l[:, wide : 2 * wide]).astype(BF)
        vl[rows, :] = (tn(x, wide_l[:, 2 * wide :]) + bias[1]).astype(BF)
        return carry

    lax.fori_loop(0, kt.shape[0] // 256, part, 0)


def attend_kernel(info, qt, kt, vt, ql, kl, vl, ct, cl, lse, cl_acc):
    own_rows, layout_width = cl.shape
    block = kt.shape[0] // 2
    cl_acc[...] = jnp.zeros_like(cl_acc)
    lse[...] = jnp.zeros_like(lse)
    lane = lax.broadcasted_iota(jnp.int32, (1, LANES), 1)

    def one_pair(pair, carry):
        text_lanes = lanes_of(pair * LANES)
        group_lanes = lanes_of((pair // 4) * LANES)
        scaled = head_masks(pair, 0.125, 0.25)
        plain = head_masks(pair, 1.0, 1.0)
        for j in range(own_rows // LANES):
            rows = pl.ds(j * LANES, LANES)
            keys_at = pl.ds(pl.multiple_of(info[LOCAL + j] * block, block), block)
            stacked = stack_heads(qt[rows, text_lanes], ql[rows, group_lanes], scaled)
            keys = jnp.concatenate([kt[keys_at, text_lanes], kl[keys_at, group_lanes]], axis=1)
            values = jnp.concatenate([vt[keys_at, text_lanes], vl[keys_at, group_lanes]], axis=1)
            scores = pair_scores(stacked, keys, info[LIMIT + j])
            highest = jnp.max(scores, axis=-1, keepdims=True)
            exponent = jnp.exp(scores - highest)
            totals = jnp.sum(exponent, axis=-1, keepdims=True)
            probs = (exponent * (1.0 / totals)).astype(BF)
            text, layout = unstack_heads(nn(probs, values), plain)
            ct[rows, text_lanes] = text.astype(BF)
            cl_acc[rows, group_lanes] += layout
            log_total = highest + jnp.log(totals)
            lse[rows, :] = (
                lse[rows, :]
                + jnp.where(lane == 2 * pair, log_total[:LANES], 0.0)
                + jnp.where(lane == 2 * pair + 1, log_total[LANES:], 0.0)
            )
        return carry

    lax.fori_loop(0, HEADS // 2, one_pair, 0)
    cl[...] = cl_acc[:, :layout_width].astype(BF)


def gelu_both(hidden):
    below = 0.5 * (1.0 + lax.erf(hidden * math.sqrt(0.5)))
    density = jnp.exp(-0.5 * hidden * hidden) * (1.0 / math.sqrt(2.0 * math.pi))
    return hidden * below, below + hidden * density


def shard_forward(low, widen, bias, narrow, active, slope, total):
    hid = widen.shape[1]
    step = 256 if hid % 256 == 0 else hid
    for n in range(hid // step):
        cols = slice(n * step, (n + 1) * step)
        value, gradient = gelu_both(nn(low[...], widen[:, cols]) + bias[:, cols])
        active[:, cols] = value.astype(BF)
        slope[:, cols] = gradient
    total[...] += nn(active[...], narrow[...])


def shard_backward(dout, narrow, slope, widen, dhid, sums, total):
    hid = widen.shape[1]
    step = 256 if hid % 256 == 0 else hid
    for n in range(hid // step):
        cols = slice(n * step, (n + 1) * step)
        dhidden = (nt(dout[...], narrow[cols, :]) * slope[:, cols]).astype(BF)
        dhid[:, cols] = dhidden
        sums[:, cols] = column_sum(dhidden)
    total[...] += nt(dhid[...], widen[...])


def first_norm_kernel(
    info, xt, xl_own, ct, cl, dense_t, dense_l, bt, bl, gt, st, gl, sl, widen, hidden, narrow,
    first_t, first_l, low_t, low_l, normed_l, active, slope, total,
):
    own_rows, width = first_t.shape
    rows = pl.ds(pl.multiple_of(info[OWN], LANES), own_rows)
    first = xt[rows, :].astype(F32) + (nn(ct[...], dense_t[...]) + bt[2:3, :])
    first_t[...] = first
    normed = normalised(first)[0] * gt[0:1, :] + st[0:1, :]
    low_t[...] = normed.astype(BF)
    total[...] = normed + bt[3:4, :]
    first = xl_own[...].astype(F32) + (nn(cl[...], dense_l[...]) + bl[2:3, :])
    first_l[...] = first
    normed = normalised(first)[0] * gl[0:1, :] + sl[0:1, :]
    low_l[...] = normed.astype(BF)
    normed_l[...] = normed + bl[3:4, :]
    shard_forward(low_t, widen, biases_of(hidden[192:, :])[0], narrow, active, slope, total)


def piece_rows(info, rel):
    return pl.ds(pl.multiple_of(info[HALF + rel // 4] + info[PIECE + rel % 4], 32), 96)


def place_shard(info, plan, refs, weights):
    for ref, (rel, low, high) in zip(refs, plan):
        for part in (0, 1):
            if low <= 96 * part and high >= 96 * (part + 1):
                weights[part, piece_rows(info, rel), :] = ref[96 * part - low : 96 * (part + 1) - low, :]


def place_layout(info, plan, refs, both):
    for ref, (rel, low, high) in zip(refs, plan):
        if high == 224:
            at = pl.multiple_of((info[HALF + rel // 4] + info[PIECE + rel % 4]) // 4, 8)
            both[pl.ds(at, 24), :] = ref[192 - low :, :512].astype(F32)[:24]


def shard_kernel(plan, info, low, total_in, *refs):
    pieces = refs[: len(plan)]
    active, slope, total, weights, layout, both = refs[len(plan) :]
    place_shard(info, plan, pieces, weights)
    place_layout(info, plan, pieces, both)
    layout[...] = both[...].astype(BF)
    total[...] = total_in[...]
    bias = biases_of(pieces[0][192:, :])[0]
    shard_forward(low, weights.at[0], bias, weights.at[1], active, slope, total)


def upper_back(total, gain, shift, cot, keep, result, dout, sums):
    normal, scale = normalised(total[...])
    result[...] = (normal * gain[1:2, :] + shift[1:2, :]).astype(BF)
    upstream = cot.astype(F32) * keep
    dsecond = norm_back(upstream, normal, scale, gain[1:2, :])
    dout[...] = dsecond.astype(BF)
    sums[0:1, :] = column_sum(upstream * normal)
    sums[1:2, :] = column_sum(upstream)
    sums[2:3, :] = column_sum(dout[...])
    sums[3:4, :] = jnp.zeros_like(sums[3:4, :])
    total[...] = dsecond


def turn_kernel(plan, info, *refs):
    refs = list(refs)
    take = lambda n: [refs.pop(0) for _ in range(n)]
    low, total_in, gain, shift, cot, widen_own, narrow_own = take(7)
    slopes_in, actives = take(3), take(3)
    low_l, normed_l, gain_l, shift_l, cot_lt = take(5)
    widen_own_l, narrow_own_l, layout_one, layout_three, mine, first_piece, third_piece = take(7)
    weights_one, weights_three = take(2)
    pieces = take(len(plan))
    result, dout, dhid, dnormed, sums, hsums, active = take(7)
    result_lt, dnormed_l, sums_l, hsums_l = take(4)
    send_a, send_b, pack = take(3)
    weights, slope, slope_l, active_l, dhid_l, dout_l, result_l, both = take(8)
    shards = dhid.shape[0]
    width = low.shape[1]
    dnormed[...] = total_in[...]
    dnormed_l[...] = normed_l[...]
    row = lax.broadcasted_iota(jnp.int32, (LANES, 1), 0)
    keep = []
    for j in range(low.shape[0] // LANES):
        place = row + info[PLACE + j]
        keep.append(jnp.where((place >= info[FLAGGED + j]) & (place < info[LIMIT + j]), 1.0, 0.0))
    keep = jnp.concatenate(keep, axis=0)

    width_l = low_l.shape[1]
    hidden_bias = [biases_of(ref[192:, :]) for ref in (mine, first_piece, pieces[0], third_piece)]
    place_layout(info, plan, pieces, both)
    last_l = both[...].astype(BF)
    layouts = [(widen_own_l[...], narrow_own_l[...])]
    layouts += [(v[:, :width_l], v[:, 256 : 256 + width_l]) for v in (layout_one[...], last_l, layout_three[...])]
    for s in range(shards):
        widen, narrow = layouts[s]
        shard_forward(low_l, widen, hidden_bias[s][1][:, :width_l], narrow, active_l.at[s], slope_l.at[s], dnormed_l)
    cot_l = tn(cot_lt[...], identity(width_l))
    upper_back(dnormed_l, gain_l, shift_l, cot_l, keep, result_l, dout_l, sums_l)
    result_lt[...] = nt(identity(width_l), result_l[...]).astype(BF)
    for s in range(shards):
        widen, narrow = layouts[s]
        shard_backward(dout_l, narrow, slope_l.at[s], widen, dhid_l.at[s], hsums_l.at[s], dnormed_l)
    for s in range(shards):
        pack[s] = jnp.zeros_like(pack[s])
        g = tn(active_l[s], dout_l[...]).astype(BF)
        pack[s, :128, :width_l] = g[:128]
        pack[s, :64, 512 : 512 + width_l] = g[128:]
        g = tn(low_l[...], dhid_l[s]).astype(BF)
        pack[s, :128, 256 : 256 + width_l] = g[:128]
        pack[s, 64:, 512 : 512 + width_l] = g[128:]

    place_shard(info, plan, pieces, weights)
    shard_forward(low, weights.at[0], hidden_bias[2][0], weights.at[1], active, slope, dnormed)
    upper_back(dnormed, gain, shift, cot[...], keep, result, dout, sums)
    shard_backward(dout, narrow_own, slopes_in[0], widen_own, dhid.at[0], hsums.at[0], dnormed)
    shard_backward(dout, weights_one.at[1], slopes_in[1], weights_one.at[0], dhid.at[1], hsums.at[1], dnormed)
    shard_backward(dout, weights.at[1], slope, weights.at[0], dhid.at[2], hsums.at[2], dnormed)
    shard_backward(dout, weights_three.at[1], slopes_in[2], weights_three.at[0], dhid.at[3], hsums.at[3], dnormed)

    half = pl.ds(pl.multiple_of(info[HALF + 1], LANES), send_b.shape[1])
    more = pl.ds(pl.multiple_of(info[HALF + 1] // 6, 64), 64)
    for s, act in enumerate((actives[0], actives[1], active, actives[2])):
        send_a[s, :384] = tn(act[:, half], dout[...]).astype(BF)
        send_a[s, 384:] = pack[s, more, :]
        send_b[s] = tn(low[:, half], dhid[s]).astype(BF)


def lower_back(first, dnormed, gain, dense, dfirst, dbranch, dcontext, sums):
    width = first.shape[1]
    wide = dcontext.shape[1]
    normal, scale = normalised(first[...])
    back = norm_back(dnormed[...], normal, scale, gain[0:1, :])
    sums[0:1, :] = column_sum(dnormed[...] * normal)
    sums[1:2, :] = column_sum(dnormed[...])
    dfirst[...] = back
    dbranch[...] = back.astype(BF)
    sums[2:3, :] = column_sum(dbranch[...])
    sums[3:4, :] = jnp.zeros_like(sums[3:4, :])
    dc = nt(dbranch[...], dense[...]).astype(BF)
    dcontext[:, :width] = dc
    if wide > width:
        dcontext[:, width:] = jnp.zeros((dc.shape[0], wide - width), BF)


def lower_kernel(
    info, first, dnormed, gain, dense, first_l, dnormed_l, gain_l, dense_l,
    dfirst, dbranch, dcontext, sums, dfirst_lt, dbranch_l, dcontext_l, sums_l, dfirst_l,
):
    lower_back(first, dnormed, gain, dense, dfirst, dbranch, dcontext, sums)
    lower_back(first_l, dnormed_l, gain_l, dense_l, dfirst_l, dbranch_l, dcontext_l, sums_l)
    dfirst_lt[...] = jnp.transpose(dfirst_l[...])


EXTRA = 16


def extra_rows(info, half, rel):
    return pl.ds(pl.multiple_of((info[HALF + half] + info[PIECE + rel]) // 6, EXTRA), EXTRA)


def ffn_keep_kernel(
    info, a0, a1, a2, a3, dout, low, dhid, recv_a, recv_b, pack, next_a1, next_a2, next_b1, next_b2, keep_a, keep_b, sum_a, sum_b,
):
    half = pl.ds(pl.multiple_of(info[HALF], LANES), 384)
    more = pl.ds(pl.multiple_of(info[HALF] // 6, 64), 64)
    for s, active in enumerate((a0, a1, a2, a3)):
        sum_a[:384] = (tn(active[:, half], dout[...]) + recv_a[s, :384].astype(F32)).astype(BF)
        sum_a[384:] = (pack[s, more, :].astype(F32) + recv_a[s, 384:].astype(F32)).astype(BF)
        sum_b[...] = (tn(low[:, half], dhid[s]) + recv_b[s].astype(F32)).astype(BF)
        next_a, next_b = ((next_a1, next_b1), (next_a2, next_b2))[s // 2]
        for rel in range(4):
            rows = pl.ds(pl.multiple_of(info[PIECE + rel], 32), 96)
            rest = pl.ds(pl.multiple_of(384 + info[PIECE + rel] // 6, EXTRA), EXTRA)
            to = next_a.at[rel // 2, s % 2] if rel % 2 else keep_a.at[rel // 2, s]
            to[:96] = sum_a[rows, :]
            to[96:] = sum_a[rest, :]
            to = next_b.at[rel % 2, s % 2] if rel // 2 else keep_b.at[rel % 2, s]
            to[...] = sum_b[rows, :]


def add(a, b, *more):
    total = a.astype(F32) + b.astype(F32)
    for value in more:
        total = total + value.astype(F32)
    return total.astype(BF)


def add_split(keep, recv, token=None):
    later = () if token is None else (token[0, 0],)
    return add(keep[1], recv[1], *later), add(keep[0], recv[0], *later)


def ffn_spread_kernel(info, keep_a, recv_a, keep_b, recv_b, out):
    rows = keep_a.shape[1]
    for s in range(4):
        group = lax.rem(info[GROUP] + s, 4)
        out[group, :rows] = (keep_a[s].astype(F32) + recv_a[s].astype(F32)).astype(BF)
        out[group, rows:] = (keep_b[s].astype(F32) + recv_b[s].astype(F32)).astype(BF)


def copied_spread_kernel(info, keep_a, recv_a, keep_b, recv_b, *outs):
    for k, out in enumerate(outs):
        keep, recv = (keep_a, recv_a) if k < 2 else (keep_b, recv_b)
        out[...] = (keep[k % 2].astype(F32) + recv[k % 2].astype(F32)).astype(out.dtype)


def ffn_final_kernel(plan, info, *refs):
    pieces, (narrow, widen, narrow_l, widen_l, pack) = refs[: len(plan)], refs[len(plan) :]
    for piece, (rel, low, high) in zip(pieces, plan):
        rows = piece_rows(info, rel)
        if low == 0:
            narrow[rows, :] = piece[:96].astype(F32)
            pack[extra_rows(info, rel // 4, rel % 4), :] = piece[96:112].astype(F32)
        if high > 112:
            widen[rows, :] = piece[112 - low :].astype(F32)
    width_l = narrow_l.shape[0]
    narrow_l[:128] = pack[:, :width_l]
    narrow_l[128:] = pack[:64, 512 : 512 + width_l]
    widen_l[:128] = pack[:, 256 : 256 + width_l]
    widen_l[128:] = pack[64:, 512 : 512 + width_l]


def copied_final_kernel(plan, info, *refs):
    pieces, refs = refs[: len(plan)], refs[len(plan) :]
    project, dense, project_l, dense_l = refs[:4]
    vectors, vectors_l, (extra,) = refs[4:8], refs[8:12], refs[12:]
    width = dense.shape[1]
    for piece, (rel, low, high) in zip(pieces, plan):
        rows = piece_rows(info, rel)
        for part in range(low, high):
            block = lax.rem(info[GROUP] + part, 4)
            at = pl.ds(pl.multiple_of(128 * block + (info[HALF + rel // 4] + info[PIECE + rel % 4]) // 6, EXTRA), EXTRA)
            extra[at, :] = piece[part - low, 96:].astype(F32)

            @pl.when(block < 3)
            def _():
                project[rows, pl.ds(pl.multiple_of(block * width, LANES), width)] = piece[part - low, :96].astype(F32)

            @pl.when(block == 3)
            def _():
                dense[rows, :] = piece[part - low, :96].astype(F32)

    width_l = dense_l.shape[0]
    for i in range(3):
        project_l[:, i * width_l : (i + 1) * width_l] = extra[:width_l, i * 256 : i * 256 + width_l]
    dense_l[...] = extra[width_l : 2 * width_l, :width_l]
    for at, (biases, gains, shifts, hidden), lanes in ((2 * width_l, vectors, width), (2 * width_l + 16, vectors_l, width_l)):
        rows = extra[at : at + 16, :lanes]
        for i, row in enumerate((8, 9, 6, 2)):
            biases[i : i + 1, :] = rows[row : row + 1]
        gains[0:1, :] = rows[4:5]
        gains[1:2, :] = rows[0:1]
        shifts[0:1, :] = rows[5:6]
        shifts[1:2, :] = rows[1:2]
        hidden[...] = extra[pl.ds(at + 12 + info[GROUP], 1), :lanes]


def attend_back_kernel(
    info, qt, kt, vt, ql, kl, vl, dct, dcl, lse,
    dq, dk, dv, dq_l, dk_l, dv_l,
    k_acc, v_acc, kl_acc, vl_acc, ql_acc,
):
    own_rows = qt.shape[0]
    window = kt.shape[0]
    block = window // 2
    pad = (dk.shape[0] - window) // 2
    for acc in (k_acc, v_acc, kl_acc, vl_acc, ql_acc):
        acc[...] = jnp.zeros_like(acc)
    for out in (dk, dv, dk_l, dv_l):
        edge = jnp.zeros((pad, out.shape[1]), BF)
        out[:pad, :] = edge
        out[pad + window :, :] = edge
    lane = lax.broadcasted_iota(jnp.int32, (1, LANES), 1)

    def one_pair(pair, carry):
        text_lanes = lanes_of(pair * LANES)
        group_lanes = lanes_of((pair // 4) * LANES)
        scaled = head_masks(pair, 0.125, 0.25)
        plain = head_masks(pair, 1.0, 1.0)
        for j in range(own_rows // LANES):
            rows = pl.ds(j * LANES, LANES)
            keys_at = pl.ds(pl.multiple_of(info[LOCAL + j] * block, block), block)
            stacked = stack_heads(qt[rows, text_lanes], ql[rows, group_lanes], scaled)
            keys = jnp.concatenate([kt[keys_at, text_lanes], kl[keys_at, group_lanes]], axis=1)
            values = jnp.concatenate([vt[keys_at, text_lanes], vl[keys_at, group_lanes]], axis=1)
            dcs = stack_heads(dct[rows, text_lanes], dcl[rows, group_lanes], plain)
            logs = lse[rows, :]
            log_total = jnp.concatenate(
                [
                    jnp.sum(jnp.where(lane == 2 * pair, logs, 0.0), axis=1, keepdims=True),
                    jnp.sum(jnp.where(lane == 2 * pair + 1, logs, 0.0), axis=1, keepdims=True),
                ],
                axis=0,
            )
            probs = jnp.exp(pair_scores(stacked, keys, info[LIMIT + j]) - log_total)
            dprobs = nt(dcs, values)
            inner = jnp.sum(probs * dprobs, axis=1, keepdims=True)
            dscores = (probs * (dprobs - inner)).astype(BF)
            text, layout = unstack_heads(nn(dscores, keys), scaled)
            dq[rows, text_lanes] = text.astype(BF)
            ql_acc[rows, group_lanes] += layout
            both = tn(dscores, stacked)
            k_acc[keys_at, text_lanes] += both[:, :LANES]
            kl_acc[keys_at, group_lanes] += both[:, LANES:]
            both = tn(probs.astype(BF), dcs)
            v_acc[keys_at, text_lanes] += both[:, :LANES]
            vl_acc[keys_at, group_lanes] += both[:, LANES:]
        return carry

    lax.fori_loop(0, HEADS // 2, one_pair, 0)
    middle = pl.ds(pad, window)
    dk[middle, :] = k_acc[...].astype(BF)
    dv[middle, :] = v_acc[...].astype(BF)
    dk_l[middle, :] = kl_acc[...].astype(BF)
    dv_l[middle, :] = vl_acc[...].astype(BF)
    dq_l[...] = ql_acc[...].astype(BF)


def key_value_grad(info, at, rows_out, wt, wl, dk, dv, dk_l, dv_l):
    width, wide = dk.shape[1], dk_l.shape[1]
    rows = pl.ds(pl.multiple_of(info[SHIFT] + at, LANES), rows_out)
    text = nt(dk[rows, :], wt[:, width : 2 * width]) + nt(dv[rows, :], wt[:, 2 * width :])
    layout = nt(wl[:, wide : 2 * wide], dk_l[rows, :]) + nt(wl[:, 2 * wide :], dv_l[rows, :])
    return text, layout


def store_packed(out, text, layout):
    own_rows = text.shape[0]
    half = layout.shape[0] // 2
    out[:own_rows, :] = text.astype(BF)
    out[own_rows:, :own_rows] = layout[:half].astype(BF)
    out[own_rows:, own_rows:] = layout[half:].astype(BF)


def sides_kernel(info, wt, wl, dk, dv, dk_l, dv_l, left, right):
    own_rows = left.shape[0] * 4 // 5
    for side, shift in ((left, 0), (right, 2 * own_rows)):
        store_packed(side, *key_value_grad(info, shift, own_rows, wt, wl, dk, dv, dk_l, dv_l))


def own_kernel(info, wt, wl, dq, dk, dv, dq_l, dk_l, dv_l, dfirst_t, dfirst_lt, left, right, out):
    own_rows, width = dq.shape
    wide = dq_l.shape[1]
    half = dfirst_lt.shape[0] // 2
    text, layout = key_value_grad(info, own_rows, own_rows, wt, wl, dk, dv, dk_l, dv_l)
    text = dfirst_t[...] + text + nt(dq[...], wt[:, :width])
    layout = dfirst_lt[...] + layout + nt(wl[:, :wide], dq_l[...])
    got = left[...].astype(F32) + right[...].astype(F32)
    text = text + got[:own_rows]
    layout = layout + jnp.concatenate([got[own_rows:, :own_rows], got[own_rows:, own_rows:]], axis=0)
    store_packed(out, text, layout)


def input_final_kernel(info, own, l1, l2, l3, r1, r2, r3, text, layout):
    own_rows, half = own.shape[0] * 4 // 5, layout.shape[0] // 2
    for distance, rows in ((0, own), (-1, l1), (-2, l2), (-3, l3), (1, r1), (2, r2), (3, r3)):
        group = info[GROUP] + distance

        @pl.when((group >= 0) & (group < 4))
        def _():
            at = pl.ds(pl.multiple_of(group * own_rows, LANES), own_rows)
            text[at, :] = rows[:own_rows, :].astype(F32)
            layout[:half, at] = rows[own_rows:, :own_rows].astype(F32)
            layout[half:, at] = rows[own_rows:, own_rows:].astype(F32)


def extras(
    info, xlt, dq, dv, dq_l, dk_l, dv_l, cl, db_l, sums_a, sums_b, hsums, sums_al, sums_bl, hsums_l, extra, small,
):
    own_rows = dq.shape[0]
    wide = dq_l.shape[1]
    width_l = xlt.shape[0]
    window = dk_l.shape[0] - 2 * own_rows
    own = pl.ds(pl.multiple_of(info[OWN], LANES), own_rows)
    seen = pl.ds(pl.multiple_of(info[WINDOW], LANES), window)
    middle = pl.ds(own_rows, window)
    extra[width_l:, :] = jnp.zeros((extra.shape[0] - width_l, extra.shape[1]), BF)
    extra[:width_l, :wide] = nn(xlt[:, own], dq_l[...]).astype(BF)
    extra[:width_l, wide : 2 * wide] = nn(xlt[:, seen], dk_l[middle, :]).astype(BF)
    extra[:width_l, 2 * wide : 3 * wide] = nn(xlt[:, seen], dv_l[middle, :]).astype(BF)
    extra[width_l : 2 * width_l, :width_l] = tn(cl[...], db_l[...]).astype(BF)
    small[...] = jnp.zeros_like(small)
    small[0:4, :] = sums_a[...]
    small[4:8, :] = sums_b[...]
    small[8:9, :] = column_sum(dq[...])
    small[9:10, :] = column_sum(dv[middle, :])
    small[16:20, :width_l] = sums_al[...]
    small[20:24, :width_l] = sums_bl[...]
    small[24:25, :wide] = column_sum(dq_l[...])
    small[25:26, :wide] = column_sum(dv_l[middle, :])
    for s in range(4):
        group = lax.rem(info[GROUP] + s, 4)
        small[pl.ds(12 + group, 1), :] = hsums[s]
        small[pl.ds(28 + group, 1), :width_l] = hsums_l[s]
    extra[2 * width_l : 2 * width_l + 32, :] = small[...].astype(BF)


def copied_grads(info, xt, dq, dk, dv, ct, db, half, store):
    own_rows = dq.shape[0]
    window = dk.shape[0] - 2 * own_rows
    own = pl.ds(pl.multiple_of(info[OWN], LANES), own_rows)
    seen = pl.ds(pl.multiple_of(info[WINDOW], LANES), window)
    middle = pl.ds(own_rows, window)
    for block in range(4):
        if block == 0:
            grad = tn(xt[own, half], dq[...])
        elif block == 1:
            grad = tn(xt[seen, half], dk[middle, :])
        elif block == 2:
            grad = tn(xt[seen, half], dv[middle, :])
        else:
            grad = tn(ct[:, half], db[...])
        store(block, info[SLOT + block], grad)


def copied_send_kernel(
    info, xt, dq, dk, dv, ct, db, xlt, dq_l, dk_l, dv_l, cl, db_l, sums_a, sums_b, hsums, sums_al, sums_bl, hsums_l,
    send, extra, small,
):
    half = pl.ds(pl.multiple_of(info[HALF + 1], LANES), 384)
    extras(info, xlt, dq, dv, dq_l, dk_l, dv_l, cl, db_l, sums_a, sums_b, hsums, sums_al, sums_bl, hsums_l, extra, small)

    def store(block, slot, grad):
        send[slot, :384] = grad.astype(BF)
        send[slot, 384:] = extra[pl.ds(pl.multiple_of(128 * block + info[HALF + 1] // 6, 64), 64), :]

    copied_grads(info, xt, dq, dk, dv, ct, db, half, store)


def copied_keep_kernel(info, xt, dq, dk, dv, ct, db, extra, recv, next_a, keep_a, next_b, keep_b, total):
    half = pl.ds(pl.multiple_of(info[HALF], LANES), 384)

    def store(block, slot, grad):
        more = pl.ds(pl.multiple_of(128 * block + info[HALF] // 6, 64), 64)
        total[slot, :384] = (grad + recv[slot, :384].astype(F32)).astype(BF)
        total[slot, 384:] = (extra[more, :].astype(F32) + recv[slot, 384:].astype(F32)).astype(BF)

    copied_grads(info, xt, dq, dk, dv, ct, db, half, store)
    for slot in range(4):
        for rel in range(4):
            x_part, y_part = rel % 2, rel // 2
            first, second = (x_part, y_part) if slot < 2 else (y_part, x_part)
            out = ((keep_a, next_a), (keep_b, next_b))[slot // 2][first].at[second, slot % 2]
            out[:96] = total[slot, pl.ds(pl.multiple_of(info[PIECE + rel], 32), 96), :]
            out[96:] = total[slot, pl.ds(pl.multiple_of(384 + info[PIECE + rel] // 6, EXTRA), EXTRA), :]


SM = pl.BlockSpec(memory_space=pltpu.SMEM)
VM = pl.BlockSpec(memory_space=pltpu.VMEM)
HB = pl.BlockSpec(memory_space=pl.ANY)


def vmem_of(operands, outs, scratch):
    held = list(operands) + list(outs) + [v for v in scratch if str(v.memory_space) == "vmem"]
    return int(1.1 * sum(math.prod(v.shape) * jnp.dtype(v.dtype).itemsize for v in held)) + (8 << 20)


def call(name, kernel, operands, outs, scratch=(), after=(), in_hbm=0):
    operands = tuple(operands)
    outs = tuple(outs) + (shape((8, LANES), F32),)
    specs = [HB] * len(after) + [SM] + [VM] * (len(operands) - 1 - in_hbm) + [pl.BlockSpec(memory_space=pltpu.HBM)] * in_hbm
    limit = vmem_of(operands[1 : len(operands) - in_hbm], outs, scratch)
    operands = tuple(after) + operands
    at = len(operands) + len(outs) - 1

    def with_token(*refs):
        kernel(*refs[len(after) : at], *refs[at + 1 :])
        refs[at][...] = jnp.zeros_like(refs[at])

    return pl.pallas_call(
        with_token,
        out_shape=outs,
        in_specs=specs,
        out_specs=[VM] * len(outs),
        scratch_shapes=list(scratch),
        cost_estimate=pl.CostEstimate(flops=int(MICROSECONDS[name] * PER_MICROSECOND), bytes_accessed=0, transcendentals=0),
        compiler_params=pltpu.CompilerParams(vmem_limit_bytes=limit),
        name=name,
    )(*operands)


def shape(dims, dtype=BF):
    return jax.ShapeDtypeStruct(dims, dtype)


def flip(planes, bit):
    return [(i, i ^ bit) for i in range(planes)]


def gate(values, *tokens):
    outs = pl.pallas_call(
        lambda *refs: None,
        out_shape=tuple(shape(v.shape, v.dtype) for v in values),
        in_specs=[HB] * (len(values) + len(tokens)),
        out_specs=[HB] * len(values),
        input_output_aliases={i: i for i in range(len(values))},
        cost_estimate=pl.CostEstimate(flops=0, bytes_accessed=0, transcendentals=0),
        compiler_params=pltpu.CompilerParams(vmem_limit_bytes=1 << 20),
        name="gate",
    )(*values, *tokens)
    return list(outs)


def around(planes):
    return lambda v, bit: lax.ppermute(v, "dp", flip(planes, bit))


def forward(piece, by_x, by_y, planes, split, mid=None):
    across, parts = around(planes), piece.shape[0]
    if split == "x":
        return [(across(by_x, Y), 3, 0, parts)]
    if split == "y":
        return [(across(by_y, X), 3, 0, parts)]
    mid = mid or parts // 2
    return [(across(by_x[:mid], Y), 3, 0, mid), (across(by_y[mid:], X), 3, mid, parts)]


def to_core(held, planes):
    across = around(planes)
    held = held + [(across(v, CORE), rel + 4, low, high) for v, rel, low, high in held]
    return [h[0] for h in held], tuple(h[1:] for h in held)


def spread(piece, planes, mid=None):
    across, parts = around(planes), piece.shape[0]
    by_x, by_y = across(piece, X), across(piece, Y)
    held = [(piece, 0, 0, parts), (by_x, 1, 0, parts), (by_y, 2, 0, parts)]
    return to_core(held + forward(piece, by_x, by_y, planes, "half", mid), planes)


def per_device(
    text_input, layout_input, block_starts, intersection_flags, text_cotangent, layout_cotangent,
    text_project, text_biases, text_dense, text_gains, text_shifts, text_widen, text_hidden_bias, text_narrow,
    layout_project, layout_biases, layout_dense, layout_gains, layout_shifts, layout_widen, layout_hidden_bias,
    layout_narrow,
):
    blocks, length = intersection_flags.shape
    total = blocks * length
    groups = lax.axis_size("tensor")
    planes = lax.axis_size("dp")
    own = total // groups
    tiles = own // LANES
    width = text_input.shape[1]
    width_l = layout_input.shape[1]
    wide = 2 * LANES
    window = 2 * length
    padded = window + 2 * own
    hid = text_narrow.shape[0]
    hid_l = layout_narrow.shape[0]
    piece = width // PIECES
    t = lax.axis_index("tensor").astype(jnp.int32)
    me = lax.axis_index("dp").astype(jnp.int32)
    core, x_bit, y_bit = me & 1, (me >> 1) & 1, (me >> 2) & 1

    def row_of(rc, rx, ry):
        return 4 * piece * (core ^ rc) + piece * ((x_bit ^ rx) + 2 * (y_bit ^ ry))

    flagged = jnp.sum(intersection_flags, axis=1, dtype=jnp.int32)
    base = jnp.minimum((t * own) // length, blocks - 2)
    tile_rows = t * own + LANES * jnp.arange(tiles, dtype=jnp.int32)
    tile_block = tile_rows // length
    pick = tile_block[:, None] == jnp.arange(blocks, dtype=jnp.int32)[None, :]
    limit = DOC - jnp.sum(jnp.where(pick, block_starts[None, :], 0), axis=1)
    flags_of = jnp.sum(jnp.where(pick, flagged[None, :], 0), axis=1)
    info = jnp.concatenate(
        [
            jnp.stack([t * own, base * length, t * own - base * length]),
            tile_block - base,
            limit,
            flags_of,
            tile_rows - tile_block * length,
            jnp.stack(
                [t, 4 * piece * core, 4 * piece * (1 - core)]
                + [row_of(0, rx, ry) - 4 * piece * core for ry in (0, 1) for rx in (0, 1)]
                + [(b - t) % groups for b in range(4)]
            ),
        ]
    ).astype(jnp.int32)

    shift_from = lambda k: [(i, (i - k) % groups) for i in range(groups)]
    shift_to = lambda k: [(i, (i + k) % groups) for i in range(groups)]
    bias = jnp.concatenate([text_hidden_bias, layout_hidden_bias, jnp.zeros((8 * LANES - hid - hid_l,), F32)])
    across = around(planes)
    row = row_of(0, 0, 0)
    mine, packed_up = call(
        "pack", pack_kernel,
        (jnp.zeros((1,), jnp.int32),
         jnp.concatenate([lax.dynamic_slice_in_dim(v, row, piece, 0) for v in (text_widen, text_narrow)], axis=0),
         jnp.concatenate([lax.dynamic_slice_in_dim(v, row // 4, piece // 4, 0) for v in (layout_widen, layout_narrow)], axis=0),
         bias.reshape(8, LANES)),
        (shape((2 * piece + 32, width)),),
    )
    from_group = lambda v, k: lax.ppermute(v, "tensor", shift_from(k))
    come = {k: from_group(mine, k) for k in (1, 3)}

    xlt = layout_input.T
    qt, kt, vt, ql, kl, vl, xl_own, wl, projected = call(
        "project", project_kernel,
        (info, text_input, xlt, text_project, layout_project, text_biases, layout_biases),
        (shape((own, width)), shape((window, width)), shape((window, width)),
         shape((own, wide)), shape((window, wide)), shape((window, wide)),
         shape((own, width_l)), shape((width_l, 3 * wide))),
        after=(packed_up,),
    )
    mine_again, come[1], come[3] = gate((mine, come[1], come[3]), projected)
    come[2] = from_group(mine_again, 2)
    by_x, by_y = {}, {}
    for k in (1, 3):
        by_x[k], by_y[k] = across(come[k], X), across(come[k], Y)
    ct, cl, lse, attended = call(
        "attend", attend_kernel,
        (info, qt, kt, vt, ql, kl, vl),
        (shape((own, width)), shape((own, width_l)), shape((own, LANES), F32)),
        scratch=(pltpu.VMEM((own, wide), F32),),
    )
    by_x[1], by_y[3] = gate((by_x[1], by_y[3]), attended)
    forwarded = {k: forward(come[k], by_x[k], by_y[k], planes, {1: "x", 3: "y"}[k]) for k in (1, 3)}
    first_t, first_l, low_t, low_l, normed_l, active0, slope0, total_t, first_done = call(
        "first_norm", first_norm_kernel,
        (info, text_input, xl_own, ct, cl, text_dense, layout_dense, text_biases, layout_biases,
         text_gains, text_shifts, layout_gains, layout_shifts, text_widen, mine, text_narrow),
        (shape((own, width), F32), shape((own, width_l), F32), shape((own, width)), shape((own, width_l)),
         shape((own, width_l), F32), shape((own, hid)), shape((own, hid), F32), shape((own, width), F32)),
        after=(by_y[1], by_x[3]),
    )
    both = gate((forwarded[1][0][0], forwarded[3][0][0]), first_done)
    shards = {}
    for k, array in zip((1, 3), both):
        parts = come[k].shape[0]
        held = [(come[k], 0, 0, parts), (by_x[k], 1, 0, parts), (by_y[k], 2, 0, parts), (array, 3, 0, parts)]
        shards[k] = to_core(held, planes)
    by_x[2], by_y[2] = across(come[2], X), across(come[2], Y)
    actives, slopes, shard_weights, layouts, shard_done = {0: active0}, {0: slope0}, {}, {}, {}
    for k in (1, 3):
        arrays, plan = shards[k]
        actives[k], slopes[k], total_t, shard_weights[k], layouts[k], shard_done[k] = call(
            "shard", functools.partial(shard_kernel, plan),
            (info, low_t, total_t, *arrays),
            (shape((own, hid)), shape((own, hid), F32), shape((own, width), F32), shape((2, width, hid)),
             shape((width_l, 2 * wide))),
            scratch=(pltpu.VMEM((width_l, 2 * wide), F32),),
            after=(by_x[2], by_y[2]) if k == 3 else (),
        )
    last = forward(come[2], by_x[2], by_y[2], planes, "half", 96)
    last = [(v,) + f[1:] for v, f in zip(gate([f[0] for f in last], shard_done[3]), last)]
    parts = come[2].shape[0]
    shards[2] = to_core([(come[2], 0, 0, parts), (by_x[2], 1, 0, parts), (by_y[2], 2, 0, parts)] + last, planes)
    arrays, plan = shards[2]
    rows_a = piece + EXTRA
    outs = call(
        "turn", functools.partial(turn_kernel, plan),
        (info, low_t, total_t, text_gains, text_shifts, text_cotangent, text_widen, text_narrow,
         slopes[0], slopes[1], slopes[3], actives[0], actives[1], actives[3],
         low_l, normed_l, layout_gains, layout_shifts, layout_cotangent.T, layout_widen, layout_narrow, layouts[1], layouts[3],
         mine, come[1], come[3],         shard_weights[1], shard_weights[3], *arrays),
        (shape((own, width)), shape((own, width)), shape((groups, own, hid)), shape((own, width), F32),
         shape((4, width), F32), shape((groups, 1, hid), F32), shape((own, hid)),
         shape((width_l, own)), shape((own, width_l), F32), shape((4, width_l), F32), shape((groups, 1, hid_l), F32),
         shape((groups, 4 * rows_a, width)), shape((groups, 4 * piece, width)), shape((groups, 128, width))),
        scratch=(pltpu.VMEM((2, width, hid), BF), pltpu.VMEM((own, hid), F32),
                 pltpu.VMEM((groups, own, hid_l), F32), pltpu.VMEM((groups, own, hid_l), BF),
                 pltpu.VMEM((groups, own, hid_l), BF), pltpu.VMEM((own, width_l), BF), pltpu.VMEM((own, width_l), BF),
                 pltpu.VMEM((width_l, 2 * wide), F32)),
    )
    result_t, dout_t, dhid_t, dnormed_t, sums_t, hsums_t, actives[2] = outs[:7]
    result_lt, dnormed_l, sums_l, hsums_l, send_a, send_b, pack, turned = outs[7:]

    in_order = [actives[k] for k in range(4)]
    recv_a, recv_b = across(send_a, CORE), across(send_b, CORE)
    dfirst_t, db_t, dc_t, low_sums_t, dfirst_lt, db_l, dc_l, low_sums_l, lowered = call(
        "lower", lower_kernel,
        (info, first_t, dnormed_t, text_gains, text_dense, first_l, dnormed_l, layout_gains, layout_dense),
        (shape((own, width), F32), shape((own, width)), shape((own, width)), shape((4, width), F32),
         shape((width_l, own), F32), shape((own, width_l)), shape((own, wide)), shape((4, width_l), F32)),
        scratch=(pltpu.VMEM((own, width_l), F32),),
    )
    next_a1, next_a2, next_b1, next_b2, keep_a, keep_b, kept = call(
        "ffn_keep", ffn_keep_kernel,
        (info, *in_order, dout_t, low_t, dhid_t, recv_a, recv_b, pack),
        (shape((2, 2, rows_a, width)),) * 2 + (shape((2, 2, piece, width)),) * 2
        + (shape((2, groups, rows_a, width)), shape((2, groups, piece, width))),
        scratch=(pltpu.VMEM((4 * rows_a, width), BF), pltpu.VMEM((4 * piece, width), BF)), after=(lowered,),
    )
    recv_a1, recv_b1 = across(next_a1, X), across(next_b1, Y)

    dq, dk, dv, dq_l, dk_l, dv_l, attended_back = call(
        "attend_back", attend_back_kernel,
        (info, qt, kt, vt, ql, kl, vl, dc_t, dc_l, lse),
        (shape((own, width)), shape((padded, width)), shape((padded, width)),
         shape((own, wide)), shape((padded, wide)), shape((padded, wide))),
        scratch=(pltpu.VMEM((window, width), F32), pltpu.VMEM((window, width), F32),
                 pltpu.VMEM((window, wide), F32), pltpu.VMEM((window, wide), F32), pltpu.VMEM((own, wide), F32)),
        after=(kept,),
    )
    copied_in = (text_input, dq, dk, dv, ct, db_t)
    send, extra, sent = call(
        "copied_send", copied_send_kernel,
        (info,) + copied_in + (xlt, dq_l, dk_l, dv_l, cl, db_l, sums_t, low_sums_t, hsums_t, sums_l, low_sums_l, hsums_l),
        (shape((groups, 4 * rows_a, width)), shape((4 * 128, width))),
        scratch=(pltpu.VMEM((32, width), F32),), after=(recv_a1, recv_b1),
    )
    packed = shape((own + own // 4, width))
    left, right, sided = call(
        "sides", sides_kernel, (info, text_project, wl, dk, dv, dk_l, dv_l), (packed, packed), after=(sent,)
    )
    recv_a2, recv_b2 = across(next_a2, X), across(next_b2, Y)
    from_right = lax.ppermute(left, "tensor", [(i + 1, i) for i in range(groups - 1)])
    from_left = lax.ppermute(right, "tensor", [(i, i + 1) for i in range(groups - 1)])

    recv = across(send, CORE)
    copied_next_a, copied_keep_a, copied_next_b, copied_keep_b, copied_kept = call(
        "copied_keep", copied_keep_kernel, (info,) + copied_in + (extra, recv),
        (shape((2, 2, rows_a, width)),) * 4,
        scratch=(pltpu.VMEM((groups, 4 * rows_a, width), BF),),
    )
    copied_recv_a, copied_recv_b = across(copied_next_a, X), across(copied_next_b, Y)
    own_sum, owned = call(
        "own", own_kernel,
        (info, text_project, wl, dq, dk, dv, dq_l, dk_l, dv_l, dfirst_t, dfirst_lt, from_right, from_left),
        (packed,), after=(copied_kept, recv_a2, recv_b2),
    )
    step_right = lambda v, far: lax.ppermute(v, "tensor", [(i, i + 1) for i in range(far, groups - 1)])
    step_left = lambda v, far: lax.ppermute(v, "tensor", [(i, i - 1) for i in range(groups - 1 - far, 0, -1)])
    lefts, rights = [step_right(own_sum, 0)], [step_left(own_sum, 0)]
    to_group = lambda v, k: lax.ppermute(v, "tensor", shift_to(k))

    def across_planes(value):
        bit = PIECES
        while bit < planes:
            value = add(value, across(value, bit))
            bit *= 2
        return value

    copied_next_a, copied_keep_a = add_split(copied_keep_a, copied_recv_a)
    copied_next_b, copied_keep_b = add_split(copied_keep_b, copied_recv_b)
    copied_recv_a, copied_recv_b = across(copied_next_a, Y), across(copied_next_b, X)
    *parts, copied_spreaded = call(
        "copied_spread", copied_spread_kernel, (info, copied_keep_a, copied_recv_a, copied_keep_b, copied_recv_b),
        (shape((rows_a, width)),) * 4,
        after=(lefts[0], rights[0]),
    )
    parts = [parts[0]] + [to_group(parts[k], k) for k in (1, 2, 3)]
    summed = across_planes(add(*parts))
    next_a, keep_a = add_split(keep_a, jnp.concatenate([recv_a1, recv_a2], axis=1), copied_spreaded)
    next_b, keep_b = add_split(keep_b, jnp.concatenate([recv_b1, recv_b2], axis=1), copied_spreaded)
    recv_a, recv_b = across(next_a, Y), across(next_b, X)
    ffn_parts, ffn_spreaded = call(
        "ffn_spread", ffn_spread_kernel, (info, keep_a, recv_a, keep_b, recv_b),
        (shape((groups, rows_a + piece, width)),), after=(summed,),
    )
    ffn_summed = lax.psum_scatter(ffn_parts, "tensor", scatter_dimension=0, tiled=False)
    ffn_arrays, ffn_plan = spread(across_planes(ffn_summed), planes, rows_a)
    every = [summed] + [from_group(summed, k) for k in (1, 2, 3)]
    left, right = gate((lefts[0], rights[0]), every[1], every[2], every[3])
    lefts, rights = [left], [right]
    for far in (1, 2):
        lefts.append(step_right(lefts[-1], far))
        rights.append(step_left(rights[-1], far))
    g_narrow, g_widen, g_narrow_l, g_widen_l, ffn_done = call(
        "ffn_final", functools.partial(ffn_final_kernel, ffn_plan), (info, *ffn_arrays),
        (shape((hid, width), F32), shape((width, hid), F32), shape((hid_l, width_l), F32), shape((width_l, hid_l), F32)),
        scratch=(pltpu.VMEM((128, width), F32),),
    )
    arrays, plan = spread(jnp.stack(every), planes)
    vectors = lambda w, h: (shape((4, w), F32), shape((2, w), F32), shape((2, w), F32), shape((1, h), F32))
    outs = call(
        "copied_final", functools.partial(copied_final_kernel, plan), (info, *arrays),
        (shape((width, 3 * width), F32), shape((width, width), F32),
         shape((width_l, 3 * width_l), F32), shape((width_l, width_l), F32)) + vectors(width, hid) + vectors(width_l, hid_l),
        scratch=(pltpu.VMEM((4 * 128, width), F32),),
    )
    text_grad, layout_grad_t, given = call(
        "input_final", input_final_kernel, (info, own_sum, *lefts, *rights),
        (shape((total, width), F32), shape((width_l, total), F32)),
        after=(ffn_done, outs[-1]),
    )
    g_project, g_dense, g_project_l, g_dense_l = outs[:4]
    bias_t, gain_t, shift_t, hb_t, bias_l, gain_l, shift_l, hb_l = outs[4:12]
    return (
        result_t, result_lt.T, text_grad, layout_grad_t.T,
        g_project, bias_t, g_dense, gain_t, shift_t, g_widen, hb_t[0], g_narrow,
        g_project_l, bias_l, g_dense_l, gain_l, shift_l, g_widen_l, hb_l[0], g_narrow_l,
    )


def solution(mesh):
    rows = P(("dp", "tensor"), None)
    weights = (P(), P(), P(), P(), P(), P(None, "tensor"), P("tensor"), P("tensor", None))
    return jax.shard_map(
        per_device,
        mesh=mesh,
        in_specs=(P("dp", None), P("dp", None), P("dp"), P("dp", None), rows, rows) + weights + weights,
        out_specs=(rows, rows, P("dp", None), P("dp", None)) + weights + weights,
        check_vma=False,
    )
```

```python
import functools
import math

import jax
import jax.numpy as jnp
from jax import lax
from jax.experimental import pallas as pl
from jax.experimental.pallas import tpu as pltpu
from jax.sharding import PartitionSpec as P

HEADS = 12
DOC = 2048
LANES = 128
epsilon = 1e-05
masked_score = -1e30
F32 = jnp.float32
BF = jnp.bfloat16

OWN, WINDOW, SHIFT, LOCAL, LIMIT, FLAGGED, PLACE, GROUP, HALF, PIECE, SLOT = 0, 1, 2, 3, 6, 9, 12, 15, 16, 18, 22
PIECES = 8
MARGIN = 8
CORE, X, Y = 1, 2, 4
PER_MICROSECOND = 0.2e9
MICROSECONDS = {
    "pack": 1, "project": 5, "attend": 9, "first_norm": 3, "shard": 3, "turn": 12, "ffn_send": 4, "ffn_keep": 4, "ffn_spread": 1,
    "attend_back": 15, "copied_send": 4, "sides": 3, "copied_keep": 3, "own": 3, "input_final": 4,
    "ffn_final": 3, "copied_spread": 1, "copied_final": 6,
}


def nn(a, b):
    return lax.dot_general(a, b, (((1,), (0,)), ((), ())), preferred_element_type=F32)


def nt(a, b):
    return lax.dot_general(a, b, (((1,), (1,)), ((), ())), preferred_element_type=F32)


def tn(a, b):
    return lax.dot_general(a, b, (((0,), (0,)), ((), ())), preferred_element_type=F32)


def mean(values):
    return jnp.mean(values, axis=-1, keepdims=True)


def column_sum(values):
    return jnp.sum(values.astype(F32), axis=0, keepdims=True)


def normalised(values):
    centre = values - mean(values)
    scale = lax.rsqrt(mean(centre * centre) + epsilon)
    return centre * scale, scale


def norm_back(upstream, normal, scale, gain_row):
    u = upstream * gain_row
    return scale * (u - mean(u) - normal * mean(u * normal))


def lanes_of(start):
    return pl.ds(pl.multiple_of(start, LANES), LANES)


def head_masks(pair, text_scale, layout_scale):
    lane = lax.broadcasted_iota(jnp.int32, (1, LANES), 1)
    first = 32 * pair - LANES * (pair // 4)
    text_a = jnp.where(lane < 64, text_scale, 0.0)
    text_b = jnp.where(lane < 64, 0.0, text_scale)
    layout_a = jnp.where((lane >= first) & (lane < first + 16), layout_scale, 0.0)
    layout_b = jnp.where((lane >= first + 16) & (lane < first + 32), layout_scale, 0.0)
    return text_a, layout_a, text_b, layout_b


def stack_heads(text, layout, masks):
    text_a, layout_a, text_b, layout_b = (m.astype(BF) for m in masks)
    upper = jnp.concatenate([text * text_a, layout * layout_a], axis=1)
    lower = jnp.concatenate([text * text_b, layout * layout_b], axis=1)
    return jnp.concatenate([upper, lower], axis=0)


def unstack_heads(stacked, masks):
    text_a, layout_a, text_b, layout_b = masks
    upper, lower = stacked[:LANES], stacked[LANES:]
    text = upper[:, :LANES] * text_a + lower[:, :LANES] * text_b
    layout = upper[:, LANES:] * layout_a + lower[:, LANES:] * layout_b
    return text, layout


def pair_scores(stacked, keys, limit):
    scores = nt(stacked, keys)
    key = lax.broadcasted_iota(jnp.int32, (1, scores.shape[1]), 1)
    return jnp.where(key < limit, scores, masked_score)


def pack_kernel(place, weights, layout, bias, mine):
    mine[:192] = weights[...]
    width_l = layout.shape[1]
    high = bias[...].astype(BF).astype(F32)
    middle = (bias[...] - high).astype(BF).astype(F32)
    low = bias[...] - high - middle
    biases = jnp.concatenate([high, middle, low, jnp.zeros_like(low)], axis=0)
    mine[192:, :] = jnp.zeros((32, mine.shape[1]), BF)
    empty = jnp.zeros((8, width_l), F32)
    both = layout[...].astype(F32)
    mine[192:, :width_l] = jnp.concatenate([both[:24], empty], axis=0).astype(BF)
    mine[192:, 256 : 256 + width_l] = jnp.concatenate([both[24:], empty], axis=0).astype(BF)
    mine[192:, 512:640] = biases.astype(BF)


def biases_of(rest):
    split = rest[:, 512:640].astype(F32)
    rows = split[:8] + split[8:16] + split[16:24]
    text = jnp.concatenate([rows[i : i + 1] for i in range(6)], axis=1)
    layout = jnp.concatenate([rows[i : i + 1] for i in (6, 7)], axis=1)
    return text, layout


def identity(size):
    row = lax.broadcasted_iota(jnp.int32, (size, size), 0)
    column = lax.broadcasted_iota(jnp.int32, (size, size), 1)
    return jnp.where(row == column, 1.0, 0.0).astype(BF)


def project_kernel(info, xt, xlt, wt, wl, bt, bl, qt, kt, vt, ql, kl, vl, xl_own, wide_l):
    own_rows, width = qt.shape
    wide = ql.shape[1]
    width_l = wl.shape[0]
    own = pl.multiple_of(info[OWN], LANES)
    start = pl.multiple_of(info[WINDOW], LANES)
    rows = pl.ds(own, own_rows)
    for i in range(3):
        wide_l[:, i * wide : i * wide + width_l] = wl[:, i * width_l : (i + 1) * width_l]
        wide_l[:, i * wide + width_l : (i + 1) * wide] = jnp.zeros((width_l, wide - width_l), BF)
    edge = jnp.zeros((1, wide - width_l), F32)
    bias = [jnp.concatenate([bl[i : i + 1, :], edge], axis=1) for i in (0, 1)]
    qt[...] = (nn(xt[rows, :], wt[:, :width]) + bt[0:1, :]).astype(BF)
    ql[...] = (tn(xlt[:, rows], wide_l[:, :wide]) + bias[0]).astype(BF)
    xl_own[...] = tn(xlt[:, rows], identity(width_l)).astype(BF)

    def part(i, carry):
        rows = pl.ds(pl.multiple_of(i * 256, 256), 256)
        from_rows = pl.ds(pl.multiple_of(start + i * 256, 256), 256)
        x = xt[from_rows, :]
        kt[rows, :] = nn(x, wt[:, width : 2 * width]).astype(BF)
        vt[rows, :] = (nn(x, wt[:, 2 * width :]) + bt[1:2, :]).astype(BF)
        x = xlt[:, from_rows]
        kl[rows, :] = tn(x, wide_l[:, wide : 2 * wide]).astype(BF)
        vl[rows, :] = (tn(x, wide_l[:, 2 * wide :]) + bias[1]).astype(BF)
        return carry

    lax.fori_loop(0, kt.shape[0] // 256, part, 0)


def attend_kernel(info, qt, kt, vt, ql, kl, vl, ct, cl, lse, cl_acc):
    own_rows, layout_width = cl.shape
    block = kt.shape[0] // 2
    cl_acc[...] = jnp.zeros_like(cl_acc)
    lse[...] = jnp.zeros_like(lse)
    lane = lax.broadcasted_iota(jnp.int32, (1, LANES), 1)

    def one_pair(pair, carry):
        text_lanes = lanes_of(pair * LANES)
        group_lanes = lanes_of((pair // 4) * LANES)
        scaled = head_masks(pair, 0.125, 0.25)
        plain = head_masks(pair, 1.0, 1.0)
        for j in range(own_rows // LANES):
            rows = pl.ds(j * LANES, LANES)
            keys_at = pl.ds(pl.multiple_of(info[LOCAL + j] * block, block), block)
            stacked = stack_heads(qt[rows, text_lanes], ql[rows, group_lanes], scaled)
            keys = jnp.concatenate([kt[keys_at, text_lanes], kl[keys_at, group_lanes]], axis=1)
            values = jnp.concatenate([vt[keys_at, text_lanes], vl[keys_at, group_lanes]], axis=1)
            scores = pair_scores(stacked, keys, info[LIMIT + j])
            highest = jnp.max(scores, axis=-1, keepdims=True)
            exponent = jnp.exp(scores - highest)
            totals = jnp.sum(exponent, axis=-1, keepdims=True)
            probs = (exponent * (1.0 / totals)).astype(BF)
            text, layout = unstack_heads(nn(probs, values), plain)
            ct[rows, text_lanes] = text.astype(BF)
            cl_acc[rows, group_lanes] += layout
            log_total = highest + jnp.log(totals)
            lse[rows, :] = (
                lse[rows, :]
                + jnp.where(lane == 2 * pair, log_total[:LANES], 0.0)
                + jnp.where(lane == 2 * pair + 1, log_total[LANES:], 0.0)
            )
        return carry

    lax.fori_loop(0, HEADS // 2, one_pair, 0)
    cl[...] = cl_acc[:, :layout_width].astype(BF)


def gelu_both(hidden):
    below = 0.5 * (1.0 + lax.erf(hidden * math.sqrt(0.5)))
    density = jnp.exp(-0.5 * hidden * hidden) * (1.0 / math.sqrt(2.0 * math.pi))
    return hidden * below, below + hidden * density


def shard_forward(low, widen, bias, narrow, active, slope, total):
    hid = widen.shape[1]
    step = 256 if hid % 256 == 0 else hid
    for n in range(hid // step):
        cols = slice(n * step, (n + 1) * step)
        value, gradient = gelu_both(nn(low[...], widen[:, cols]) + bias[:, cols])
        active[:, cols] = value.astype(BF)
        slope[:, cols] = gradient
    total[...] += nn(active[...], narrow[...])


def shard_backward(dout, narrow, slope, widen, dhid, sums, total):
    hid = widen.shape[1]
    step = 256 if hid % 256 == 0 else hid
    for n in range(hid // step):
        cols = slice(n * step, (n + 1) * step)
        dhidden = (nt(dout[...], narrow[cols, :]) * slope[:, cols]).astype(BF)
        dhid[:, cols] = dhidden
        sums[:, cols] = column_sum(dhidden)
    total[...] += nt(dhid[...], widen[...])


def first_norm_kernel(
    info, xt, xl_own, ct, cl, dense_t, dense_l, bt, bl, gt, st, gl, sl, widen, hidden, narrow,
    first_t, first_l, low_t, low_l, normed_l, active, slope, total,
):
    own_rows, width = first_t.shape
    rows = pl.ds(pl.multiple_of(info[OWN], LANES), own_rows)
    first = xt[rows, :].astype(F32) + (nn(ct[...], dense_t[...]) + bt[2:3, :])
    first_t[...] = first
    normed = normalised(first)[0] * gt[0:1, :] + st[0:1, :]
    low_t[...] = normed.astype(BF)
    total[...] = normed + bt[3:4, :]
    first = xl_own[...].astype(F32) + (nn(cl[...], dense_l[...]) + bl[2:3, :])
    first_l[...] = first
    normed = normalised(first)[0] * gl[0:1, :] + sl[0:1, :]
    low_l[...] = normed.astype(BF)
    normed_l[...] = normed + bl[3:4, :]
    shard_forward(low_t, widen, biases_of(hidden[192:, :])[0], narrow, active, slope, total)


def piece_rows(info, rel):
    return pl.ds(pl.multiple_of(info[HALF + rel // 4] + info[PIECE + rel % 4], 32), 96)


def place_shard(info, plan, refs, weights):
    for ref, (rel, low, high) in zip(refs, plan):
        for part in (0, 1):
            if low <= 96 * part and high >= 96 * (part + 1):
                weights[part, piece_rows(info, rel), :] = ref[96 * part - low : 96 * (part + 1) - low, :]


def place_layout(info, plan, refs, both):
    for ref, (rel, low, high) in zip(refs, plan):
        if high == 224:
            at = pl.multiple_of((info[HALF + rel // 4] + info[PIECE + rel % 4]) // 4, 8)
            both[pl.ds(at, 24), :] = ref[192 - low :, :512].astype(F32)[:24]


def shard_kernel(plan, info, low, total_in, *refs):
    pieces = refs[: len(plan)]
    active, slope, total, weights, layout, both = refs[len(plan) :]
    place_shard(info, plan, pieces, weights)
    place_layout(info, plan, pieces, both)
    layout[...] = both[...].astype(BF)
    total[...] = total_in[...]
    bias = biases_of(pieces[0][192:, :])[0]
    shard_forward(low, weights.at[0], bias, weights.at[1], active, slope, total)


def upper_back(total, gain, shift, cot, keep, result, dout, sums):
    normal, scale = normalised(total[...])
    result[...] = (normal * gain[1:2, :] + shift[1:2, :]).astype(BF)
    upstream = cot.astype(F32) * keep
    dsecond = norm_back(upstream, normal, scale, gain[1:2, :])
    dout[...] = dsecond.astype(BF)
    sums[0:1, :] = column_sum(upstream * normal)
    sums[1:2, :] = column_sum(upstream)
    sums[2:3, :] = column_sum(dout[...])
    sums[3:4, :] = jnp.zeros_like(sums[3:4, :])
    total[...] = dsecond


def turn_kernel(plan, info, *refs):
    refs = list(refs)
    take = lambda n: [refs.pop(0) for _ in range(n)]
    low, total_in, gain, shift, cot, widen_own, narrow_own = take(7)
    slopes_in, actives = take(3), take(3)
    low_l, normed_l, gain_l, shift_l, cot_lt = take(5)
    first, first_l, dense, dense_l = take(4)
    widen_own_l, narrow_own_l, layout_one, layout_three, mine, first_piece, third_piece = take(7)
    weights_one, weights_three = take(2)
    pieces = take(len(plan))
    result, dout, dhid, sums, hsums, active = take(6)
    result_lt, sums_l, hsums_l, pack = take(4)
    lower, lower_l = take(4), take(4)
    weights, slope, dnormed, slope_l, active_l, dhid_l, dout_l, result_l, dnormed_l, dfirst_l, both = take(11)
    shards = dhid.shape[0]
    width = low.shape[1]
    dnormed[...] = total_in[...]
    dnormed_l[...] = normed_l[...]
    row = lax.broadcasted_iota(jnp.int32, (LANES, 1), 0)
    keep = []
    for j in range(low.shape[0] // LANES):
        place = row + info[PLACE + j]
        keep.append(jnp.where((place >= info[FLAGGED + j]) & (place < info[LIMIT + j]), 1.0, 0.0))
    keep = jnp.concatenate(keep, axis=0)

    width_l = low_l.shape[1]
    hidden_bias = [biases_of(ref[192:, :]) for ref in (mine, first_piece, pieces[0], third_piece)]
    place_layout(info, plan, pieces, both)
    last_l = both[...].astype(BF)
    layouts = [(widen_own_l[...], narrow_own_l[...])]
    layouts += [(v[:, :width_l], v[:, 256 : 256 + width_l]) for v in (layout_one[...], last_l, layout_three[...])]
    for s in range(shards):
        widen, narrow = layouts[s]
        shard_forward(low_l, widen, hidden_bias[s][1][:, :width_l], narrow, active_l.at[s], slope_l.at[s], dnormed_l)
    cot_l = tn(cot_lt[...], identity(width_l))
    upper_back(dnormed_l, gain_l, shift_l, cot_l, keep, result_l, dout_l, sums_l)
    result_lt[...] = nt(identity(width_l), result_l[...]).astype(BF)
    for s in range(shards):
        widen, narrow = layouts[s]
        shard_backward(dout_l, narrow, slope_l.at[s], widen, dhid_l.at[s], hsums_l.at[s], dnormed_l)
    for s in range(shards):
        pack[s] = jnp.zeros_like(pack[s])
        g = tn(active_l[s], dout_l[...]).astype(BF)
        pack[s, :128, :width_l] = g[:128]
        pack[s, :64, 512 : 512 + width_l] = g[128:]
        g = tn(low_l[...], dhid_l[s]).astype(BF)
        pack[s, :128, 256 : 256 + width_l] = g[:128]
        pack[s, 64:, 512 : 512 + width_l] = g[128:]

    place_shard(info, plan, pieces, weights)
    shard_forward(low, weights.at[0], hidden_bias[2][0], weights.at[1], active, slope, dnormed)
    upper_back(dnormed, gain, shift, cot[...], keep, result, dout, sums)
    shard_backward(dout, narrow_own, slopes_in[0], widen_own, dhid.at[0], hsums.at[0], dnormed)
    shard_backward(dout, weights_one.at[1], slopes_in[1], weights_one.at[0], dhid.at[1], hsums.at[1], dnormed)
    shard_backward(dout, weights.at[1], slope, weights.at[0], dhid.at[2], hsums.at[2], dnormed)
    shard_backward(dout, weights_three.at[1], slopes_in[2], weights_three.at[0], dhid.at[3], hsums.at[3], dnormed)

    lower_back(first, dnormed, gain, dense, *lower)
    dfirst_lt = lower_l[0]
    lower_back(first_l, dnormed_l, gain_l, dense_l, dfirst_l, *lower_l[1:])
    dfirst_lt[...] = jnp.transpose(dfirst_l[...])


def lower_back(first, dnormed, gain, dense, dfirst, dbranch, dcontext, sums):
    width = first.shape[1]
    wide = dcontext.shape[1]
    normal, scale = normalised(first[...])
    back = norm_back(dnormed[...], normal, scale, gain[0:1, :])
    sums[0:1, :] = column_sum(dnormed[...] * normal)
    sums[1:2, :] = column_sum(dnormed[...])
    dfirst[...] = back
    dbranch[...] = back.astype(BF)
    sums[2:3, :] = column_sum(dbranch[...])
    sums[3:4, :] = jnp.zeros_like(sums[3:4, :])
    dc = nt(dbranch[...], dense[...]).astype(BF)
    dcontext[:, :width] = dc
    if wide > width:
        dcontext[:, width:] = jnp.zeros((dc.shape[0], wide - width), BF)


EXTRA = 16


def ffn_send_kernel(info, a0, a1, a2, a3, dout, low, dhid, pack, send_a, send_b):
    half = pl.ds(pl.multiple_of(info[HALF + 1], LANES), 384)
    more = pl.ds(pl.multiple_of(info[HALF + 1] // 6, 64), 64)
    for s, active in enumerate((a0, a1, a2, a3)):
        send_a[s, :384] = tn(active[:, half], dout[...]).astype(BF)
        send_a[s, 384:] = pack[s, more, :]
        send_b[s] = tn(low[:, half], dhid[s]).astype(BF)


def ffn_keep_kernel(
    info, a0, a1, a2, a3, dout, low, dhid, recv_a, recv_b, pack, next_a, next_b, keep_a, keep_b, sum_a, sum_b,
):
    half = pl.ds(pl.multiple_of(info[HALF], LANES), 384)
    more = pl.ds(pl.multiple_of(info[HALF] // 6, 64), 64)
    for s, active in enumerate((a0, a1, a2, a3)):
        sum_a[:384] = (tn(active[:, half], dout[...]) + recv_a[s, :384].astype(F32)).astype(BF)
        sum_a[384:] = (pack[s, more, :].astype(F32) + recv_a[s, 384:].astype(F32)).astype(BF)
        sum_b[...] = (tn(low[:, half], dhid[s]) + recv_b[s].astype(F32)).astype(BF)
        for rel in range(4):
            rows = pl.ds(pl.multiple_of(info[PIECE + rel], 32), 96)
            rest = pl.ds(pl.multiple_of(384 + info[PIECE + rel] // 6, EXTRA), EXTRA)
            to = (next_a if rel % 2 else keep_a).at[rel // 2, s]
            to[:96] = sum_a[rows, :]
            to[96:] = sum_a[rest, :]
            (next_b if rel // 2 else keep_b)[rel % 2, s] = sum_b[rows, :]


def ffn_spread_kernel(info, keep_a, recv_a, keep_b, recv_b, out):
    rows = keep_a.shape[1]
    for s in range(4):
        group = lax.rem(info[GROUP] + s, 4)
        out[group, :rows] = (keep_a[s].astype(F32) + recv_a[s].astype(F32)).astype(BF)
        out[group, rows:] = (keep_b[s].astype(F32) + recv_b[s].astype(F32)).astype(BF)


def add(a, b, *more):
    total = a.astype(F32) + b.astype(F32)
    for value in more:
        total = total + value.astype(F32)
    return total.astype(BF)


def add_split(keep, recv, *zeros):
    return add(keep[1], recv[1], *zeros), add(keep[0], recv[0], *zeros)


def zero_of(value):
    return value[(0,) * value.ndim].astype(F32) * 0.0


def copied_spread_kernel(info, keep_a, recv_a, keep_b, recv_b, *outs):
    for k, out in enumerate(outs):
        keep, recv = (keep_a, recv_a) if k < 2 else (keep_b, recv_b)
        out[...] = (keep[k % 2].astype(F32) + recv[k % 2].astype(F32)).astype(out.dtype)


def ffn_final_kernel(plan, info, *refs):
    pieces, (narrow, widen, narrow_l, widen_l, pack) = refs[: len(plan)], refs[len(plan) :]
    for piece, (rel, low, high) in zip(pieces, plan):
        rows = piece_rows(info, rel)
        if low == 0:
            narrow[rows, :] = piece[:96].astype(F32)
            rest = pl.ds(pl.multiple_of((info[HALF + rel // 4] + info[PIECE + rel % 4]) // 6, EXTRA), EXTRA)
            pack[rest, :] = piece[96:112].astype(F32)
        if high > 112:
            widen[rows, :] = piece[112 - low :].astype(F32)
    width_l = narrow_l.shape[0]
    narrow_l[:128] = pack[:, :width_l]
    narrow_l[128:] = pack[:64, 512 : 512 + width_l]
    widen_l[:128] = pack[:, 256 : 256 + width_l]
    widen_l[128:] = pack[64:, 512 : 512 + width_l]


def copied_final_kernel(plan, info, *refs):
    pieces, refs = refs[: len(plan)], refs[len(plan) :]
    project, dense, project_l, dense_l = refs[:4]
    vectors, vectors_l, (extra,) = refs[4:8], refs[8:12], refs[12:]
    width = dense.shape[1]
    for piece, (rel, low, high) in zip(pieces, plan):
        rows = piece_rows(info, rel)
        for part in range(low, high):
            block = lax.rem(info[GROUP] + part, 4)
            at = pl.ds(pl.multiple_of(128 * block + (info[HALF + rel // 4] + info[PIECE + rel % 4]) // 6, EXTRA), EXTRA)
            extra[at, :] = piece[part - low, 96:].astype(F32)

            @pl.when(block < 3)
            def _():
                project[rows, pl.ds(pl.multiple_of(block * width, LANES), width)] = piece[part - low, :96].astype(F32)

            @pl.when(block == 3)
            def _():
                dense[rows, :] = piece[part - low, :96].astype(F32)

    width_l = dense_l.shape[0]
    for i in range(3):
        project_l[:, i * width_l : (i + 1) * width_l] = extra[:width_l, i * 256 : i * 256 + width_l]
    dense_l[...] = extra[width_l : 2 * width_l, :width_l]
    for at, (biases, gains, shifts, hidden), lanes in ((2 * width_l, vectors, width), (2 * width_l + 16, vectors_l, width_l)):
        rows = extra[at : at + 16, :lanes]
        for i, row in enumerate((8, 9, 6, 2)):
            biases[i : i + 1, :] = rows[row : row + 1]
        gains[0:1, :] = rows[4:5]
        gains[1:2, :] = rows[0:1]
        shifts[0:1, :] = rows[5:6]
        shifts[1:2, :] = rows[1:2]
        hidden[...] = extra[pl.ds(at + 12 + info[GROUP], 1), :lanes]


def attend_back_kernel(
    info, qt, kt, vt, ql, kl, vl, dct, dcl, lse,
    dq, dk, dv, dq_l, dk_l, dv_l,
    k_acc, v_acc, kl_acc, vl_acc, ql_acc,
):
    own_rows = qt.shape[0]
    window = kt.shape[0]
    block = window // 2
    pad = (dk.shape[0] - window) // 2
    for acc in (k_acc, v_acc, kl_acc, vl_acc, ql_acc):
        acc[...] = jnp.zeros_like(acc)
    for out in (dk, dv, dk_l, dv_l):
        edge = jnp.zeros((pad, out.shape[1]), BF)
        out[:pad, :] = edge
        out[pad + window :, :] = edge
    lane = lax.broadcasted_iota(jnp.int32, (1, LANES), 1)

    def one_pair(pair, carry):
        text_lanes = lanes_of(pair * LANES)
        group_lanes = lanes_of((pair // 4) * LANES)
        scaled = head_masks(pair, 0.125, 0.25)
        plain = head_masks(pair, 1.0, 1.0)
        for j in range(own_rows // LANES):
            rows = pl.ds(j * LANES, LANES)
            keys_at = pl.ds(pl.multiple_of(info[LOCAL + j] * block, block), block)
            stacked = stack_heads(qt[rows, text_lanes], ql[rows, group_lanes], scaled)
            keys = jnp.concatenate([kt[keys_at, text_lanes], kl[keys_at, group_lanes]], axis=1)
            values = jnp.concatenate([vt[keys_at, text_lanes], vl[keys_at, group_lanes]], axis=1)
            dcs = stack_heads(dct[rows, text_lanes], dcl[rows, group_lanes], plain)
            logs = lse[rows, :]
            log_total = jnp.concatenate(
                [
                    jnp.sum(jnp.where(lane == 2 * pair, logs, 0.0), axis=1, keepdims=True),
                    jnp.sum(jnp.where(lane == 2 * pair + 1, logs, 0.0), axis=1, keepdims=True),
                ],
                axis=0,
            )
            probs = jnp.exp(pair_scores(stacked, keys, info[LIMIT + j]) - log_total)
            dprobs = nt(dcs, values)
            inner = jnp.sum(probs * dprobs, axis=1, keepdims=True)
            dscores = (probs * (dprobs - inner)).astype(BF)
            text, layout = unstack_heads(nn(dscores, keys), scaled)
            dq[rows, text_lanes] = text.astype(BF)
            ql_acc[rows, group_lanes] += layout
            both = tn(dscores, stacked)
            k_acc[keys_at, text_lanes] += both[:, :LANES]
            kl_acc[keys_at, group_lanes] += both[:, LANES:]
            both = tn(probs.astype(BF), dcs)
            v_acc[keys_at, text_lanes] += both[:, :LANES]
            vl_acc[keys_at, group_lanes] += both[:, LANES:]
        return carry

    lax.fori_loop(0, HEADS // 2, one_pair, 0)
    middle = pl.ds(pad, window)
    dk[middle, :] = k_acc[...].astype(BF)
    dv[middle, :] = v_acc[...].astype(BF)
    dk_l[middle, :] = kl_acc[...].astype(BF)
    dv_l[middle, :] = vl_acc[...].astype(BF)
    dq_l[...] = ql_acc[...].astype(BF)


def key_value_grad(info, at, rows_out, wt, wl, dk, dv, dk_l, dv_l):
    width, wide = dk.shape[1], dk_l.shape[1]
    rows = pl.ds(pl.multiple_of(info[SHIFT] + at, LANES), rows_out)
    text = nt(dk[rows, :], wt[:, width : 2 * width]) + nt(dv[rows, :], wt[:, 2 * width :])
    layout = nt(wl[:, wide : 2 * wide], dk_l[rows, :]) + nt(wl[:, 2 * wide :], dv_l[rows, :])
    return text, layout


def store_packed(out, text, layout):
    own_rows = text.shape[0]
    half = layout.shape[0] // 2
    out[:own_rows, :] = text.astype(BF)
    out[own_rows:, :own_rows] = layout[:half].astype(BF)
    out[own_rows:, own_rows:] = layout[half:].astype(BF)


def sides_kernel(info, wt, wl, dk, dv, dk_l, dv_l, left, right):
    own_rows = left.shape[0] * 4 // 5
    for side, shift in ((left, 0), (right, 2 * own_rows)):
        store_packed(side, *key_value_grad(info, shift, own_rows, wt, wl, dk, dv, dk_l, dv_l))


def own_kernel(info, wt, wl, dq, dk, dv, dq_l, dk_l, dv_l, dfirst_t, dfirst_lt, left, right, out):
    own_rows, width = dq.shape
    wide = dq_l.shape[1]
    half = dfirst_lt.shape[0] // 2
    text, layout = key_value_grad(info, own_rows, own_rows, wt, wl, dk, dv, dk_l, dv_l)
    text = dfirst_t[...] + text + nt(dq[...], wt[:, :width])
    layout = dfirst_lt[...] + layout + nt(wl[:, :wide], dq_l[...])
    got = left[...].astype(F32) + right[...].astype(F32)
    text = text + got[:own_rows]
    layout = layout + jnp.concatenate([got[own_rows:, :own_rows], got[own_rows:, own_rows:]], axis=0)
    store_packed(out, text, layout)


def input_final_kernel(info, own, l1, l2, l3, r1, r2, r3, text, layout):
    own_rows, half = own.shape[0] * 4 // 5, layout.shape[0] // 2
    for distance, rows in ((0, own), (-1, l1), (-2, l2), (-3, l3), (1, r1), (2, r2), (3, r3)):
        group = info[GROUP] + distance

        @pl.when((group >= 0) & (group < 4))
        def _():
            at = pl.ds(pl.multiple_of(group * own_rows, LANES), own_rows)
            text[at, :] = rows[:own_rows, :].astype(F32)
            layout[:half, at] = rows[own_rows:, :own_rows].astype(F32)
            layout[half:, at] = rows[own_rows:, own_rows:].astype(F32)


def extras(
    info, xlt, dq, dv, dq_l, dk_l, dv_l, cl, db_l, sums_a, sums_b, hsums, sums_al, sums_bl, hsums_l, extra, small,
):
    own_rows = dq.shape[0]
    wide = dq_l.shape[1]
    width_l = xlt.shape[0]
    window = dk_l.shape[0] - 2 * own_rows
    own = pl.ds(pl.multiple_of(info[OWN], LANES), own_rows)
    seen = pl.ds(pl.multiple_of(info[WINDOW], LANES), window)
    middle = pl.ds(own_rows, window)
    extra[width_l:, :] = jnp.zeros((extra.shape[0] - width_l, extra.shape[1]), BF)
    extra[:width_l, :wide] = nn(xlt[:, own], dq_l[...]).astype(BF)
    extra[:width_l, wide : 2 * wide] = nn(xlt[:, seen], dk_l[middle, :]).astype(BF)
    extra[:width_l, 2 * wide : 3 * wide] = nn(xlt[:, seen], dv_l[middle, :]).astype(BF)
    extra[width_l : 2 * width_l, :width_l] = tn(cl[...], db_l[...]).astype(BF)
    small[...] = jnp.zeros_like(small)
    small[0:4, :] = sums_a[...]
    small[4:8, :] = sums_b[...]
    small[8:9, :] = column_sum(dq[...])
    small[9:10, :] = column_sum(dv[middle, :])
    small[16:20, :width_l] = sums_al[...]
    small[20:24, :width_l] = sums_bl[...]
    small[24:25, :wide] = column_sum(dq_l[...])
    small[25:26, :wide] = column_sum(dv_l[middle, :])
    for s in range(4):
        group = lax.rem(info[GROUP] + s, 4)
        small[pl.ds(12 + group, 1), :] = hsums[s]
        small[pl.ds(28 + group, 1), :width_l] = hsums_l[s]
    extra[2 * width_l : 2 * width_l + 32, :] = small[...].astype(BF)


def copied_grads(info, xt, dq, dk, dv, ct, db, half, store):
    own_rows = dq.shape[0]
    window = dk.shape[0] - 2 * own_rows
    own = pl.ds(pl.multiple_of(info[OWN], LANES), own_rows)
    seen = pl.ds(pl.multiple_of(info[WINDOW], LANES), window)
    middle = pl.ds(own_rows, window)
    for block in range(4):
        if block == 0:
            grad = tn(xt[own, half], dq[...])
        elif block == 1:
            grad = tn(xt[seen, half], dk[middle, :])
        elif block == 2:
            grad = tn(xt[seen, half], dv[middle, :])
        else:
            grad = tn(ct[:, half], db[...])
        store(block, info[SLOT + block], grad)


def copied_send_kernel(
    info, xt, dq, dk, dv, ct, db, xlt, dq_l, dk_l, dv_l, cl, db_l, sums_a, sums_b, hsums, sums_al, sums_bl, hsums_l,
    send, extra, small,
):
    half = pl.ds(pl.multiple_of(info[HALF + 1], LANES), 384)
    extras(info, xlt, dq, dv, dq_l, dk_l, dv_l, cl, db_l, sums_a, sums_b, hsums, sums_al, sums_bl, hsums_l, extra, small)

    def store(block, slot, grad):
        send[slot, :384] = grad.astype(BF)
        send[slot, 384:] = extra[pl.ds(pl.multiple_of(128 * block + info[HALF + 1] // 6, 64), 64), :]

    copied_grads(info, xt, dq, dk, dv, ct, db, half, store)


def copied_keep_kernel(info, xt, dq, dk, dv, ct, db, extra, recv, next_a, keep_a, next_b, keep_b, total):
    half = pl.ds(pl.multiple_of(info[HALF], LANES), 384)

    def store(block, slot, grad):
        more = pl.ds(pl.multiple_of(128 * block + info[HALF] // 6, 64), 64)
        total[slot, :384] = (grad + recv[slot, :384].astype(F32)).astype(BF)
        total[slot, 384:] = (extra[more, :].astype(F32) + recv[slot, 384:].astype(F32)).astype(BF)

    copied_grads(info, xt, dq, dk, dv, ct, db, half, store)
    for slot in range(4):
        for rel in range(4):
            x_part, y_part = rel % 2, rel // 2
            first, second = (x_part, y_part) if slot < 2 else (y_part, x_part)
            out = ((keep_a, next_a), (keep_b, next_b))[slot // 2][first].at[second, slot % 2]
            out[:96] = total[slot, pl.ds(pl.multiple_of(info[PIECE + rel], 32), 96), :]
            out[96:] = total[slot, pl.ds(pl.multiple_of(384 + info[PIECE + rel] // 6, EXTRA), EXTRA), :]


SM = pl.BlockSpec(memory_space=pltpu.SMEM)
VM = pl.BlockSpec(memory_space=pltpu.VMEM)
HB = pl.BlockSpec(memory_space=pl.ANY)


class InHbm:
    def __init__(self, dims, dtype=BF):
        self.shape, self.dtype = dims, dtype


def vmem_of(outs, scratch):
    held = list(outs) + [v for v in scratch if str(v.memory_space) == "vmem"]
    return int(1.1 * sum(math.prod(v.shape) * jnp.dtype(v.dtype).itemsize for v in held)) + (MARGIN << 20)


def call(name, kernel, operands, outs, scratch=(), after=(), in_hbm=0, final=False):
    operands = tuple(operands)
    outs = tuple(outs) + (shape((8, LANES), F32),)
    specs = [HB] * len(after) + [SM] + [VM] * (len(operands) - 1 - in_hbm) + [pl.BlockSpec(memory_space=pltpu.HBM)] * in_hbm
    limit = vmem_of(outs if final else (), scratch)
    operands = tuple(after) + operands
    at = len(operands) + len(outs) - 1

    def with_token(*refs):
        kernel(*refs[len(after) : at], *refs[at + 1 :])
        refs[at][...] = jnp.zeros_like(refs[at])

    return pl.pallas_call(
        with_token,
        out_shape=tuple(shape(o.shape, o.dtype) for o in outs),
        in_specs=specs,
        out_specs=[HB if isinstance(o, InHbm) else VM for o in outs],
        scratch_shapes=list(scratch),
        cost_estimate=pl.CostEstimate(flops=int(MICROSECONDS[name] * PER_MICROSECOND), bytes_accessed=0, transcendentals=0),
        compiler_params=pltpu.CompilerParams(vmem_limit_bytes=limit),
        name=name,
    )(*operands)


def shape(dims, dtype=BF):
    return jax.ShapeDtypeStruct(dims, dtype)


def flip(planes, bit):
    return [(i, i ^ bit) for i in range(planes)]


def gate(values, *tokens):
    outs = pl.pallas_call(
        lambda *refs: None,
        out_shape=tuple(shape(v.shape, v.dtype) for v in values),
        in_specs=[HB] * (len(values) + len(tokens)),
        out_specs=[HB] * len(values),
        input_output_aliases={i: i for i in range(len(values))},
        cost_estimate=pl.CostEstimate(flops=0, bytes_accessed=0, transcendentals=0),
        compiler_params=pltpu.CompilerParams(vmem_limit_bytes=1 << 20),
        name="gate",
    )(*values, *tokens)
    return list(outs)


def around(planes):
    return lambda v, bit: lax.ppermute(v, "dp", flip(planes, bit))


def forward(piece, by_x, by_y, planes, split, mid=None, zero=None):
    across, parts = around(planes), piece.shape[0]
    if split == "x":
        return [(across(by_x, Y), 3, 0, parts)]
    if split == "y":
        return [(across(by_y, X), 3, 0, parts)]
    mid = mid or parts // 2
    low, high = by_x[:mid], by_y[mid:]
    if zero is not None:
        low, high = add(low, zero), add(high, zero)
    return [(across(low, Y), 3, 0, mid), (across(high, X), 3, mid, parts)]


def to_core(held, planes):
    across = around(planes)
    held = held + [(across(v, CORE), rel + 4, low, high) for v, rel, low, high in held]
    return [h[0] for h in held], tuple(h[1:] for h in held)


def spread(piece, planes, mid=None, zero=None):
    across, parts = around(planes), piece.shape[0]
    by_x, by_y = across(piece, X), across(piece, Y)
    held = [(piece, 0, 0, parts), (by_x, 1, 0, parts), (by_y, 2, 0, parts)]
    return to_core(held + forward(piece, by_x, by_y, planes, "half", mid, zero), planes)


def per_device(
    text_input, layout_input, block_starts, intersection_flags, text_cotangent, layout_cotangent,
    text_project, text_biases, text_dense, text_gains, text_shifts, text_widen, text_hidden_bias, text_narrow,
    layout_project, layout_biases, layout_dense, layout_gains, layout_shifts, layout_widen, layout_hidden_bias,
    layout_narrow,
):
    blocks, length = intersection_flags.shape
    total = blocks * length
    groups = lax.axis_size("tensor")
    planes = lax.axis_size("dp")
    own = total // groups
    tiles = own // LANES
    width = text_input.shape[1]
    width_l = layout_input.shape[1]
    wide = 2 * LANES
    window = 2 * length
    padded = window + 2 * own
    hid = text_narrow.shape[0]
    hid_l = layout_narrow.shape[0]
    piece = width // PIECES
    t = lax.axis_index("tensor").astype(jnp.int32)
    me = lax.axis_index("dp").astype(jnp.int32)
    core, x_bit, y_bit = me & 1, (me >> 1) & 1, (me >> 2) & 1

    def row_of(rc, rx, ry):
        return 4 * piece * (core ^ rc) + piece * ((x_bit ^ rx) + 2 * (y_bit ^ ry))

    flagged = jnp.sum(intersection_flags, axis=1, dtype=jnp.int32)
    base = jnp.minimum((t * own) // length, blocks - 2)
    tile_rows = t * own + LANES * jnp.arange(tiles, dtype=jnp.int32)
    tile_block = tile_rows // length
    pick = tile_block[:, None] == jnp.arange(blocks, dtype=jnp.int32)[None, :]
    limit = DOC - jnp.sum(jnp.where(pick, block_starts[None, :], 0), axis=1)
    flags_of = jnp.sum(jnp.where(pick, flagged[None, :], 0), axis=1)
    info = jnp.concatenate(
        [
            jnp.stack([t * own, base * length, t * own - base * length]),
            tile_block - base,
            limit,
            flags_of,
            tile_rows - tile_block * length,
            jnp.stack(
                [t, 4 * piece * core, 4 * piece * (1 - core)]
                + [row_of(0, rx, ry) - 4 * piece * core for ry in (0, 1) for rx in (0, 1)]
                + [(b - t) % groups for b in range(4)]
            ),
        ]
    ).astype(jnp.int32)

    shift_from = lambda k: [(i, (i - k) % groups) for i in range(groups)]
    shift_to = lambda k: [(i, (i + k) % groups) for i in range(groups)]
    bias = jnp.concatenate([text_hidden_bias, layout_hidden_bias, jnp.zeros((8 * LANES - hid - hid_l,), F32)])
    across = around(planes)
    row = row_of(0, 0, 0)
    mine, packed_up = call(
        "pack", pack_kernel,
        (jnp.zeros((1,), jnp.int32),
         jnp.concatenate([lax.dynamic_slice_in_dim(v, row, piece, 0) for v in (text_widen, text_narrow)], axis=0),
         jnp.concatenate([lax.dynamic_slice_in_dim(v, row // 4, piece // 4, 0) for v in (layout_widen, layout_narrow)], axis=0),
         bias.reshape(8, LANES)),
        (shape((2 * piece + 32, width)),),
    )
    from_group = lambda v, k: lax.ppermute(v, "tensor", shift_from(k))
    come = {k: from_group(mine, k) for k in (1, 3)}

    xlt = layout_input.T
    qt, kt, vt, ql, kl, vl, xl_own, wl, projected = call(
        "project", project_kernel,
        (info, text_input, xlt, text_project, layout_project, text_biases, layout_biases),
        (shape((own, width)), shape((window, width)), shape((window, width)),
         shape((own, wide)), shape((window, wide)), shape((window, wide)),
         shape((own, width_l)), shape((width_l, 3 * wide))),
        after=(packed_up,),
    )
    mine_again, come[1], come[3] = gate((mine, come[1], come[3]), projected)
    come[2] = from_group(mine_again, 2)
    by_x, by_y = {}, {}
    for k in (1, 3):
        by_x[k], by_y[k] = across(come[k], X), across(come[k], Y)
    ct, cl, lse, attended = call(
        "attend", attend_kernel,
        (info, qt, kt, vt, ql, kl, vl),
        (shape((own, width)), shape((own, width_l)), shape((own, LANES), F32)),
        scratch=(pltpu.VMEM((own, wide), F32),),
    )
    by_x[1], by_y[1], by_x[3], by_y[3], *came = gate(
        (by_x[1], by_y[1], by_x[3], by_y[3], come[1], come[2], come[3]), attended
    )
    come = dict(zip((1, 2, 3), came))
    forwarded = {k: forward(come[k], by_x[k], by_y[k], planes, {1: "x", 3: "y"}[k]) for k in (1, 3)}
    first_t, first_l, low_t, low_l, normed_l, active0, slope0, total_t, first_done = call(
        "first_norm", first_norm_kernel,
        (info, text_input, xl_own, ct, cl, text_dense, layout_dense, text_biases, layout_biases,
         text_gains, text_shifts, layout_gains, layout_shifts, text_widen, mine, text_narrow),
        (shape((own, width), F32), shape((own, width_l), F32), shape((own, width)), shape((own, width_l)),
         shape((own, width_l), F32), shape((own, hid)), shape((own, hid), F32), shape((own, width), F32)),
    )
    both = gate((forwarded[1][0][0], forwarded[3][0][0]), first_done)
    shards = {}
    for k, array in zip((1, 3), both):
        parts = come[k].shape[0]
        held = [(come[k], 0, 0, parts), (by_x[k], 1, 0, parts), (by_y[k], 2, 0, parts), (array, 3, 0, parts)]
        shards[k] = to_core(held, planes)
    by_x[2], by_y[2] = across(come[2], X), across(come[2], Y)
    last = forward(come[2], by_x[2], by_y[2], planes, "half", 96)
    actives, slopes, shard_weights, layouts, shard_done = {0: active0}, {0: slope0}, {}, {}, {}
    for k in (1, 3):
        arrays, plan = shards[k]
        actives[k], slopes[k], total_t, shard_weights[k], layouts[k], shard_done[k] = call(
            "shard", functools.partial(shard_kernel, plan),
            (info, low_t, total_t, *arrays),
            (shape((own, hid)), shape((own, hid), F32), shape((own, width), F32), shape((2, width, hid)),
             shape((width_l, 2 * wide))),
            scratch=(pltpu.VMEM((width_l, 2 * wide), F32),),
            after=tuple(f[0] for f in last) if k == 3 else (),
        )
    parts = come[2].shape[0]
    shards[2] = to_core([(come[2], 0, 0, parts), (by_x[2], 1, 0, parts), (by_y[2], 2, 0, parts)] + last, planes)
    arrays, plan = shards[2]
    rows_a = piece + EXTRA
    outs = call(
        "turn", functools.partial(turn_kernel, plan),
        (info, low_t, total_t, text_gains, text_shifts, text_cotangent, text_widen, text_narrow,
         slopes[0], slopes[1], slopes[3], actives[0], actives[1], actives[3],
         low_l, normed_l, layout_gains, layout_shifts, layout_cotangent.T, first_t, first_l, text_dense, layout_dense,
         layout_widen, layout_narrow, layouts[1], layouts[3],
         mine, come[1], come[3], shard_weights[1], shard_weights[3], *arrays),
        (shape((own, width)), shape((own, width)), shape((groups, own, hid)),
         shape((4, width), F32), shape((groups, 1, hid), F32), shape((own, hid)),
         shape((width_l, own)), shape((4, width_l), F32), shape((groups, 1, hid_l), F32), shape((groups, 128, width)),
         shape((own, width), F32), shape((own, width)), shape((own, width)), shape((4, width), F32),
         shape((width_l, own), F32), shape((own, width_l)), shape((own, wide)), shape((4, width_l), F32)),
        scratch=(pltpu.VMEM((2, width, hid), BF), pltpu.VMEM((own, hid), F32), pltpu.VMEM((own, width), F32),
                 pltpu.VMEM((groups, own, hid_l), F32), pltpu.VMEM((groups, own, hid_l), BF),
                 pltpu.VMEM((groups, own, hid_l), BF), pltpu.VMEM((own, width_l), BF), pltpu.VMEM((own, width_l), BF),
                 pltpu.VMEM((own, width_l), F32), pltpu.VMEM((own, width_l), F32), pltpu.VMEM((width_l, 2 * wide), F32)),
    )
    result_t, dout_t, dhid_t, sums_t, hsums_t, actives[2] = outs[:6]
    result_lt, sums_l, hsums_l, pack = outs[6:10]
    dfirst_t, db_t, dc_t, low_sums_t, dfirst_lt, db_l, dc_l, low_sums_l, turned = outs[10:]

    def across_planes(value):
        bit = PIECES
        while bit < planes:
            value = add(value, across(value, bit))
            bit *= 2
        return value

    ffn_in = (*(actives[k] for k in range(4)), dout_t, low_t, dhid_t)
    send_a, send_b, ffn_sent = call(
        "ffn_send", ffn_send_kernel, (info, *ffn_in, pack),
        (shape((groups, 4 * rows_a, width)), shape((groups, 4 * piece, width))),
    )
    recv_a, recv_b = across(send_a, CORE), across(send_b, CORE)
    dq, dk, dv, dq_l, dk_l, dv_l, attended_back = call(
        "attend_back", attend_back_kernel,
        (info, qt, kt, vt, ql, kl, vl, dc_t, dc_l, lse),
        (shape((own, width)), shape((padded, width)), shape((padded, width)),
         shape((own, wide)), shape((padded, wide)), shape((padded, wide))),
        scratch=(pltpu.VMEM((window, width), F32), pltpu.VMEM((window, width), F32),
                 pltpu.VMEM((window, wide), F32), pltpu.VMEM((window, wide), F32), pltpu.VMEM((own, wide), F32)),
        after=(ffn_sent,),
    )
    next_a, next_b, keep_a, keep_b, kept = call(
        "ffn_keep", ffn_keep_kernel, (info, *ffn_in, recv_a, recv_b, pack),
        (shape((2, groups, rows_a, width)), shape((2, groups, piece, width))) * 2,
        scratch=(pltpu.VMEM((4 * rows_a, width), BF), pltpu.VMEM((4 * piece, width), BF)), after=(attended_back,),
    )
    recv_a, recv_b = across(next_a, X), across(next_b, Y)
    copied_in = (text_input, dq, dk, dv, ct, db_t)
    send, extra, sent = call(
        "copied_send", copied_send_kernel,
        (info,) + copied_in + (xlt, dq_l, dk_l, dv_l, cl, db_l, sums_t, low_sums_t, hsums_t, sums_l, low_sums_l, hsums_l),
        (shape((groups, 4 * rows_a, width)), shape((4 * 128, width))),
        scratch=(pltpu.VMEM((32, width), F32),), after=(kept,),
    )
    packed = shape((own + own // 4, width))
    left, right, sided = call(
        "sides", sides_kernel, (info, text_project, wl, dk, dv, dk_l, dv_l), (packed, packed), after=(sent,)
    )
    from_right = lax.ppermute(left, "tensor", [(i + 1, i) for i in range(groups - 1)])
    from_left = lax.ppermute(right, "tensor", [(i, i + 1) for i in range(groups - 1)])

    recv = across(send, CORE)
    copied_next_a, copied_keep_a, copied_next_b, copied_keep_b, copied_kept = call(
        "copied_keep", copied_keep_kernel, (info,) + copied_in + (extra, recv),
        (shape((2, 2, rows_a, width)),) * 4,
        scratch=(pltpu.VMEM((groups, 4 * rows_a, width), BF),), after=(sided,),
    )
    copied_recv_a, copied_recv_b = across(copied_next_a, X), across(copied_next_b, Y)
    own_sum, owned = call(
        "own", own_kernel,
        (info, text_project, wl, dq, dk, dv, dq_l, dk_l, dv_l, dfirst_t, dfirst_lt, from_right, from_left),
        (packed,), after=(copied_kept, recv_a, recv_b),
    )
    step_right = lambda v, far: lax.ppermute(v, "tensor", [(i, i + 1) for i in range(far, groups - 1)])
    step_left = lambda v, far: lax.ppermute(v, "tensor", [(i, i - 1) for i in range(groups - 1 - far, 0, -1)])
    lefts, rights = [step_right(own_sum, 0)], [step_left(own_sum, 0)]
    for far in (1, 2):
        lefts.append(step_right(lefts[-1], far))
        rights.append(step_left(rights[-1], far))
    to_group = lambda v, k: lax.ppermute(v, "tensor", shift_to(k))
    copied_next_a, copied_keep_a = add_split(copied_keep_a, copied_recv_a)
    copied_next_b, copied_keep_b = add_split(copied_keep_b, copied_recv_b)
    copied_recv_a, copied_recv_b = across(copied_next_a, Y), across(copied_next_b, X)
    *parts, copied_spreaded = call(
        "copied_spread", copied_spread_kernel, (info, copied_keep_a, copied_recv_a, copied_keep_b, copied_recv_b),
        (shape((rows_a, width)),) * 4,
        after=(lefts[0], rights[0]),
    )
    parts = [parts[0]] + [to_group(parts[k], k) for k in (1, 2, 3)]
    summed = across_planes(add(*parts, zero_of(lefts[1]), zero_of(rights[1])))
    next_a, keep_a = add_split(keep_a, recv_a, zero_of(summed))
    next_b, keep_b = add_split(keep_b, recv_b, zero_of(summed))
    recv_a, recv_b = across(next_a, Y), across(next_b, X)
    every = [summed] + [from_group(summed, k) for k in (1, 2, 3)]
    ffn_parts, _ = call(
        "ffn_spread", ffn_spread_kernel, (info, keep_a, recv_a, keep_b, recv_b),
        (shape((groups, rows_a + piece, width)),), after=tuple(every[1:]),
    )
    ffn_grads = lax.psum_scatter(ffn_parts, "tensor", scatter_dimension=0, tiled=False)
    every = jnp.stack(every)
    arrays, plan = spread(every, planes)
    vectors = lambda w, h: (shape((4, w), F32), shape((2, w), F32), shape((2, w), F32), shape((1, h), F32))
    outs = call(
        "copied_final", functools.partial(copied_final_kernel, plan), (info, *arrays),
        (shape((width, 3 * width), F32), shape((width, width), F32),
         shape((width_l, 3 * width_l), F32), shape((width_l, width_l), F32)) + vectors(width, hid) + vectors(width_l, hid_l),
        scratch=(pltpu.VMEM((4 * 128, width), F32),), final=True,
    )
    text_grad, layout_grad_t, given = call(
        "input_final", input_final_kernel, (info, own_sum, *lefts, *rights),
        (shape((total, width), F32), shape((width_l, total), F32)), after=(outs[-1],), final=True,
    )
    ffn_grads = add(across_planes(ffn_grads), zero_of(outs[-1]))
    ffn_arrays, ffn_plan = spread(ffn_grads, planes, rows_a, zero_of(given))
    g_narrow, g_widen, g_narrow_l, g_widen_l, _ = call(
        "ffn_final", functools.partial(ffn_final_kernel, ffn_plan), (info, *ffn_arrays),
        (shape((hid, width), F32), shape((width, hid), F32), shape((hid_l, width_l), F32), shape((width_l, hid_l), F32)),
        scratch=(pltpu.VMEM((128, width), F32),), final=True,
    )
    g_project, g_dense, g_project_l, g_dense_l = outs[:4]
    bias_t, gain_t, shift_t, hb_t, bias_l, gain_l, shift_l, hb_l = outs[4:12]
    return (
        result_t, result_lt.T, text_grad, layout_grad_t.T,
        g_project, bias_t, g_dense, gain_t, shift_t, g_widen, hb_t[0], g_narrow,
        g_project_l, bias_l, g_dense_l, gain_l, shift_l, g_widen_l, hb_l[0], g_narrow_l,
    )


def solution(mesh):
    rows = P(("dp", "tensor"), None)
    weights = (P(), P(), P(), P(), P(), P(None, "tensor"), P("tensor"), P("tensor", None))
    return jax.shard_map(
        per_device,
        mesh=mesh,
        in_specs=(P("dp", None), P("dp", None), P("dp"), P("dp", None), rows, rows) + weights + weights,
        out_specs=(rows, rows, P("dp", None), P("dp", None)) + weights + weights,
        check_vma=False,
    )
```

```python
import functools
import math

import jax
import jax.numpy as jnp
from jax import lax
from jax.experimental import pallas as pl
from jax.experimental.pallas import tpu as pltpu
from jax.sharding import PartitionSpec as P

HEADS = 12
DOC = 2048
LANES = 128
epsilon = 1e-05
masked_score = -1e30
F32 = jnp.float32
BF = jnp.bfloat16

OWN, WINDOW, SHIFT, LOCAL, LIMIT, FLAGGED, PLACE, GROUP, HALF, PIECE, SLOT = 0, 1, 2, 3, 6, 9, 12, 15, 16, 18, 22
PIECES = 8
MARGIN = 8
CORE, X, Y = 1, 2, 4
PER_MICROSECOND = 0.2e9
MICROSECONDS = {
    "pack": 1, "project": 5, "attend": 9, "first_norm": 3, "shard": 3, "turn": 12, "ffn_send": 4, "ffn_keep": 4, "ffn_spread": 1,
    "attend_back": 15, "copied_send": 4, "sides": 3, "copied_keep": 3, "own": 3, "input_final": 4,
    "ffn_final": 3, "copied_spread": 1, "copied_final": 6,
}


def nn(a, b):
    return lax.dot_general(a, b, (((1,), (0,)), ((), ())), preferred_element_type=F32)


def nt(a, b):
    return lax.dot_general(a, b, (((1,), (1,)), ((), ())), preferred_element_type=F32)


def tn(a, b):
    return lax.dot_general(a, b, (((0,), (0,)), ((), ())), preferred_element_type=F32)


def mean(values):
    return jnp.mean(values, axis=-1, keepdims=True)


def column_sum(values):
    return jnp.sum(values.astype(F32), axis=0, keepdims=True)


def normalised(values):
    centre = values - mean(values)
    scale = lax.rsqrt(mean(centre * centre) + epsilon)
    return centre * scale, scale


def norm_back(upstream, normal, scale, gain_row):
    u = upstream * gain_row
    return scale * (u - mean(u) - normal * mean(u * normal))


def lanes_of(start):
    return pl.ds(pl.multiple_of(start, LANES), LANES)


def head_masks(pair, text_scale, layout_scale):
    lane = lax.broadcasted_iota(jnp.int32, (1, LANES), 1)
    first = 32 * pair - LANES * (pair // 4)
    text_a = jnp.where(lane < 64, text_scale, 0.0)
    text_b = jnp.where(lane < 64, 0.0, text_scale)
    layout_a = jnp.where((lane >= first) & (lane < first + 16), layout_scale, 0.0)
    layout_b = jnp.where((lane >= first + 16) & (lane < first + 32), layout_scale, 0.0)
    return text_a, layout_a, text_b, layout_b


def stack_heads(text, layout, masks):
    text_a, layout_a, text_b, layout_b = (m.astype(BF) for m in masks)
    upper = jnp.concatenate([text * text_a, layout * layout_a], axis=1)
    lower = jnp.concatenate([text * text_b, layout * layout_b], axis=1)
    return jnp.concatenate([upper, lower], axis=0)


def unstack_heads(stacked, masks):
    text_a, layout_a, text_b, layout_b = masks
    upper, lower = stacked[:LANES], stacked[LANES:]
    text = upper[:, :LANES] * text_a + lower[:, :LANES] * text_b
    layout = upper[:, LANES:] * layout_a + lower[:, LANES:] * layout_b
    return text, layout


def pair_scores(stacked, keys, limit):
    scores = nt(stacked, keys)
    key = lax.broadcasted_iota(jnp.int32, (1, scores.shape[1]), 1)
    return jnp.where(key < limit, scores, masked_score)


def pack_kernel(place, weights, layout, bias, mine):
    mine[:192] = weights[...]
    width_l = layout.shape[1]
    high = bias[...].astype(BF).astype(F32)
    middle = (bias[...] - high).astype(BF).astype(F32)
    low = bias[...] - high - middle
    biases = jnp.concatenate([high, middle, low, jnp.zeros_like(low)], axis=0)
    mine[192:, :] = jnp.zeros((32, mine.shape[1]), BF)
    empty = jnp.zeros((8, width_l), F32)
    both = layout[...].astype(F32)
    mine[192:, :width_l] = jnp.concatenate([both[:24], empty], axis=0).astype(BF)
    mine[192:, 256 : 256 + width_l] = jnp.concatenate([both[24:], empty], axis=0).astype(BF)
    mine[192:, 512:640] = biases.astype(BF)


def biases_of(rest):
    split = rest[:, 512:640].astype(F32)
    rows = split[:8] + split[8:16] + split[16:24]
    text = jnp.concatenate([rows[i : i + 1] for i in range(6)], axis=1)
    layout = jnp.concatenate([rows[i : i + 1] for i in (6, 7)], axis=1)
    return text, layout


def identity(size):
    row = lax.broadcasted_iota(jnp.int32, (size, size), 0)
    column = lax.broadcasted_iota(jnp.int32, (size, size), 1)
    return jnp.where(row == column, 1.0, 0.0).astype(BF)


def project_kernel(info, xt, xlt, wt, wl, bt, bl, qt, kt, vt, ql, kl, vl, xl_own, wide_l):
    own_rows, width = qt.shape
    wide = ql.shape[1]
    width_l = wl.shape[0]
    own = pl.multiple_of(info[OWN], LANES)
    start = pl.multiple_of(info[WINDOW], LANES)
    rows = pl.ds(own, own_rows)
    for i in range(3):
        wide_l[:, i * wide : i * wide + width_l] = wl[:, i * width_l : (i + 1) * width_l]
        wide_l[:, i * wide + width_l : (i + 1) * wide] = jnp.zeros((width_l, wide - width_l), BF)
    edge = jnp.zeros((1, wide - width_l), F32)
    bias = [jnp.concatenate([bl[i : i + 1, :], edge], axis=1) for i in (0, 1)]
    qt[...] = (nn(xt[rows, :], wt[:, :width]) + bt[0:1, :]).astype(BF)
    ql[...] = (tn(xlt[:, rows], wide_l[:, :wide]) + bias[0]).astype(BF)
    xl_own[...] = tn(xlt[:, rows], identity(width_l)).astype(BF)

    def part(i, carry):
        rows = pl.ds(pl.multiple_of(i * 256, 256), 256)
        from_rows = pl.ds(pl.multiple_of(start + i * 256, 256), 256)
        x = xt[from_rows, :]
        kt[rows, :] = nn(x, wt[:, width : 2 * width]).astype(BF)
        vt[rows, :] = (nn(x, wt[:, 2 * width :]) + bt[1:2, :]).astype(BF)
        x = xlt[:, from_rows]
        kl[rows, :] = tn(x, wide_l[:, wide : 2 * wide]).astype(BF)
        vl[rows, :] = (tn(x, wide_l[:, 2 * wide :]) + bias[1]).astype(BF)
        return carry

    lax.fori_loop(0, kt.shape[0] // 256, part, 0)


def attend_kernel(info, qt, kt, vt, ql, kl, vl, ct, cl, lse, cl_acc):
    own_rows, layout_width = cl.shape
    block = kt.shape[0] // 2
    cl_acc[...] = jnp.zeros_like(cl_acc)
    lse[...] = jnp.zeros_like(lse)
    lane = lax.broadcasted_iota(jnp.int32, (1, LANES), 1)

    def one_pair(pair, carry):
        text_lanes = lanes_of(pair * LANES)
        group_lanes = lanes_of((pair // 4) * LANES)
        scaled = head_masks(pair, 0.125, 0.25)
        plain = head_masks(pair, 1.0, 1.0)
        for j in range(own_rows // LANES):
            rows = pl.ds(j * LANES, LANES)
            keys_at = pl.ds(pl.multiple_of(info[LOCAL + j] * block, block), block)
            stacked = stack_heads(qt[rows, text_lanes], ql[rows, group_lanes], scaled)
            keys = jnp.concatenate([kt[keys_at, text_lanes], kl[keys_at, group_lanes]], axis=1)
            values = jnp.concatenate([vt[keys_at, text_lanes], vl[keys_at, group_lanes]], axis=1)
            scores = pair_scores(stacked, keys, info[LIMIT + j])
            highest = jnp.max(scores, axis=-1, keepdims=True)
            exponent = jnp.exp(scores - highest)
            totals = jnp.sum(exponent, axis=-1, keepdims=True)
            probs = (exponent * (1.0 / totals)).astype(BF)
            text, layout = unstack_heads(nn(probs, values), plain)
            ct[rows, text_lanes] = text.astype(BF)
            cl_acc[rows, group_lanes] += layout
            log_total = highest + jnp.log(totals)
            lse[rows, :] = (
                lse[rows, :]
                + jnp.where(lane == 2 * pair, log_total[:LANES], 0.0)
                + jnp.where(lane == 2 * pair + 1, log_total[LANES:], 0.0)
            )
        return carry

    lax.fori_loop(0, HEADS // 2, one_pair, 0)
    cl[...] = cl_acc[:, :layout_width].astype(BF)


def gelu_both(hidden):
    below = 0.5 * (1.0 + lax.erf(hidden * math.sqrt(0.5)))
    density = jnp.exp(-0.5 * hidden * hidden) * (1.0 / math.sqrt(2.0 * math.pi))
    return hidden * below, below + hidden * density


def shard_forward(low, widen, bias, narrow, active, slope, total):
    hid = widen.shape[1]
    step = 256 if hid % 256 == 0 else hid
    for n in range(hid // step):
        cols = slice(n * step, (n + 1) * step)
        value, gradient = gelu_both(nn(low[...], widen[:, cols]) + bias[:, cols])
        active[:, cols] = value.astype(BF)
        slope[:, cols] = gradient
    total[...] += nn(active[...], narrow[...])


def shard_backward(dout, narrow, slope, widen, dhid, sums, total):
    hid = widen.shape[1]
    step = 256 if hid % 256 == 0 else hid
    for n in range(hid // step):
        cols = slice(n * step, (n + 1) * step)
        dhidden = (nt(dout[...], narrow[cols, :]) * slope[:, cols]).astype(BF)
        dhid[:, cols] = dhidden
        sums[:, cols] = column_sum(dhidden)
    total[...] += nt(dhid[...], widen[...])


def first_norm_kernel(
    info, xt, xl_own, ct, cl, dense_t, dense_l, bt, bl, gt, st, gl, sl, widen, hidden, narrow,
    first_t, first_l, low_t, low_l, normed_l, active, slope, total,
):
    own_rows, width = first_t.shape
    rows = pl.ds(pl.multiple_of(info[OWN], LANES), own_rows)
    first = xt[rows, :].astype(F32) + (nn(ct[...], dense_t[...]) + bt[2:3, :])
    first_t[...] = first
    normed = normalised(first)[0] * gt[0:1, :] + st[0:1, :]
    low_t[...] = normed.astype(BF)
    total[...] = normed + bt[3:4, :]
    first = xl_own[...].astype(F32) + (nn(cl[...], dense_l[...]) + bl[2:3, :])
    first_l[...] = first
    normed = normalised(first)[0] * gl[0:1, :] + sl[0:1, :]
    low_l[...] = normed.astype(BF)
    normed_l[...] = normed + bl[3:4, :]
    shard_forward(low_t, widen, biases_of(hidden[192:, :])[0], narrow, active, slope, total)


def piece_rows(info, rel):
    return pl.ds(pl.multiple_of(info[HALF + rel // 4] + info[PIECE + rel % 4], 32), 96)


def place_shard(info, plan, refs, weights):
    for ref, (rel, low, high) in zip(refs, plan):
        for part in (0, 1):
            if low <= 96 * part and high >= 96 * (part + 1):
                weights[part, piece_rows(info, rel), :] = ref[96 * part - low : 96 * (part + 1) - low, :]


def place_layout(info, plan, refs, both):
    for ref, (rel, low, high) in zip(refs, plan):
        if high == 224:
            at = pl.multiple_of((info[HALF + rel // 4] + info[PIECE + rel % 4]) // 4, 8)
            both[pl.ds(at, 24), :] = ref[192 - low :, :512].astype(F32)[:24]


def shard_kernel(plan, info, low, total_in, *refs):
    pieces = refs[: len(plan)]
    active, slope, total, weights, layout, both = refs[len(plan) :]
    place_shard(info, plan, pieces, weights)
    place_layout(info, plan, pieces, both)
    layout[...] = both[...].astype(BF)
    total[...] = total_in[...]
    bias = biases_of(pieces[0][192:, :])[0]
    shard_forward(low, weights.at[0], bias, weights.at[1], active, slope, total)


def upper_back(total, gain, shift, cot, keep, result, dout, sums):
    normal, scale = normalised(total[...])
    result[...] = (normal * gain[1:2, :] + shift[1:2, :]).astype(BF)
    upstream = cot.astype(F32) * keep
    dsecond = norm_back(upstream, normal, scale, gain[1:2, :])
    dout[...] = dsecond.astype(BF)
    sums[0:1, :] = column_sum(upstream * normal)
    sums[1:2, :] = column_sum(upstream)
    sums[2:3, :] = column_sum(dout[...])
    sums[3:4, :] = jnp.zeros_like(sums[3:4, :])
    total[...] = dsecond


def turn_kernel(plan, info, *refs):
    refs = list(refs)
    take = lambda n: [refs.pop(0) for _ in range(n)]
    low, total_in, gain, shift, cot, widen_own, narrow_own = take(7)
    slopes_in, actives = take(3), take(3)
    low_l, normed_l, gain_l, shift_l, cot_lt = take(5)
    first, first_l, dense, dense_l = take(4)
    widen_own_l, narrow_own_l, layout_one, layout_three, mine, first_piece, third_piece = take(7)
    weights_one, weights_three = take(2)
    pieces = take(len(plan))
    result, dout, dhid, sums, hsums, active = take(6)
    result_lt, sums_l, hsums_l, pack = take(4)
    lower, lower_l = take(4), take(4)
    weights, slope, dnormed, slope_l, active_l, dhid_l, dout_l, result_l, dnormed_l, dfirst_l, both = take(11)
    shards = dhid.shape[0]
    width = low.shape[1]
    dnormed[...] = total_in[...]
    dnormed_l[...] = normed_l[...]
    row = lax.broadcasted_iota(jnp.int32, (LANES, 1), 0)
    keep = []
    for j in range(low.shape[0] // LANES):
        place = row + info[PLACE + j]
        keep.append(jnp.where((place >= info[FLAGGED + j]) & (place < info[LIMIT + j]), 1.0, 0.0))
    keep = jnp.concatenate(keep, axis=0)

    width_l = low_l.shape[1]
    hidden_bias = [biases_of(ref[192:, :]) for ref in (mine, first_piece, pieces[0], third_piece)]
    place_layout(info, plan, pieces, both)
    last_l = both[...].astype(BF)
    layouts = [(widen_own_l[...], narrow_own_l[...])]
    layouts += [(v[:, :width_l], v[:, 256 : 256 + width_l]) for v in (layout_one[...], last_l, layout_three[...])]
    for s in range(shards):
        widen, narrow = layouts[s]
        shard_forward(low_l, widen, hidden_bias[s][1][:, :width_l], narrow, active_l.at[s], slope_l.at[s], dnormed_l)
    cot_l = tn(cot_lt[...], identity(width_l))
    upper_back(dnormed_l, gain_l, shift_l, cot_l, keep, result_l, dout_l, sums_l)
    result_lt[...] = nt(identity(width_l), result_l[...]).astype(BF)
    for s in range(shards):
        widen, narrow = layouts[s]
        shard_backward(dout_l, narrow, slope_l.at[s], widen, dhid_l.at[s], hsums_l.at[s], dnormed_l)
    for s in range(shards):
        pack[s] = jnp.zeros_like(pack[s])
        g = tn(active_l[s], dout_l[...]).astype(BF)
        pack[s, :128, :width_l] = g[:128]
        pack[s, :64, 512 : 512 + width_l] = g[128:]
        g = tn(low_l[...], dhid_l[s]).astype(BF)
        pack[s, :128, 256 : 256 + width_l] = g[:128]
        pack[s, 64:, 512 : 512 + width_l] = g[128:]

    place_shard(info, plan, pieces, weights)
    shard_forward(low, weights.at[0], hidden_bias[2][0], weights.at[1], active, slope, dnormed)
    upper_back(dnormed, gain, shift, cot[...], keep, result, dout, sums)
    shard_backward(dout, narrow_own, slopes_in[0], widen_own, dhid.at[0], hsums.at[0], dnormed)
    shard_backward(dout, weights_one.at[1], slopes_in[1], weights_one.at[0], dhid.at[1], hsums.at[1], dnormed)
    shard_backward(dout, weights.at[1], slope, weights.at[0], dhid.at[2], hsums.at[2], dnormed)
    shard_backward(dout, weights_three.at[1], slopes_in[2], weights_three.at[0], dhid.at[3], hsums.at[3], dnormed)

    lower_back(first, dnormed, gain, dense, *lower)
    dfirst_lt = lower_l[0]
    lower_back(first_l, dnormed_l, gain_l, dense_l, dfirst_l, *lower_l[1:])
    dfirst_lt[...] = jnp.transpose(dfirst_l[...])


def lower_back(first, dnormed, gain, dense, dfirst, dbranch, dcontext, sums):
    width = first.shape[1]
    wide = dcontext.shape[1]
    normal, scale = normalised(first[...])
    back = norm_back(dnormed[...], normal, scale, gain[0:1, :])
    sums[0:1, :] = column_sum(dnormed[...] * normal)
    sums[1:2, :] = column_sum(dnormed[...])
    dfirst[...] = back
    dbranch[...] = back.astype(BF)
    sums[2:3, :] = column_sum(dbranch[...])
    sums[3:4, :] = jnp.zeros_like(sums[3:4, :])
    dc = nt(dbranch[...], dense[...]).astype(BF)
    dcontext[:, :width] = dc
    if wide > width:
        dcontext[:, width:] = jnp.zeros((dc.shape[0], wide - width), BF)


EXTRA = 16


def ffn_send_kernel(info, a0, a1, a2, a3, dout, low, dhid, pack, send_a, send_b):
    half = pl.ds(pl.multiple_of(info[HALF + 1], LANES), 384)
    more = pl.ds(pl.multiple_of(info[HALF + 1] // 6, 64), 64)
    for s, active in enumerate((a0, a1, a2, a3)):
        send_a[s, :384] = tn(active[:, half], dout[...]).astype(BF)
        send_a[s, 384:] = pack[s, more, :]
        send_b[s] = tn(low[:, half], dhid[s]).astype(BF)


def ffn_keep_kernel(
    info, a0, a1, a2, a3, dout, low, dhid, recv_a, recv_b, pack, next_a, next_b, keep_a, keep_b, sum_a, sum_b,
):
    half = pl.ds(pl.multiple_of(info[HALF], LANES), 384)
    more = pl.ds(pl.multiple_of(info[HALF] // 6, 64), 64)
    for s, active in enumerate((a0, a1, a2, a3)):
        sum_a[:384] = (tn(active[:, half], dout[...]) + recv_a[s, :384].astype(F32)).astype(BF)
        sum_a[384:] = (pack[s, more, :].astype(F32) + recv_a[s, 384:].astype(F32)).astype(BF)
        sum_b[...] = (tn(low[:, half], dhid[s]) + recv_b[s].astype(F32)).astype(BF)
        for rel in range(4):
            rows = pl.ds(pl.multiple_of(info[PIECE + rel], 32), 96)
            rest = pl.ds(pl.multiple_of(384 + info[PIECE + rel] // 6, EXTRA), EXTRA)
            to = (next_a if rel % 2 else keep_a).at[rel // 2, s]
            to[:96] = sum_a[rows, :]
            to[96:] = sum_a[rest, :]
            (next_b if rel // 2 else keep_b)[rel % 2, s] = sum_b[rows, :]


def ffn_spread_kernel(info, keep_a, recv_a, keep_b, recv_b, out):
    rows = keep_a.shape[1]
    for s in range(4):
        group = lax.rem(info[GROUP] + s, 4)
        out[group, :rows] = (keep_a[s].astype(F32) + recv_a[s].astype(F32)).astype(BF)
        out[group, rows:] = (keep_b[s].astype(F32) + recv_b[s].astype(F32)).astype(BF)


def add(a, b, *more):
    total = a.astype(F32) + b.astype(F32)
    for value in more:
        total = total + value.astype(F32)
    return total.astype(BF)


def add_split(keep, recv, *zeros):
    return add(keep[1], recv[1], *zeros), add(keep[0], recv[0], *zeros)


def zero_of(value):
    return value[(0,) * value.ndim].astype(F32) * 0.0


def copied_spread_kernel(info, keep_a, recv_a, keep_b, recv_b, *outs):
    for k, out in enumerate(outs):
        keep, recv = (keep_a, recv_a) if k < 2 else (keep_b, recv_b)
        out[...] = (keep[k % 2].astype(F32) + recv[k % 2].astype(F32)).astype(out.dtype)


def ffn_final_kernel(plan, info, *refs):
    pieces, (narrow, widen, narrow_l, widen_l, pack) = refs[: len(plan)], refs[len(plan) :]
    for piece, (rel, low, high) in zip(pieces, plan):
        rows = piece_rows(info, rel)
        if low == 0:
            narrow[rows, :] = piece[:96].astype(F32)
            rest = pl.ds(pl.multiple_of((info[HALF + rel // 4] + info[PIECE + rel % 4]) // 6, EXTRA), EXTRA)
            pack[rest, :] = piece[96:112].astype(F32)
        if high > 112:
            widen[rows, :] = piece[112 - low :].astype(F32)
    width_l = narrow_l.shape[0]
    narrow_l[:128] = pack[:, :width_l]
    narrow_l[128:] = pack[:64, 512 : 512 + width_l]
    widen_l[:128] = pack[:, 256 : 256 + width_l]
    widen_l[128:] = pack[64:, 512 : 512 + width_l]


def copied_final_kernel(plan, info, *refs):
    pieces, refs = refs[: len(plan)], refs[len(plan) :]
    project, dense, project_l, dense_l = refs[:4]
    vectors, vectors_l, (extra,) = refs[4:8], refs[8:12], refs[12:]
    width = dense.shape[1]
    for piece, (rel, low, high) in zip(pieces, plan):
        rows = piece_rows(info, rel)
        for part in range(low, high):
            block = lax.rem(info[GROUP] + part, 4)
            at = pl.ds(pl.multiple_of(128 * block + (info[HALF + rel // 4] + info[PIECE + rel % 4]) // 6, EXTRA), EXTRA)
            extra[at, :] = piece[part - low, 96:].astype(F32)

            @pl.when(block < 3)
            def _():
                project[rows, pl.ds(pl.multiple_of(block * width, LANES), width)] = piece[part - low, :96].astype(F32)

            @pl.when(block == 3)
            def _():
                dense[rows, :] = piece[part - low, :96].astype(F32)

    width_l = dense_l.shape[0]
    for i in range(3):
        project_l[:, i * width_l : (i + 1) * width_l] = extra[:width_l, i * 256 : i * 256 + width_l]
    dense_l[...] = extra[width_l : 2 * width_l, :width_l]
    for at, (biases, gains, shifts, hidden), lanes in ((2 * width_l, vectors, width), (2 * width_l + 16, vectors_l, width_l)):
        rows = extra[at : at + 16, :lanes]
        for i, row in enumerate((8, 9, 6, 2)):
            biases[i : i + 1, :] = rows[row : row + 1]
        gains[0:1, :] = rows[4:5]
        gains[1:2, :] = rows[0:1]
        shifts[0:1, :] = rows[5:6]
        shifts[1:2, :] = rows[1:2]
        hidden[...] = extra[pl.ds(at + 12 + info[GROUP], 1), :lanes]


def attend_back_kernel(
    info, qt, kt, vt, ql, kl, vl, dct, dcl, lse,
    dq, dk, dv, dq_l, dk_l, dv_l,
    k_acc, v_acc, kl_acc, vl_acc, ql_acc,
):
    own_rows = qt.shape[0]
    window = kt.shape[0]
    block = window // 2
    pad = (dk.shape[0] - window) // 2
    for acc in (k_acc, v_acc, kl_acc, vl_acc, ql_acc):
        acc[...] = jnp.zeros_like(acc)
    for out in (dk, dv, dk_l, dv_l):
        edge = jnp.zeros((pad, out.shape[1]), BF)
        out[:pad, :] = edge
        out[pad + window :, :] = edge
    lane = lax.broadcasted_iota(jnp.int32, (1, LANES), 1)

    def one_pair(pair, carry):
        text_lanes = lanes_of(pair * LANES)
        group_lanes = lanes_of((pair // 4) * LANES)
        scaled = head_masks(pair, 0.125, 0.25)
        plain = head_masks(pair, 1.0, 1.0)
        for j in range(own_rows // LANES):
            rows = pl.ds(j * LANES, LANES)
            keys_at = pl.ds(pl.multiple_of(info[LOCAL + j] * block, block), block)
            stacked = stack_heads(qt[rows, text_lanes], ql[rows, group_lanes], scaled)
            keys = jnp.concatenate([kt[keys_at, text_lanes], kl[keys_at, group_lanes]], axis=1)
            values = jnp.concatenate([vt[keys_at, text_lanes], vl[keys_at, group_lanes]], axis=1)
            dcs = stack_heads(dct[rows, text_lanes], dcl[rows, group_lanes], plain)
            logs = lse[rows, :]
            log_total = jnp.concatenate(
                [
                    jnp.sum(jnp.where(lane == 2 * pair, logs, 0.0), axis=1, keepdims=True),
                    jnp.sum(jnp.where(lane == 2 * pair + 1, logs, 0.0), axis=1, keepdims=True),
                ],
                axis=0,
            )
            probs = jnp.exp(pair_scores(stacked, keys, info[LIMIT + j]) - log_total)
            dprobs = nt(dcs, values)
            inner = jnp.sum(probs * dprobs, axis=1, keepdims=True)
            dscores = (probs * (dprobs - inner)).astype(BF)
            text, layout = unstack_heads(nn(dscores, keys), scaled)
            dq[rows, text_lanes] = text.astype(BF)
            ql_acc[rows, group_lanes] += layout
            both = tn(dscores, stacked)
            k_acc[keys_at, text_lanes] += both[:, :LANES]
            kl_acc[keys_at, group_lanes] += both[:, LANES:]
            both = tn(probs.astype(BF), dcs)
            v_acc[keys_at, text_lanes] += both[:, :LANES]
            vl_acc[keys_at, group_lanes] += both[:, LANES:]
        return carry

    lax.fori_loop(0, HEADS // 2, one_pair, 0)
    middle = pl.ds(pad, window)
    dk[middle, :] = k_acc[...].astype(BF)
    dv[middle, :] = v_acc[...].astype(BF)
    dk_l[middle, :] = kl_acc[...].astype(BF)
    dv_l[middle, :] = vl_acc[...].astype(BF)
    dq_l[...] = ql_acc[...].astype(BF)


def key_value_grad(info, at, rows_out, wt, wl, dk, dv, dk_l, dv_l):
    width, wide = dk.shape[1], dk_l.shape[1]
    rows = pl.ds(pl.multiple_of(info[SHIFT] + at, LANES), rows_out)
    text = nt(dk[rows, :], wt[:, width : 2 * width]) + nt(dv[rows, :], wt[:, 2 * width :])
    layout = nt(wl[:, wide : 2 * wide], dk_l[rows, :]) + nt(wl[:, 2 * wide :], dv_l[rows, :])
    return text, layout


def store_packed(out, text, layout):
    own_rows = text.shape[0]
    half = layout.shape[0] // 2
    out[:own_rows, :] = text.astype(BF)
    out[own_rows:, :own_rows] = layout[:half].astype(BF)
    out[own_rows:, own_rows:] = layout[half:].astype(BF)


def sides_kernel(info, wt, wl, dk, dv, dk_l, dv_l, left, right):
    own_rows = left.shape[0] * 4 // 5
    for side, shift in ((left, 0), (right, 2 * own_rows)):
        store_packed(side, *key_value_grad(info, shift, own_rows, wt, wl, dk, dv, dk_l, dv_l))


def own_kernel(info, wt, wl, dq, dk, dv, dq_l, dk_l, dv_l, dfirst_t, dfirst_lt, left, right, out):
    own_rows, width = dq.shape
    wide = dq_l.shape[1]
    half = dfirst_lt.shape[0] // 2
    text, layout = key_value_grad(info, own_rows, own_rows, wt, wl, dk, dv, dk_l, dv_l)
    text = dfirst_t[...] + text + nt(dq[...], wt[:, :width])
    layout = dfirst_lt[...] + layout + nt(wl[:, :wide], dq_l[...])
    got = left[...].astype(F32) + right[...].astype(F32)
    text = text + got[:own_rows]
    layout = layout + jnp.concatenate([got[own_rows:, :own_rows], got[own_rows:, own_rows:]], axis=0)
    store_packed(out, text, layout)


def input_final_kernel(info, own, l1, l2, l3, r1, r2, r3, text, layout):
    own_rows, half = own.shape[0] * 4 // 5, layout.shape[0] // 2
    for distance, rows in ((0, own), (-1, l1), (-2, l2), (-3, l3), (1, r1), (2, r2), (3, r3)):
        group = info[GROUP] + distance

        @pl.when((group >= 0) & (group < 4))
        def _():
            at = pl.ds(pl.multiple_of(group * own_rows, LANES), own_rows)
            text[at, :] = rows[:own_rows, :].astype(F32)
            layout[:half, at] = rows[own_rows:, :own_rows].astype(F32)
            layout[half:, at] = rows[own_rows:, own_rows:].astype(F32)


def extras(
    info, xlt, dq, dv, dq_l, dk_l, dv_l, cl, db_l, sums_a, sums_b, hsums, sums_al, sums_bl, hsums_l, extra, small,
):
    own_rows = dq.shape[0]
    wide = dq_l.shape[1]
    width_l = xlt.shape[0]
    window = dk_l.shape[0] - 2 * own_rows
    own = pl.ds(pl.multiple_of(info[OWN], LANES), own_rows)
    seen = pl.ds(pl.multiple_of(info[WINDOW], LANES), window)
    middle = pl.ds(own_rows, window)
    extra[width_l:, :] = jnp.zeros((extra.shape[0] - width_l, extra.shape[1]), BF)
    extra[:width_l, :wide] = nn(xlt[:, own], dq_l[...]).astype(BF)
    extra[:width_l, wide : 2 * wide] = nn(xlt[:, seen], dk_l[middle, :]).astype(BF)
    extra[:width_l, 2 * wide : 3 * wide] = nn(xlt[:, seen], dv_l[middle, :]).astype(BF)
    extra[width_l : 2 * width_l, :width_l] = tn(cl[...], db_l[...]).astype(BF)
    small[...] = jnp.zeros_like(small)
    small[0:4, :] = sums_a[...]
    small[4:8, :] = sums_b[...]
    small[8:9, :] = column_sum(dq[...])
    small[9:10, :] = column_sum(dv[middle, :])
    small[16:20, :width_l] = sums_al[...]
    small[20:24, :width_l] = sums_bl[...]
    small[24:25, :wide] = column_sum(dq_l[...])
    small[25:26, :wide] = column_sum(dv_l[middle, :])
    for s in range(4):
        group = lax.rem(info[GROUP] + s, 4)
        small[pl.ds(12 + group, 1), :] = hsums[s]
        small[pl.ds(28 + group, 1), :width_l] = hsums_l[s]
    extra[2 * width_l : 2 * width_l + 32, :] = small[...].astype(BF)


def copied_grads(info, xt, dq, dk, dv, ct, db, half, store):
    own_rows = dq.shape[0]
    window = dk.shape[0] - 2 * own_rows
    own = pl.ds(pl.multiple_of(info[OWN], LANES), own_rows)
    seen = pl.ds(pl.multiple_of(info[WINDOW], LANES), window)
    middle = pl.ds(own_rows, window)
    for block in range(4):
        if block == 0:
            grad = tn(xt[own, half], dq[...])
        elif block == 1:
            grad = tn(xt[seen, half], dk[middle, :])
        elif block == 2:
            grad = tn(xt[seen, half], dv[middle, :])
        else:
            grad = tn(ct[:, half], db[...])
        store(block, info[SLOT + block], grad)


def copied_send_kernel(
    info, xt, dq, dk, dv, ct, db, xlt, dq_l, dk_l, dv_l, cl, db_l, sums_a, sums_b, hsums, sums_al, sums_bl, hsums_l,
    send, extra, small,
):
    half = pl.ds(pl.multiple_of(info[HALF + 1], LANES), 384)
    extras(info, xlt, dq, dv, dq_l, dk_l, dv_l, cl, db_l, sums_a, sums_b, hsums, sums_al, sums_bl, hsums_l, extra, small)

    def store(block, slot, grad):
        send[slot, :384] = grad.astype(BF)
        send[slot, 384:] = extra[pl.ds(pl.multiple_of(128 * block + info[HALF + 1] // 6, 64), 64), :]

    copied_grads(info, xt, dq, dk, dv, ct, db, half, store)


def copied_keep_kernel(info, xt, dq, dk, dv, ct, db, extra, recv, next_a, keep_a, next_b, keep_b, total):
    half = pl.ds(pl.multiple_of(info[HALF], LANES), 384)

    def store(block, slot, grad):
        more = pl.ds(pl.multiple_of(128 * block + info[HALF] // 6, 64), 64)
        total[slot, :384] = (grad + recv[slot, :384].astype(F32)).astype(BF)
        total[slot, 384:] = (extra[more, :].astype(F32) + recv[slot, 384:].astype(F32)).astype(BF)

    copied_grads(info, xt, dq, dk, dv, ct, db, half, store)
    for slot in range(4):
        for rel in range(4):
            x_part, y_part = rel % 2, rel // 2
            first, second = (x_part, y_part) if slot < 2 else (y_part, x_part)
            out = ((keep_a, next_a), (keep_b, next_b))[slot // 2][first].at[second, slot % 2]
            out[:96] = total[slot, pl.ds(pl.multiple_of(info[PIECE + rel], 32), 96), :]
            out[96:] = total[slot, pl.ds(pl.multiple_of(384 + info[PIECE + rel] // 6, EXTRA), EXTRA), :]


SM = pl.BlockSpec(memory_space=pltpu.SMEM)
VM = pl.BlockSpec(memory_space=pltpu.VMEM)
HB = pl.BlockSpec(memory_space=pl.ANY)


class InHbm:
    def __init__(self, dims, dtype=BF):
        self.shape, self.dtype = dims, dtype


def vmem_of(outs, scratch):
    held = list(outs) + [v for v in scratch if str(v.memory_space) == "vmem"]
    return int(1.1 * sum(math.prod(v.shape) * jnp.dtype(v.dtype).itemsize for v in held)) + (MARGIN << 20)


def call(name, kernel, operands, outs, scratch=(), after=(), in_hbm=0, final=False):
    operands = tuple(operands)
    outs = tuple(outs) + (shape((8, LANES), F32),)
    specs = [HB] * len(after) + [SM] + [VM] * (len(operands) - 1 - in_hbm) + [pl.BlockSpec(memory_space=pltpu.HBM)] * in_hbm
    limit = vmem_of(outs if final else (), scratch)
    operands = tuple(after) + operands
    at = len(operands) + len(outs) - 1

    def with_token(*refs):
        kernel(*refs[len(after) : at], *refs[at + 1 :])
        refs[at][...] = jnp.zeros_like(refs[at])

    return pl.pallas_call(
        with_token,
        out_shape=tuple(shape(o.shape, o.dtype) for o in outs),
        in_specs=specs,
        out_specs=[HB if isinstance(o, InHbm) else VM for o in outs],
        scratch_shapes=list(scratch),
        cost_estimate=pl.CostEstimate(flops=int(MICROSECONDS[name] * PER_MICROSECOND), bytes_accessed=0, transcendentals=0),
        compiler_params=pltpu.CompilerParams(vmem_limit_bytes=limit),
        name=name,
    )(*operands)


def shape(dims, dtype=BF):
    return jax.ShapeDtypeStruct(dims, dtype)


def flip(planes, bit):
    return [(i, i ^ bit) for i in range(planes)]


def gate(values, *tokens):
    outs = pl.pallas_call(
        lambda *refs: None,
        out_shape=tuple(shape(v.shape, v.dtype) for v in values),
        in_specs=[HB] * (len(values) + len(tokens)),
        out_specs=[HB] * len(values),
        input_output_aliases={i: i for i in range(len(values))},
        cost_estimate=pl.CostEstimate(flops=0, bytes_accessed=0, transcendentals=0),
        compiler_params=pltpu.CompilerParams(vmem_limit_bytes=1 << 20),
        name="gate",
    )(*values, *tokens)
    return list(outs)


def around(planes):
    return lambda v, bit: lax.ppermute(v, "dp", flip(planes, bit))


def forward(piece, by_x, by_y, planes, split, mid=None, token=None):
    across, parts = around(planes), piece.shape[0]
    if split == "x":
        return [(across(by_x, Y), 3, 0, parts)]
    if split == "y":
        return [(across(by_y, X), 3, 0, parts)]
    mid = mid or parts // 2
    low, high = across(by_x[:mid], Y), across(by_y[mid:], X)
    if token is not None:
        low, high = gate((low, high), token)
    return [(low, 3, 0, mid), (high, 3, mid, parts)]


def to_core(held, planes):
    across = around(planes)
    held = held + [(across(v, CORE), rel + 4, low, high) for v, rel, low, high in held]
    return [h[0] for h in held], tuple(h[1:] for h in held)


def spread(piece, planes, mid=None, token=None):
    across, parts = around(planes), piece.shape[0]
    by_x, by_y = across(piece, X), across(piece, Y)
    held = [(piece, 0, 0, parts), (by_x, 1, 0, parts), (by_y, 2, 0, parts)]
    return to_core(held + forward(piece, by_x, by_y, planes, "half", mid, token), planes)


def per_device(
    text_input, layout_input, block_starts, intersection_flags, text_cotangent, layout_cotangent,
    text_project, text_biases, text_dense, text_gains, text_shifts, text_widen, text_hidden_bias, text_narrow,
    layout_project, layout_biases, layout_dense, layout_gains, layout_shifts, layout_widen, layout_hidden_bias,
    layout_narrow,
):
    blocks, length = intersection_flags.shape
    total = blocks * length
    groups = lax.axis_size("tensor")
    planes = lax.axis_size("dp")
    own = total // groups
    tiles = own // LANES
    width = text_input.shape[1]
    width_l = layout_input.shape[1]
    wide = 2 * LANES
    window = 2 * length
    padded = window + 2 * own
    hid = text_narrow.shape[0]
    hid_l = layout_narrow.shape[0]
    piece = width // PIECES
    t = lax.axis_index("tensor").astype(jnp.int32)
    me = lax.axis_index("dp").astype(jnp.int32)
    core, x_bit, y_bit = me & 1, (me >> 1) & 1, (me >> 2) & 1

    def row_of(rc, rx, ry):
        return 4 * piece * (core ^ rc) + piece * ((x_bit ^ rx) + 2 * (y_bit ^ ry))

    flagged = jnp.sum(intersection_flags, axis=1, dtype=jnp.int32)
    base = jnp.minimum((t * own) // length, blocks - 2)
    tile_rows = t * own + LANES * jnp.arange(tiles, dtype=jnp.int32)
    tile_block = tile_rows // length
    pick = tile_block[:, None] == jnp.arange(blocks, dtype=jnp.int32)[None, :]
    limit = DOC - jnp.sum(jnp.where(pick, block_starts[None, :], 0), axis=1)
    flags_of = jnp.sum(jnp.where(pick, flagged[None, :], 0), axis=1)
    info = jnp.concatenate(
        [
            jnp.stack([t * own, base * length, t * own - base * length]),
            tile_block - base,
            limit,
            flags_of,
            tile_rows - tile_block * length,
            jnp.stack(
                [t, 4 * piece * core, 4 * piece * (1 - core)]
                + [row_of(0, rx, ry) - 4 * piece * core for ry in (0, 1) for rx in (0, 1)]
                + [(b - t) % groups for b in range(4)]
            ),
        ]
    ).astype(jnp.int32)

    shift_from = lambda k: [(i, (i - k) % groups) for i in range(groups)]
    shift_to = lambda k: [(i, (i + k) % groups) for i in range(groups)]
    bias = jnp.concatenate([text_hidden_bias, layout_hidden_bias, jnp.zeros((8 * LANES - hid - hid_l,), F32)])
    across = around(planes)
    row = row_of(0, 0, 0)
    mine, packed_up = call(
        "pack", pack_kernel,
        (jnp.zeros((1,), jnp.int32),
         jnp.concatenate([lax.dynamic_slice_in_dim(v, row, piece, 0) for v in (text_widen, text_narrow)], axis=0),
         jnp.concatenate([lax.dynamic_slice_in_dim(v, row // 4, piece // 4, 0) for v in (layout_widen, layout_narrow)], axis=0),
         bias.reshape(8, LANES)),
        (shape((2 * piece + 32, width)),),
    )
    from_group = lambda v, k: lax.ppermute(v, "tensor", shift_from(k))
    come = {k: from_group(mine, k) for k in (1, 3)}

    xlt = layout_input.T
    qt, kt, vt, ql, kl, vl, xl_own, wl, projected = call(
        "project", project_kernel,
        (info, text_input, xlt, text_project, layout_project, text_biases, layout_biases),
        (shape((own, width)), shape((window, width)), shape((window, width)),
         shape((own, wide)), shape((window, wide)), shape((window, wide)),
         shape((own, width_l)), shape((width_l, 3 * wide))),
        after=(packed_up,),
    )
    mine_again, come[1], come[3] = gate((mine, come[1], come[3]), projected)
    come[2] = from_group(mine_again, 2)
    by_x, by_y = {}, {}
    for k in (1, 3):
        by_x[k], by_y[k] = across(come[k], X), across(come[k], Y)
    ct, cl, lse, attended = call(
        "attend", attend_kernel,
        (info, qt, kt, vt, ql, kl, vl),
        (shape((own, width)), shape((own, width_l)), shape((own, LANES), F32)),
        scratch=(pltpu.VMEM((own, wide), F32),),
    )
    by_x[1], by_y[1], by_x[3], by_y[3], *came = gate(
        (by_x[1], by_y[1], by_x[3], by_y[3], come[1], come[2], come[3]), attended
    )
    come = dict(zip((1, 2, 3), came))
    forwarded = {k: forward(come[k], by_x[k], by_y[k], planes, {1: "x", 3: "y"}[k]) for k in (1, 3)}
    first_t, first_l, low_t, low_l, normed_l, active0, slope0, total_t, first_done = call(
        "first_norm", first_norm_kernel,
        (info, text_input, xl_own, ct, cl, text_dense, layout_dense, text_biases, layout_biases,
         text_gains, text_shifts, layout_gains, layout_shifts, text_widen, mine, text_narrow),
        (shape((own, width), F32), shape((own, width_l), F32), shape((own, width)), shape((own, width_l)),
         shape((own, width_l), F32), shape((own, hid)), shape((own, hid), F32), shape((own, width), F32)),
    )
    last_x, last_y = across(come[2], X), across(come[2], Y)
    *both, come[1], come[3], by_x[1], by_y[1], by_x[3], by_y[3] = gate(
        (forwarded[1][0][0], forwarded[3][0][0], come[1], come[3], by_x[1], by_y[1], by_x[3], by_y[3]), first_done
    )
    shards = {}
    for k, array in zip((1, 3), both):
        parts = come[k].shape[0]
        held = [(come[k], 0, 0, parts), (by_x[k], 1, 0, parts), (by_y[k], 2, 0, parts), (array, 3, 0, parts)]
        shards[k] = to_core(held, planes)
    by_x[2], by_y[2] = last_x, last_y
    last = forward(come[2], by_x[2], by_y[2], planes, "half", 96)
    actives, slopes, shard_weights, layouts, shard_done = {0: active0}, {0: slope0}, {}, {}, {}
    for k in (1, 3):
        arrays, plan = shards[k]
        actives[k], slopes[k], total_t, shard_weights[k], layouts[k], shard_done[k] = call(
            "shard", functools.partial(shard_kernel, plan),
            (info, low_t, total_t, *arrays),
            (shape((own, hid)), shape((own, hid), F32), shape((own, width), F32), shape((2, width, hid)),
             shape((width_l, 2 * wide))),
            scratch=(pltpu.VMEM((width_l, 2 * wide), F32),),
        )
    last = [(v,) + f[1:] for v, f in zip(gate([f[0] for f in last], shard_done[3]), last)]
    parts = come[2].shape[0]
    shards[2] = to_core([(come[2], 0, 0, parts), (by_x[2], 1, 0, parts), (by_y[2], 2, 0, parts)] + last, planes)
    arrays, plan = shards[2]
    rows_a = piece + EXTRA
    outs = call(
        "turn", functools.partial(turn_kernel, plan),
        (info, low_t, total_t, text_gains, text_shifts, text_cotangent, text_widen, text_narrow,
         slopes[0], slopes[1], slopes[3], actives[0], actives[1], actives[3],
         low_l, normed_l, layout_gains, layout_shifts, layout_cotangent.T, first_t, first_l, text_dense, layout_dense,
         layout_widen, layout_narrow, layouts[1], layouts[3],
         mine, come[1], come[3], shard_weights[1], shard_weights[3], *arrays),
        (shape((own, width)), shape((own, width)), shape((groups, own, hid)),
         shape((4, width), F32), shape((groups, 1, hid), F32), shape((own, hid)),
         shape((width_l, own)), shape((4, width_l), F32), shape((groups, 1, hid_l), F32), shape((groups, 128, width)),
         shape((own, width), F32), shape((own, width)), shape((own, width)), shape((4, width), F32),
         shape((width_l, own), F32), shape((own, width_l)), shape((own, wide)), shape((4, width_l), F32)),
        scratch=(pltpu.VMEM((2, width, hid), BF), pltpu.VMEM((own, hid), F32), pltpu.VMEM((own, width), F32),
                 pltpu.VMEM((groups, own, hid_l), F32), pltpu.VMEM((groups, own, hid_l), BF),
                 pltpu.VMEM((groups, own, hid_l), BF), pltpu.VMEM((own, width_l), BF), pltpu.VMEM((own, width_l), BF),
                 pltpu.VMEM((own, width_l), F32), pltpu.VMEM((own, width_l), F32), pltpu.VMEM((width_l, 2 * wide), F32)),
    )
    result_t, dout_t, dhid_t, sums_t, hsums_t, actives[2] = outs[:6]
    result_lt, sums_l, hsums_l, pack = outs[6:10]
    dfirst_t, db_t, dc_t, low_sums_t, dfirst_lt, db_l, dc_l, low_sums_l, turned = outs[10:]

    def across_planes(value):
        bit = PIECES
        while bit < planes:
            value = add(value, across(value, bit))
            bit *= 2
        return value

    ffn_in = (*(actives[k] for k in range(4)), dout_t, low_t, dhid_t)
    send_a, send_b, ffn_sent = call(
        "ffn_send", ffn_send_kernel, (info, *ffn_in, pack),
        (shape((groups, 4 * rows_a, width)), shape((groups, 4 * piece, width))),
    )
    recv_a, recv_b = across(send_a, CORE), across(send_b, CORE)
    dq, dk, dv, dq_l, dk_l, dv_l, attended_back = call(
        "attend_back", attend_back_kernel,
        (info, qt, kt, vt, ql, kl, vl, dc_t, dc_l, lse),
        (shape((own, width)), shape((padded, width)), shape((padded, width)),
         shape((own, wide)), shape((padded, wide)), shape((padded, wide))),
        scratch=(pltpu.VMEM((window, width), F32), pltpu.VMEM((window, width), F32),
                 pltpu.VMEM((window, wide), F32), pltpu.VMEM((window, wide), F32), pltpu.VMEM((own, wide), F32)),
        after=(ffn_sent,),
    )
    next_a, next_b, keep_a, keep_b, kept = call(
        "ffn_keep", ffn_keep_kernel, (info, *ffn_in, recv_a, recv_b, pack),
        (shape((2, groups, rows_a, width)), shape((2, groups, piece, width))) * 2,
        scratch=(pltpu.VMEM((4 * rows_a, width), BF), pltpu.VMEM((4 * piece, width), BF)), after=(attended_back,),
    )
    recv_a, recv_b = across(next_a, X), across(next_b, Y)
    copied_in = (text_input, dq, dk, dv, ct, db_t)
    send, extra, sent = call(
        "copied_send", copied_send_kernel,
        (info,) + copied_in + (xlt, dq_l, dk_l, dv_l, cl, db_l, sums_t, low_sums_t, hsums_t, sums_l, low_sums_l, hsums_l),
        (shape((groups, 4 * rows_a, width)), shape((4 * 128, width))),
        scratch=(pltpu.VMEM((32, width), F32),), after=(kept,),
    )
    packed = shape((own + own // 4, width))
    left, right, sided = call(
        "sides", sides_kernel, (info, text_project, wl, dk, dv, dk_l, dv_l), (packed, packed), after=(sent,)
    )
    from_right = lax.ppermute(left, "tensor", [(i + 1, i) for i in range(groups - 1)])
    from_left = lax.ppermute(right, "tensor", [(i, i + 1) for i in range(groups - 1)])

    recv = across(send, CORE)
    copied_next_a, copied_keep_a, copied_next_b, copied_keep_b, copied_kept = call(
        "copied_keep", copied_keep_kernel, (info,) + copied_in + (extra, recv),
        (shape((2, 2, rows_a, width)),) * 4,
        scratch=(pltpu.VMEM((groups, 4 * rows_a, width), BF),), after=(sided,),
    )
    copied_recv_a, copied_recv_b = across(copied_next_a, X), across(copied_next_b, Y)
    own_sum, owned = call(
        "own", own_kernel,
        (info, text_project, wl, dq, dk, dv, dq_l, dk_l, dv_l, dfirst_t, dfirst_lt, from_right, from_left),
        (packed,), after=(copied_kept,),
    )
    step_right = lambda v, far: lax.ppermute(v, "tensor", [(i, i + 1) for i in range(far, groups - 1)])
    step_left = lambda v, far: lax.ppermute(v, "tensor", [(i, i - 1) for i in range(groups - 1 - far, 0, -1)])
    lefts, rights = [step_right(own_sum, 0)], [step_left(own_sum, 0)]
    for far in (1, 2):
        lefts.append(step_right(lefts[-1], far))
        rights.append(step_left(rights[-1], far))
    to_group = lambda v, k: lax.ppermute(v, "tensor", shift_to(k))
    copied_next_a, copied_keep_a = add_split(copied_keep_a, copied_recv_a, zero_of(recv_a))
    copied_next_b, copied_keep_b = add_split(copied_keep_b, copied_recv_b, zero_of(recv_b))
    copied_recv_a, copied_recv_b = across(copied_next_a, Y), across(copied_next_b, X)
    *parts, copied_spreaded = call(
        "copied_spread", copied_spread_kernel, (info, copied_keep_a, copied_recv_a, copied_keep_b, copied_recv_b),
        (shape((rows_a, width)),) * 4,
        after=(lefts[0], rights[0]),
    )
    parts = [parts[0]] + [to_group(parts[k], k) for k in (1, 2, 3)]
    summed = across_planes(add(*parts, zero_of(lefts[1]), zero_of(rights[1])))
    next_a, keep_a = add_split(keep_a, recv_a, zero_of(lefts[1]), zero_of(rights[1]))
    next_b, keep_b = add_split(keep_b, recv_b, zero_of(lefts[1]), zero_of(rights[1]))
    recv_a, recv_b = across(next_a, Y), across(next_b, X)
    every = [summed] + [from_group(summed, k) for k in (1, 2, 3)]
    ffn_parts, _ = call(
        "ffn_spread", ffn_spread_kernel, (info, keep_a, recv_a, keep_b, recv_b),
        (shape((groups, rows_a + piece, width)),), after=tuple(every[1:]),
    )
    ffn_grads = lax.psum_scatter(ffn_parts, "tensor", scatter_dimension=0, tiled=False)
    every = jnp.stack(every)
    arrays, plan = spread(every, planes)
    vectors = lambda w, h: (shape((4, w), F32), shape((2, w), F32), shape((2, w), F32), shape((1, h), F32))
    outs = call(
        "copied_final", functools.partial(copied_final_kernel, plan), (info, *arrays),
        (shape((width, 3 * width), F32), shape((width, width), F32),
         shape((width_l, 3 * width_l), F32), shape((width_l, width_l), F32)) + vectors(width, hid) + vectors(width_l, hid_l),
        scratch=(pltpu.VMEM((4 * 128, width), F32),), final=True,
    )
    text_grad, layout_grad_t, given = call(
        "input_final", input_final_kernel, (info, own_sum, *lefts, *rights),
        (shape((total, width), F32), shape((width_l, total), F32)), after=(outs[-1],), final=True,
    )
    ffn_grads = add(across_planes(ffn_grads), zero_of(outs[-1]))
    ffn_arrays, ffn_plan = spread(ffn_grads, planes, rows_a, given)
    g_narrow, g_widen, g_narrow_l, g_widen_l, _ = call(
        "ffn_final", functools.partial(ffn_final_kernel, ffn_plan), (info, *ffn_arrays),
        (shape((hid, width), F32), shape((width, hid), F32), shape((hid_l, width_l), F32), shape((width_l, hid_l), F32)),
        scratch=(pltpu.VMEM((128, width), F32),), final=True,
    )
    g_project, g_dense, g_project_l, g_dense_l = outs[:4]
    bias_t, gain_t, shift_t, hb_t, bias_l, gain_l, shift_l, hb_l = outs[4:12]
    return (
        result_t, result_lt.T, text_grad, layout_grad_t.T,
        g_project, bias_t, g_dense, gain_t, shift_t, g_widen, hb_t[0], g_narrow,
        g_project_l, bias_l, g_dense_l, gain_l, shift_l, g_widen_l, hb_l[0], g_narrow_l,
    )


def solution(mesh):
    rows = P(("dp", "tensor"), None)
    weights = (P(), P(), P(), P(), P(), P(None, "tensor"), P("tensor"), P("tensor", None))
    return jax.shard_map(
        per_device,
        mesh=mesh,
        in_specs=(P("dp", None), P("dp", None), P("dp"), P("dp", None), rows, rows) + weights + weights,
        out_specs=(rows, rows, P("dp", None), P("dp", None)) + weights + weights,
        check_vma=False,
    )
```

```python
import functools
import math

import jax
import jax.numpy as jnp
from jax import lax
from jax.experimental import pallas as pl
from jax.experimental.pallas import tpu as pltpu
from jax.sharding import PartitionSpec as P

HEADS = 12
DOC = 2048
LANES = 128
epsilon = 1e-05
masked_score = -1e30
F32 = jnp.float32
BF = jnp.bfloat16

OWN, WINDOW, SHIFT, LOCAL, LIMIT, FLAGGED, PLACE, GROUP, HALF, PIECE, SLOT = 0, 1, 2, 3, 6, 9, 12, 15, 16, 18, 22
PIECES = 8
MARGIN = 8
CORE, X, Y = 1, 2, 4
PER_MICROSECOND = 0.2e9
MICROSECONDS = {
    "pack": 1, "project": 5, "attend": 9, "first_norm": 3, "shard": 3, "turn": 12, "ffn_send": 4, "ffn_keep": 4, "ffn_spread": 1,
    "attend_back": 15, "copied_send": 4, "sides": 3, "copied_keep": 3, "own": 3, "input_final": 4,
    "ffn_final": 3, "copied_spread": 1, "copied_final": 6,
}


def nn(a, b):
    return lax.dot_general(a, b, (((1,), (0,)), ((), ())), preferred_element_type=F32)


def nt(a, b):
    return lax.dot_general(a, b, (((1,), (1,)), ((), ())), preferred_element_type=F32)


def tn(a, b):
    return lax.dot_general(a, b, (((0,), (0,)), ((), ())), preferred_element_type=F32)


def mean(values):
    return jnp.mean(values, axis=-1, keepdims=True)


def column_sum(values):
    return jnp.sum(values.astype(F32), axis=0, keepdims=True)


def normalised(values):
    centre = values - mean(values)
    scale = lax.rsqrt(mean(centre * centre) + epsilon)
    return centre * scale, scale


def norm_back(upstream, normal, scale, gain_row):
    u = upstream * gain_row
    return scale * (u - mean(u) - normal * mean(u * normal))


def lanes_of(start):
    return pl.ds(pl.multiple_of(start, LANES), LANES)


def head_masks(pair, text_scale, layout_scale):
    lane = lax.broadcasted_iota(jnp.int32, (1, LANES), 1)
    first = 32 * pair - LANES * (pair // 4)
    text_a = jnp.where(lane < 64, text_scale, 0.0)
    text_b = jnp.where(lane < 64, 0.0, text_scale)
    layout_a = jnp.where((lane >= first) & (lane < first + 16), layout_scale, 0.0)
    layout_b = jnp.where((lane >= first + 16) & (lane < first + 32), layout_scale, 0.0)
    return text_a, layout_a, text_b, layout_b


def stack_heads(text, layout, masks):
    text_a, layout_a, text_b, layout_b = (m.astype(BF) for m in masks)
    upper = jnp.concatenate([text * text_a, layout * layout_a], axis=1)
    lower = jnp.concatenate([text * text_b, layout * layout_b], axis=1)
    return jnp.concatenate([upper, lower], axis=0)


def unstack_heads(stacked, masks):
    text_a, layout_a, text_b, layout_b = masks
    upper, lower = stacked[:LANES], stacked[LANES:]
    text = upper[:, :LANES] * text_a + lower[:, :LANES] * text_b
    layout = upper[:, LANES:] * layout_a + lower[:, LANES:] * layout_b
    return text, layout


def pair_scores(stacked, keys, limit):
    scores = nt(stacked, keys)
    key = lax.broadcasted_iota(jnp.int32, (1, scores.shape[1]), 1)
    return jnp.where(key < limit, scores, masked_score)


def pack_kernel(place, weights, layout, bias, bias_l, mine, rest):
    mine[:192] = weights[...]
    both = layout[...].astype(F32)
    for i, (row, lane) in enumerate(((0, 0), (0, 384), (8, 0))):
        rest[row : row + 8, lane : lane + 192] = both[8 * i : 8 * i + 8]
        rest[row : row + 8, lane + 192 : lane + 384] = both[24 + 8 * i : 32 + 8 * i]

    def split(values):
        high = values.astype(BF).astype(F32)
        middle = (values - high).astype(BF).astype(F32)
        return high, middle, values - high - middle

    for i, part in enumerate(split(bias[...])):
        rest[8 + 2 * i : 9 + 2 * i, 384:] = part[:, :384]
        rest[9 + 2 * i : 10 + 2 * i, 384:] = part[:, 384:]
    high, middle, low = split(bias_l[...])
    rest[14:15, 384:576] = high
    rest[14:15, 576:] = middle
    rest[15:16, 384:576] = low
    rest[15:16, 576:] = jnp.zeros_like(low)
    mine[192:, :] = rest[...].astype(BF)


def biases_of(piece):
    split = piece[192:208, 384:768].astype(F32)[8:]
    text = [split[i : i + 1] + split[i + 2 : i + 3] + split[i + 4 : i + 5] for i in (0, 1)]
    left, right = piece[192:208, 384:576].astype(F32), piece[192:208, 576:768].astype(F32)
    return jnp.concatenate(text, axis=1), left[14:15] + right[14:15] + left[15:16]


def identity(size):
    row = lax.broadcasted_iota(jnp.int32, (size, size), 0)
    column = lax.broadcasted_iota(jnp.int32, (size, size), 1)
    return jnp.where(row == column, 1.0, 0.0).astype(BF)


def project_kernel(info, xt, xlt, wt, wl, bt, bl, qt, kt, vt, ql, kl, vl, xl_own, wide_l):
    own_rows, width = qt.shape
    wide = ql.shape[1]
    width_l = wl.shape[0]
    own = pl.multiple_of(info[OWN], LANES)
    start = pl.multiple_of(info[WINDOW], LANES)
    rows = pl.ds(own, own_rows)
    for i in range(3):
        wide_l[:, i * wide : i * wide + width_l] = wl[:, i * width_l : (i + 1) * width_l]
        wide_l[:, i * wide + width_l : (i + 1) * wide] = jnp.zeros((width_l, wide - width_l), BF)
    edge = jnp.zeros((1, wide - width_l), F32)
    bias = [jnp.concatenate([bl[i : i + 1, :], edge], axis=1) for i in (0, 1)]
    qt[...] = (nn(xt[rows, :], wt[:, :width]) + bt[0:1, :]).astype(BF)
    ql[...] = (tn(xlt[:, rows], wide_l[:, :wide]) + bias[0]).astype(BF)
    xl_own[...] = tn(xlt[:, rows], identity(width_l)).astype(BF)

    def part(i, carry):
        rows = pl.ds(pl.multiple_of(i * 256, 256), 256)
        from_rows = pl.ds(pl.multiple_of(start + i * 256, 256), 256)
        x = xt[from_rows, :]
        kt[rows, :] = nn(x, wt[:, width : 2 * width]).astype(BF)
        vt[rows, :] = (nn(x, wt[:, 2 * width :]) + bt[1:2, :]).astype(BF)
        x = xlt[:, from_rows]
        kl[rows, :] = tn(x, wide_l[:, wide : 2 * wide]).astype(BF)
        vl[rows, :] = (tn(x, wide_l[:, 2 * wide :]) + bias[1]).astype(BF)
        return carry

    lax.fori_loop(0, kt.shape[0] // 256, part, 0)


def attend_kernel(info, qt, kt, vt, ql, kl, vl, ct, cl, lse, cl_acc):
    own_rows, layout_width = cl.shape
    block = kt.shape[0] // 2
    cl_acc[...] = jnp.zeros_like(cl_acc)
    lse[...] = jnp.zeros_like(lse)
    lane = lax.broadcasted_iota(jnp.int32, (1, LANES), 1)

    def one_pair(pair, carry):
        text_lanes = lanes_of(pair * LANES)
        group_lanes = lanes_of((pair // 4) * LANES)
        scaled = head_masks(pair, 0.125, 0.25)
        plain = head_masks(pair, 1.0, 1.0)
        for j in range(own_rows // LANES):
            rows = pl.ds(j * LANES, LANES)
            keys_at = pl.ds(pl.multiple_of(info[LOCAL + j] * block, block), block)
            stacked = stack_heads(qt[rows, text_lanes], ql[rows, group_lanes], scaled)
            keys = jnp.concatenate([kt[keys_at, text_lanes], kl[keys_at, group_lanes]], axis=1)
            values = jnp.concatenate([vt[keys_at, text_lanes], vl[keys_at, group_lanes]], axis=1)
            scores = pair_scores(stacked, keys, info[LIMIT + j])
            highest = jnp.max(scores, axis=-1, keepdims=True)
            exponent = jnp.exp(scores - highest)
            totals = jnp.sum(exponent, axis=-1, keepdims=True)
            probs = (exponent * (1.0 / totals)).astype(BF)
            text, layout = unstack_heads(nn(probs, values), plain)
            ct[rows, text_lanes] = text.astype(BF)
            cl_acc[rows, group_lanes] += layout
            log_total = highest + jnp.log(totals)
            lse[rows, :] = (
                lse[rows, :]
                + jnp.where(lane == 2 * pair, log_total[:LANES], 0.0)
                + jnp.where(lane == 2 * pair + 1, log_total[LANES:], 0.0)
            )
        return carry

    lax.fori_loop(0, HEADS // 2, one_pair, 0, unroll=2)
    cl[...] = cl_acc[:, :layout_width].astype(BF)


def gelu_both(hidden):
    below = 0.5 * (1.0 + lax.erf(hidden * math.sqrt(0.5)))
    density = jnp.exp(-0.5 * hidden * hidden) * (1.0 / math.sqrt(2.0 * math.pi))
    return hidden * below, below + hidden * density


def shard_forward(low, widen, bias, narrow, active, slope, total):
    hid = widen.shape[1]
    step = 256 if hid % 256 == 0 else hid
    for n in range(hid // step):
        cols = slice(n * step, (n + 1) * step)
        value, gradient = gelu_both(nn(low[...], widen[:, cols]) + bias[:, cols])
        active[:, cols] = value.astype(BF)
        slope[:, cols] = gradient
    total[...] += nn(active[...], narrow[...])


def shard_backward(dout, narrow, slope, widen, dhid, sums, total):
    hid = widen.shape[1]
    step = 256 if hid % 256 == 0 else hid
    for n in range(hid // step):
        cols = slice(n * step, (n + 1) * step)
        dhidden = (nt(dout[...], narrow[cols, :]) * slope[:, cols]).astype(BF)
        dhid[:, cols] = dhidden
        sums[:, cols] = column_sum(dhidden)
    total[...] += nt(dhid[...], widen[...])


def first_norm_kernel(
    info, xt, xl_own, ct, cl, dense_t, dense_l, bt, bl, gt, st, gl, sl, widen, hidden, narrow,
    first_t, first_l, low_t, low_l, normed_l, active, slope, total,
):
    own_rows, width = first_t.shape
    rows = pl.ds(pl.multiple_of(info[OWN], LANES), own_rows)
    first = xt[rows, :].astype(F32) + (nn(ct[...], dense_t[...]) + bt[2:3, :])
    first_t[...] = first
    normed = normalised(first)[0] * gt[0:1, :] + st[0:1, :]
    low_t[...] = normed.astype(BF)
    total[...] = normed + bt[3:4, :]
    first = xl_own[...].astype(F32) + (nn(cl[...], dense_l[...]) + bl[2:3, :])
    first_l[...] = first
    normed = normalised(first)[0] * gl[0:1, :] + sl[0:1, :]
    low_l[...] = normed.astype(BF)
    normed_l[...] = normed + bl[3:4, :]
    shard_forward(low_t, widen, biases_of(hidden)[0], narrow, active, slope, total)


def piece_rows(info, rel):
    return pl.ds(pl.multiple_of(info[HALF + rel // 4] + info[PIECE + rel % 4], 32), 96)


def place_shard(info, plan, refs, weights):
    for ref, (rel, low, high) in zip(refs, plan):
        for part in (0, 1):
            if low <= 96 * part and high >= 96 * (part + 1):
                weights[part, piece_rows(info, rel), :] = ref[96 * part - low : 96 * (part + 1) - low, :]


def place_layout(info, plan, refs, both):
    for ref, (rel, low, high) in zip(refs, plan):
        if high == 208:
            at = (info[HALF + rel // 4] + info[PIECE + rel % 4]) // 4
            for i, (row, lane) in enumerate(((0, 0), (0, 384), (8, 0))):
                rows = pl.ds(pl.multiple_of(at + 8 * i, 8), 8)
                for half in (0, 1):
                    lanes = slice(lane + 192 * half, lane + 192 * half + 192)
                    got = ref[192 - low : 208 - low, lanes].astype(F32)
                    both[rows, 256 * half : 256 * half + 192] = got[row : row + 8]


def shard_kernel(plan, info, low, total_in, *refs):
    pieces = refs[: len(plan)]
    active, slope, total, weights, layout, both = refs[len(plan) :]
    place_shard(info, plan, pieces, weights)
    place_layout(info, plan, pieces, both)
    layout[...] = both[...].astype(BF)
    total[...] = total_in[...]
    bias = biases_of(pieces[0])[0]
    shard_forward(low, weights.at[0], bias, weights.at[1], active, slope, total)


def upper_back(total, gain, shift, cot, keep, result, dout, sums):
    normal, scale = normalised(total[...])
    result[...] = (normal * gain[1:2, :] + shift[1:2, :]).astype(BF)
    upstream = cot.astype(F32) * keep
    dsecond = norm_back(upstream, normal, scale, gain[1:2, :])
    dout[...] = dsecond.astype(BF)
    sums[0:1, :] = column_sum(upstream * normal)
    sums[1:2, :] = column_sum(upstream)
    sums[2:3, :] = column_sum(dout[...])
    sums[3:4, :] = jnp.zeros_like(sums[3:4, :])
    total[...] = dsecond


def turn_kernel(plan, info, *refs):
    refs = list(refs)
    take = lambda n: [refs.pop(0) for _ in range(n)]
    low, total_in, gain, shift, cot, widen_own, narrow_own = take(7)
    slopes_in, actives = take(3), take(3)
    low_l, normed_l, gain_l, shift_l, cot_lt = take(5)
    first, first_l, dense, dense_l = take(4)
    widen_own_l, narrow_own_l, layout_one, layout_three, mine, first_piece, third_piece = take(7)
    weights_one, weights_three = take(2)
    pieces = take(len(plan))
    result, dout, dhid, sums, hsums, active = take(6)
    result_lt, sums_l, hsums_l, pack = take(4)
    lower, lower_l = take(4), take(4)
    weights, slope, dnormed, slope_l, active_l, dhid_l, dout_l, result_l, dnormed_l, dfirst_l, both = take(11)
    shards = dhid.shape[0]
    width = low.shape[1]
    dnormed[...] = total_in[...]
    dnormed_l[...] = normed_l[...]
    row = lax.broadcasted_iota(jnp.int32, (LANES, 1), 0)
    keep = []
    for j in range(low.shape[0] // LANES):
        place = row + info[PLACE + j]
        keep.append(jnp.where((place >= info[FLAGGED + j]) & (place < info[LIMIT + j]), 1.0, 0.0))
    keep = jnp.concatenate(keep, axis=0)

    width_l = low_l.shape[1]
    hidden_bias = [biases_of(ref) for ref in (mine, first_piece, pieces[0], third_piece)]
    place_layout(info, plan, pieces, both)
    last_l = both[...].astype(BF)
    layouts = [(widen_own_l[...], narrow_own_l[...])]
    layouts += [(v[:, :width_l], v[:, 256 : 256 + width_l]) for v in (layout_one[...], last_l, layout_three[...])]
    for s in range(shards):
        widen, narrow = layouts[s]
        shard_forward(low_l, widen, hidden_bias[s][1], narrow, active_l.at[s], slope_l.at[s], dnormed_l)
    cot_l = tn(cot_lt[...], identity(width_l))
    upper_back(dnormed_l, gain_l, shift_l, cot_l, keep, result_l, dout_l, sums_l)
    result_lt[...] = nt(identity(width_l), result_l[...]).astype(BF)
    for s in range(shards):
        widen, narrow = layouts[s]
        shard_backward(dout_l, narrow, slope_l.at[s], widen, dhid_l.at[s], hsums_l.at[s], dnormed_l)
    for s in range(shards):
        pack[s] = jnp.zeros_like(pack[s])
        g = tn(active_l[s], dout_l[...]).astype(BF)
        pack[s, :128, :width_l] = g[:128]
        pack[s, :64, 512 : 512 + width_l] = g[128:]
        g = tn(low_l[...], dhid_l[s]).astype(BF)
        pack[s, :128, 256 : 256 + width_l] = g[:128]
        pack[s, 64:, 512 : 512 + width_l] = g[128:]

    place_shard(info, plan, pieces, weights)
    shard_forward(low, weights.at[0], hidden_bias[2][0], weights.at[1], active, slope, dnormed)
    upper_back(dnormed, gain, shift, cot[...], keep, result, dout, sums)
    shard_backward(dout, narrow_own, slopes_in[0], widen_own, dhid.at[0], hsums.at[0], dnormed)
    shard_backward(dout, weights_one.at[1], slopes_in[1], weights_one.at[0], dhid.at[1], hsums.at[1], dnormed)
    shard_backward(dout, weights.at[1], slope, weights.at[0], dhid.at[2], hsums.at[2], dnormed)
    shard_backward(dout, weights_three.at[1], slopes_in[2], weights_three.at[0], dhid.at[3], hsums.at[3], dnormed)

    lower_back(first, dnormed, gain, dense, *lower)
    dfirst_lt = lower_l[0]
    lower_back(first_l, dnormed_l, gain_l, dense_l, dfirst_l, *lower_l[1:])
    dfirst_lt[...] = jnp.transpose(dfirst_l[...])


def lower_back(first, dnormed, gain, dense, dfirst, dbranch, dcontext, sums):
    width = first.shape[1]
    wide = dcontext.shape[1]
    normal, scale = normalised(first[...])
    back = norm_back(dnormed[...], normal, scale, gain[0:1, :])
    sums[0:1, :] = column_sum(dnormed[...] * normal)
    sums[1:2, :] = column_sum(dnormed[...])
    dfirst[...] = back
    dbranch[...] = back.astype(BF)
    sums[2:3, :] = column_sum(dbranch[...])
    sums[3:4, :] = jnp.zeros_like(sums[3:4, :])
    dc = nt(dbranch[...], dense[...]).astype(BF)
    dcontext[:, :width] = dc
    if wide > width:
        dcontext[:, width:] = jnp.zeros((dc.shape[0], wide - width), BF)


EXTRA = 16


def ffn_send_kernel(info, a0, a1, a2, a3, dout, low, dhid, pack, send_a, send_b):
    half = pl.ds(pl.multiple_of(info[HALF + 1], LANES), 384)
    more = pl.ds(pl.multiple_of(info[HALF + 1] // 6, 64), 64)
    for s, active in enumerate((a0, a1, a2, a3)):
        send_a[s, :384] = tn(active[:, half], dout[...]).astype(BF)
        send_a[s, 384:] = pack[s, more, :]
        send_b[s] = tn(low[:, half], dhid[s]).astype(BF)


def ffn_keep_kernel(
    info, a0, a1, a2, a3, dout, low, dhid, recv_a, recv_b, pack, next_a, next_b, keep_a, keep_b, sum_a, sum_b,
):
    half = pl.ds(pl.multiple_of(info[HALF], LANES), 384)
    more = pl.ds(pl.multiple_of(info[HALF] // 6, 64), 64)
    for s, active in enumerate((a0, a1, a2, a3)):
        sum_a[:384] = (tn(active[:, half], dout[...]) + recv_a[s, :384].astype(F32)).astype(BF)
        sum_a[384:] = (pack[s, more, :].astype(F32) + recv_a[s, 384:].astype(F32)).astype(BF)
        sum_b[...] = (tn(low[:, half], dhid[s]) + recv_b[s].astype(F32)).astype(BF)
        for rel in range(4):
            rows = pl.ds(pl.multiple_of(info[PIECE + rel], 32), 96)
            rest = pl.ds(pl.multiple_of(384 + info[PIECE + rel] // 6, EXTRA), EXTRA)
            to = (next_a if rel % 2 else keep_a).at[rel // 2, s]
            to[:96] = sum_a[rows, :]
            to[96:] = sum_a[rest, :]
            (next_b if rel // 2 else keep_b)[rel % 2, s] = sum_b[rows, :]


def ffn_spread_kernel(info, keep_a, recv_a, keep_b, recv_b, out):
    rows = keep_a.shape[1]
    for s in range(4):
        group = lax.rem(info[GROUP] + s, 4)
        out[group, :rows] = (keep_a[s].astype(F32) + recv_a[s].astype(F32)).astype(BF)
        out[group, rows:] = (keep_b[s].astype(F32) + recv_b[s].astype(F32)).astype(BF)


def add(a, b, *more):
    total = a.astype(F32) + b.astype(F32)
    for value in more:
        total = total + value.astype(F32)
    return total.astype(BF)


def add_split(keep, recv, *zeros):
    return add(keep[1], recv[1], *zeros), add(keep[0], recv[0], *zeros)


def zero_of(value):
    return value[(0,) * value.ndim].astype(F32) * 0.0


def copied_spread_kernel(info, keep_a, recv_a, keep_b, recv_b, *outs):
    for k, out in enumerate(outs):
        keep, recv = (keep_a, recv_a) if k < 2 else (keep_b, recv_b)
        out[...] = (keep[k % 2].astype(F32) + recv[k % 2].astype(F32)).astype(out.dtype)


def ffn_final_kernel(plan, info, *refs):
    pieces, (narrow, widen, narrow_l, widen_l, pack) = refs[: len(plan)], refs[len(plan) :]
    for piece, (rel, low, high) in zip(pieces, plan):
        rows = piece_rows(info, rel)
        if low == 0:
            narrow[rows, :] = piece[:96].astype(F32)
            rest = pl.ds(pl.multiple_of((info[HALF + rel // 4] + info[PIECE + rel % 4]) // 6, EXTRA), EXTRA)
            pack[rest, :] = piece[96:112].astype(F32)
        if high > 112:
            widen[rows, :] = piece[112 - low :].astype(F32)
    width_l = narrow_l.shape[0]
    narrow_l[:128] = pack[:, :width_l]
    narrow_l[128:] = pack[:64, 512 : 512 + width_l]
    widen_l[:128] = pack[:, 256 : 256 + width_l]
    widen_l[128:] = pack[64:, 512 : 512 + width_l]


def copied_final_kernel(plan, info, *refs):
    pieces, refs = refs[: len(plan)], refs[len(plan) :]
    project, dense, project_l, dense_l = refs[:4]
    vectors, vectors_l, (extra,) = refs[4:8], refs[8:12], refs[12:]
    width = dense.shape[1]
    for piece, (rel, low, high) in zip(pieces, plan):
        rows = piece_rows(info, rel)
        for part in range(low, high):
            block = lax.rem(info[GROUP] + part, 4)
            at = pl.ds(pl.multiple_of(128 * block + (info[HALF + rel // 4] + info[PIECE + rel % 4]) // 6, EXTRA), EXTRA)
            extra[at, :] = piece[part - low, 96:].astype(F32)

            @pl.when(block < 3)
            def _():
                project[rows, pl.ds(pl.multiple_of(block * width, LANES), width)] = piece[part - low, :96].astype(F32)

            @pl.when(block == 3)
            def _():
                dense[rows, :] = piece[part - low, :96].astype(F32)

    width_l = dense_l.shape[0]
    for i in range(3):
        project_l[:, i * width_l : (i + 1) * width_l] = extra[:width_l, i * 256 : i * 256 + width_l]
    dense_l[...] = extra[width_l : 2 * width_l, :width_l]
    for at, (biases, gains, shifts, hidden), lanes in ((2 * width_l, vectors, width), (2 * width_l + 16, vectors_l, width_l)):
        rows = extra[at : at + 16, :lanes]
        for i, row in enumerate((8, 9, 6, 2)):
            biases[i : i + 1, :] = rows[row : row + 1]
        gains[0:1, :] = rows[4:5]
        gains[1:2, :] = rows[0:1]
        shifts[0:1, :] = rows[5:6]
        shifts[1:2, :] = rows[1:2]
        hidden[...] = extra[pl.ds(at + 12 + info[GROUP], 1), :lanes]


def attend_back_kernel(
    info, qt, kt, vt, ql, kl, vl, dct, dcl, lse,
    dq, dk, dv, dq_l, dk_l, dv_l,
    k_acc, v_acc, kl_acc, vl_acc, ql_acc,
):
    own_rows = qt.shape[0]
    window = kt.shape[0]
    block = window // 2
    pad = (dk.shape[0] - window) // 2
    for acc in (k_acc, v_acc, kl_acc, vl_acc, ql_acc):
        acc[...] = jnp.zeros_like(acc)
    for out in (dk, dv, dk_l, dv_l):
        edge = jnp.zeros((pad, out.shape[1]), BF)
        out[:pad, :] = edge
        out[pad + window :, :] = edge
    lane = lax.broadcasted_iota(jnp.int32, (1, LANES), 1)

    def one_pair(pair, carry):
        text_lanes = lanes_of(pair * LANES)
        group_lanes = lanes_of((pair // 4) * LANES)
        scaled = head_masks(pair, 0.125, 0.25)
        plain = head_masks(pair, 1.0, 1.0)
        for j in range(own_rows // LANES):
            rows = pl.ds(j * LANES, LANES)
            keys_at = pl.ds(pl.multiple_of(info[LOCAL + j] * block, block), block)
            stacked = stack_heads(qt[rows, text_lanes], ql[rows, group_lanes], scaled)
            keys = jnp.concatenate([kt[keys_at, text_lanes], kl[keys_at, group_lanes]], axis=1)
            values = jnp.concatenate([vt[keys_at, text_lanes], vl[keys_at, group_lanes]], axis=1)
            dcs = stack_heads(dct[rows, text_lanes], dcl[rows, group_lanes], plain)
            logs = lse[rows, :]
            log_total = jnp.concatenate(
                [
                    jnp.sum(jnp.where(lane == 2 * pair, logs, 0.0), axis=1, keepdims=True),
                    jnp.sum(jnp.where(lane == 2 * pair + 1, logs, 0.0), axis=1, keepdims=True),
                ],
                axis=0,
            )
            probs = jnp.exp(pair_scores(stacked, keys, info[LIMIT + j]) - log_total)
            dprobs = nt(dcs, values)
            inner = jnp.sum(probs * dprobs, axis=1, keepdims=True)
            dscores = (probs * (dprobs - inner)).astype(BF)
            text, layout = unstack_heads(nn(dscores, keys), scaled)
            dq[rows, text_lanes] = text.astype(BF)
            ql_acc[rows, group_lanes] += layout
            both = tn(dscores, stacked)
            k_acc[keys_at, text_lanes] += both[:, :LANES]
            kl_acc[keys_at, group_lanes] += both[:, LANES:]
            both = tn(probs.astype(BF), dcs)
            v_acc[keys_at, text_lanes] += both[:, :LANES]
            vl_acc[keys_at, group_lanes] += both[:, LANES:]
        return carry

    lax.fori_loop(0, HEADS // 2, one_pair, 0, unroll=2)
    middle = pl.ds(pad, window)
    dk[middle, :] = k_acc[...].astype(BF)
    dv[middle, :] = v_acc[...].astype(BF)
    dk_l[middle, :] = kl_acc[...].astype(BF)
    dv_l[middle, :] = vl_acc[...].astype(BF)
    dq_l[...] = ql_acc[...].astype(BF)


def key_value_grad(info, at, rows_out, wt, wl, dk, dv, dk_l, dv_l):
    width, wide = dk.shape[1], dk_l.shape[1]
    rows = pl.ds(pl.multiple_of(info[SHIFT] + at, LANES), rows_out)
    text = nt(dk[rows, :], wt[:, width : 2 * width]) + nt(dv[rows, :], wt[:, 2 * width :])
    layout = nt(wl[:, wide : 2 * wide], dk_l[rows, :]) + nt(wl[:, 2 * wide :], dv_l[rows, :])
    return text, layout


def store_packed(out, text, layout):
    own_rows = text.shape[0]
    half = layout.shape[0] // 2
    out[:own_rows, :] = text.astype(BF)
    out[own_rows:, :own_rows] = layout[:half].astype(BF)
    out[own_rows:, own_rows:] = layout[half:].astype(BF)


def sides_kernel(info, wt, wl, dk, dv, dk_l, dv_l, left, right):
    own_rows = left.shape[0] * 4 // 5
    for side, shift in ((left, 0), (right, 2 * own_rows)):
        store_packed(side, *key_value_grad(info, shift, own_rows, wt, wl, dk, dv, dk_l, dv_l))


def own_kernel(info, wt, wl, dq, dk, dv, dq_l, dk_l, dv_l, dfirst_t, dfirst_lt, left, right, out):
    own_rows, width = dq.shape
    wide = dq_l.shape[1]
    half = dfirst_lt.shape[0] // 2
    text, layout = key_value_grad(info, own_rows, own_rows, wt, wl, dk, dv, dk_l, dv_l)
    text = dfirst_t[...] + text + nt(dq[...], wt[:, :width])
    layout = dfirst_lt[...] + layout + nt(wl[:, :wide], dq_l[...])
    got = left[...].astype(F32) + right[...].astype(F32)
    text = text + got[:own_rows]
    layout = layout + jnp.concatenate([got[own_rows:, :own_rows], got[own_rows:, own_rows:]], axis=0)
    store_packed(out, text, layout)


def input_final_kernel(info, own, l1, l2, l3, r1, r2, r3, text, layout):
    own_rows, half = own.shape[0] * 4 // 5, layout.shape[0] // 2
    for distance, rows in ((0, own), (-1, l1), (-2, l2), (-3, l3), (1, r1), (2, r2), (3, r3)):
        group = info[GROUP] + distance

        @pl.when((group >= 0) & (group < 4))
        def _():
            at = pl.ds(pl.multiple_of(group * own_rows, LANES), own_rows)
            text[at, :] = rows[:own_rows, :].astype(F32)
            layout[:half, at] = rows[own_rows:, :own_rows].astype(F32)
            layout[half:, at] = rows[own_rows:, own_rows:].astype(F32)


def extras(
    info, xlt, dq, dv, dq_l, dk_l, dv_l, cl, db_l, sums_a, sums_b, hsums, sums_al, sums_bl, hsums_l, extra, small,
):
    own_rows = dq.shape[0]
    wide = dq_l.shape[1]
    width_l = xlt.shape[0]
    window = dk_l.shape[0] - 2 * own_rows
    own = pl.ds(pl.multiple_of(info[OWN], LANES), own_rows)
    seen = pl.ds(pl.multiple_of(info[WINDOW], LANES), window)
    middle = pl.ds(own_rows, window)
    extra[width_l:, :] = jnp.zeros((extra.shape[0] - width_l, extra.shape[1]), BF)
    extra[:width_l, :wide] = nn(xlt[:, own], dq_l[...]).astype(BF)
    extra[:width_l, wide : 2 * wide] = nn(xlt[:, seen], dk_l[middle, :]).astype(BF)
    extra[:width_l, 2 * wide : 3 * wide] = nn(xlt[:, seen], dv_l[middle, :]).astype(BF)
    extra[width_l : 2 * width_l, :width_l] = tn(cl[...], db_l[...]).astype(BF)
    small[...] = jnp.zeros_like(small)
    small[0:4, :] = sums_a[...]
    small[4:8, :] = sums_b[...]
    small[8:9, :] = column_sum(dq[...])
    small[9:10, :] = column_sum(dv[middle, :])
    small[16:20, :width_l] = sums_al[...]
    small[20:24, :width_l] = sums_bl[...]
    small[24:25, :wide] = column_sum(dq_l[...])
    small[25:26, :wide] = column_sum(dv_l[middle, :])
    for s in range(4):
        group = lax.rem(info[GROUP] + s, 4)
        small[pl.ds(12 + group, 1), :] = hsums[s]
        small[pl.ds(28 + group, 1), :width_l] = hsums_l[s]
    extra[2 * width_l : 2 * width_l + 32, :] = small[...].astype(BF)


def copied_grads(info, xt, dq, dk, dv, ct, db, half, store):
    own_rows = dq.shape[0]
    window = dk.shape[0] - 2 * own_rows
    own = pl.ds(pl.multiple_of(info[OWN], LANES), own_rows)
    seen = pl.ds(pl.multiple_of(info[WINDOW], LANES), window)
    middle = pl.ds(own_rows, window)
    for block in range(4):
        if block == 0:
            grad = tn(xt[own, half], dq[...])
        elif block == 1:
            grad = tn(xt[seen, half], dk[middle, :])
        elif block == 2:
            grad = tn(xt[seen, half], dv[middle, :])
        else:
            grad = tn(ct[:, half], db[...])
        store(block, info[SLOT + block], grad)


def copied_send_kernel(
    info, xt, dq, dk, dv, ct, db, xlt, dq_l, dk_l, dv_l, cl, db_l, sums_a, sums_b, hsums, sums_al, sums_bl, hsums_l,
    send, extra, small,
):
    half = pl.ds(pl.multiple_of(info[HALF + 1], LANES), 384)
    extras(info, xlt, dq, dv, dq_l, dk_l, dv_l, cl, db_l, sums_a, sums_b, hsums, sums_al, sums_bl, hsums_l, extra, small)

    def store(block, slot, grad):
        send[slot, :384] = grad.astype(BF)
        send[slot, 384:] = extra[pl.ds(pl.multiple_of(128 * block + info[HALF + 1] // 6, 64), 64), :]

    copied_grads(info, xt, dq, dk, dv, ct, db, half, store)


def copied_keep_kernel(info, xt, dq, dk, dv, ct, db, extra, recv, next_a, keep_a, next_b, keep_b, total):
    half = pl.ds(pl.multiple_of(info[HALF], LANES), 384)

    def store(block, slot, grad):
        more = pl.ds(pl.multiple_of(128 * block + info[HALF] // 6, 64), 64)
        total[slot, :384] = (grad + recv[slot, :384].astype(F32)).astype(BF)
        total[slot, 384:] = (extra[more, :].astype(F32) + recv[slot, 384:].astype(F32)).astype(BF)

    copied_grads(info, xt, dq, dk, dv, ct, db, half, store)
    for slot in range(4):
        for rel in range(4):
            x_part, y_part = rel % 2, rel // 2
            first, second = (x_part, y_part) if slot < 2 else (y_part, x_part)
            out = ((keep_a, next_a), (keep_b, next_b))[slot // 2][first].at[second, slot % 2]
            out[:96] = total[slot, pl.ds(pl.multiple_of(info[PIECE + rel], 32), 96), :]
            out[96:] = total[slot, pl.ds(pl.multiple_of(384 + info[PIECE + rel] // 6, EXTRA), EXTRA), :]


SM = pl.BlockSpec(memory_space=pltpu.SMEM)
VM = pl.BlockSpec(memory_space=pltpu.VMEM)
HB = pl.BlockSpec(memory_space=pl.ANY)


class InHbm:
    def __init__(self, dims, dtype=BF):
        self.shape, self.dtype = dims, dtype


def vmem_of(outs, scratch):
    held = list(outs) + [v for v in scratch if str(v.memory_space) == "vmem"]
    return int(1.1 * sum(math.prod(v.shape) * jnp.dtype(v.dtype).itemsize for v in held)) + (MARGIN << 20)


def call(name, kernel, operands, outs, scratch=(), after=(), in_hbm=0, final=False):
    operands = tuple(operands)
    outs = tuple(outs) + (shape((8, LANES), F32),)
    specs = [HB] * len(after) + [SM] + [VM] * (len(operands) - 1 - in_hbm) + [pl.BlockSpec(memory_space=pltpu.HBM)] * in_hbm
    limit = vmem_of(outs if final else (), scratch)
    operands = tuple(after) + operands
    at = len(operands) + len(outs) - 1

    def with_token(*refs):
        kernel(*refs[len(after) : at], *refs[at + 1 :])
        refs[at][...] = jnp.zeros_like(refs[at])

    return pl.pallas_call(
        with_token,
        out_shape=tuple(shape(o.shape, o.dtype) for o in outs),
        in_specs=specs,
        out_specs=[HB if isinstance(o, InHbm) else VM for o in outs],
        scratch_shapes=list(scratch),
        cost_estimate=pl.CostEstimate(flops=int(MICROSECONDS[name] * PER_MICROSECOND), bytes_accessed=0, transcendentals=0),
        compiler_params=pltpu.CompilerParams(vmem_limit_bytes=limit),
        name=name,
    )(*operands)


def shape(dims, dtype=BF):
    return jax.ShapeDtypeStruct(dims, dtype)


def flip(planes, bit):
    return [(i, i ^ bit) for i in range(planes)]


def gate(values, *tokens):
    outs = pl.pallas_call(
        lambda *refs: None,
        out_shape=tuple(shape(v.shape, v.dtype) for v in values),
        in_specs=[HB] * (len(values) + len(tokens)),
        out_specs=[HB] * len(values),
        input_output_aliases={i: i for i in range(len(values))},
        cost_estimate=pl.CostEstimate(flops=0, bytes_accessed=0, transcendentals=0),
        compiler_params=pltpu.CompilerParams(vmem_limit_bytes=1 << 20),
        name="gate",
    )(*values, *tokens)
    return list(outs)


def around(planes):
    return lambda v, bit: lax.ppermute(v, "dp", flip(planes, bit))


def forward(piece, by_x, by_y, planes, split, mid=None, token=None):
    across, parts = around(planes), piece.shape[0]
    if split == "x":
        return [(across(by_x, Y), 3, 0, parts)]
    if split == "y":
        return [(across(by_y, X), 3, 0, parts)]
    mid = mid or parts // 2
    low, high = across(by_x[:mid], Y), across(by_y[mid:], X)
    if token is not None:
        low, high = gate((low, high), token)
    return [(low, 3, 0, mid), (high, 3, mid, parts)]


def to_core(held, planes):
    across = around(planes)
    held = held + [(across(v, CORE), rel + 4, low, high) for v, rel, low, high in held]
    return [h[0] for h in held], tuple(h[1:] for h in held)


def spread(piece, planes, mid=None, token=None):
    across, parts = around(planes), piece.shape[0]
    by_x, by_y = across(piece, X), across(piece, Y)
    held = [(piece, 0, 0, parts), (by_x, 1, 0, parts), (by_y, 2, 0, parts)]
    return to_core(held + forward(piece, by_x, by_y, planes, "half", mid, token), planes)


def per_device(
    text_input, layout_input, block_starts, intersection_flags, text_cotangent, layout_cotangent,
    text_project, text_biases, text_dense, text_gains, text_shifts, text_widen, text_hidden_bias, text_narrow,
    layout_project, layout_biases, layout_dense, layout_gains, layout_shifts, layout_widen, layout_hidden_bias,
    layout_narrow,
):
    blocks, length = intersection_flags.shape
    total = blocks * length
    groups = lax.axis_size("tensor")
    planes = lax.axis_size("dp")
    own = total // groups
    tiles = own // LANES
    width = text_input.shape[1]
    width_l = layout_input.shape[1]
    wide = 2 * LANES
    window = 2 * length
    padded = window + 2 * own
    hid = text_narrow.shape[0]
    hid_l = layout_narrow.shape[0]
    piece = width // PIECES
    t = lax.axis_index("tensor").astype(jnp.int32)
    me = lax.axis_index("dp").astype(jnp.int32)
    core, x_bit, y_bit = me & 1, (me >> 1) & 1, (me >> 2) & 1

    def row_of(rc, rx, ry):
        return 4 * piece * (core ^ rc) + piece * ((x_bit ^ rx) + 2 * (y_bit ^ ry))

    flagged = jnp.sum(intersection_flags, axis=1, dtype=jnp.int32)
    base = jnp.minimum((t * own) // length, blocks - 2)
    tile_rows = t * own + LANES * jnp.arange(tiles, dtype=jnp.int32)
    tile_block = tile_rows // length
    pick = tile_block[:, None] == jnp.arange(blocks, dtype=jnp.int32)[None, :]
    limit = DOC - jnp.sum(jnp.where(pick, block_starts[None, :], 0), axis=1)
    flags_of = jnp.sum(jnp.where(pick, flagged[None, :], 0), axis=1)
    info = jnp.concatenate(
        [
            jnp.stack([t * own, base * length, t * own - base * length]),
            tile_block - base,
            limit,
            flags_of,
            tile_rows - tile_block * length,
            jnp.stack(
                [t, 4 * piece * core, 4 * piece * (1 - core)]
                + [row_of(0, rx, ry) - 4 * piece * core for ry in (0, 1) for rx in (0, 1)]
                + [(b - t) % groups for b in range(4)]
            ),
        ]
    ).astype(jnp.int32)

    shift_from = lambda k: [(i, (i - k) % groups) for i in range(groups)]
    shift_to = lambda k: [(i, (i + k) % groups) for i in range(groups)]
    across = around(planes)
    row = row_of(0, 0, 0)
    mine, packed_up = call(
        "pack", pack_kernel,
        (jnp.zeros((1,), jnp.int32),
         jnp.concatenate([lax.dynamic_slice_in_dim(v, row, piece, 0) for v in (text_widen, text_narrow)], axis=0),
         jnp.concatenate([lax.dynamic_slice_in_dim(v, row // 4, piece // 4, 0) for v in (layout_widen, layout_narrow)], axis=0),
         text_hidden_bias[None, :], layout_hidden_bias[None, :]),
        (shape((2 * piece + EXTRA, width)),),
        scratch=(pltpu.VMEM((EXTRA, width), F32),),
    )
    from_group = lambda v, k: lax.ppermute(v, "tensor", shift_from(k))
    come = {k: from_group(mine, k) for k in (1, 3)}

    xlt = layout_input.T
    qt, kt, vt, ql, kl, vl, xl_own, wl, projected = call(
        "project", project_kernel,
        (info, text_input, xlt, text_project, layout_project, text_biases, layout_biases),
        (shape((own, width)), shape((window, width)), shape((window, width)),
         shape((own, wide)), shape((window, wide)), shape((window, wide)),
         shape((own, width_l)), shape((width_l, 3 * wide))),
        after=(packed_up,),
    )
    mine_again, come[1], come[3] = gate((mine, come[1], come[3]), projected)
    come[2] = from_group(mine_again, 2)
    by_x, by_y = {}, {}
    for k in (1, 3):
        by_x[k], by_y[k] = across(come[k], X), across(come[k], Y)
    ct, cl, lse, attended = call(
        "attend", attend_kernel,
        (info, qt, kt, vt, ql, kl, vl),
        (shape((own, width)), shape((own, width_l)), shape((own, LANES), F32)),
        scratch=(pltpu.VMEM((own, wide), F32),),
    )
    by_x[1], by_y[1], by_x[3], by_y[3], *came = gate(
        (by_x[1], by_y[1], by_x[3], by_y[3], come[1], come[2], come[3]), attended
    )
    come = dict(zip((1, 2, 3), came))
    forwarded = {k: forward(come[k], by_x[k], by_y[k], planes, {1: "x", 3: "y"}[k]) for k in (1, 3)}
    first_t, first_l, low_t, low_l, normed_l, active0, slope0, total_t, first_done = call(
        "first_norm", first_norm_kernel,
        (info, text_input, xl_own, ct, cl, text_dense, layout_dense, text_biases, layout_biases,
         text_gains, text_shifts, layout_gains, layout_shifts, text_widen, mine, text_narrow),
        (shape((own, width), F32), shape((own, width_l), F32), shape((own, width)), shape((own, width_l)),
         shape((own, width_l), F32), shape((own, hid)), shape((own, hid), F32), shape((own, width), F32)),
    )
    last_x, last_y = across(come[2], X), across(come[2], Y)
    *both, come[1], come[3], by_x[1], by_y[1], by_x[3], by_y[3] = gate(
        (forwarded[1][0][0], forwarded[3][0][0], come[1], come[3], by_x[1], by_y[1], by_x[3], by_y[3]), first_done
    )
    shards = {}
    for k, array in zip((1, 3), both):
        parts = come[k].shape[0]
        held = [(come[k], 0, 0, parts), (by_x[k], 1, 0, parts), (by_y[k], 2, 0, parts), (array, 3, 0, parts)]
        shards[k] = to_core(held, planes)
    by_x[2], by_y[2] = last_x, last_y
    last = forward(come[2], by_x[2], by_y[2], planes, "half", 96)
    actives, slopes, shard_weights, layouts, shard_done = {0: active0}, {0: slope0}, {}, {}, {}
    for k in (1, 3):
        arrays, plan = shards[k]
        actives[k], slopes[k], total_t, shard_weights[k], layouts[k], shard_done[k] = call(
            "shard", functools.partial(shard_kernel, plan),
            (info, low_t, total_t, *arrays),
            (shape((own, hid)), shape((own, hid), F32), shape((own, width), F32), shape((2, width, hid)),
             shape((width_l, 2 * wide))),
            scratch=(pltpu.VMEM((width_l, 2 * wide), F32),),
        )
    last = [(v,) + f[1:] for v, f in zip(gate([f[0] for f in last], shard_done[3]), last)]
    parts = come[2].shape[0]
    shards[2] = to_core([(come[2], 0, 0, parts), (by_x[2], 1, 0, parts), (by_y[2], 2, 0, parts)] + last, planes)
    arrays, plan = shards[2]
    rows_a = piece + EXTRA
    outs = call(
        "turn", functools.partial(turn_kernel, plan),
        (info, low_t, total_t, text_gains, text_shifts, text_cotangent, text_widen, text_narrow,
         slopes[0], slopes[1], slopes[3], actives[0], actives[1], actives[3],
         low_l, normed_l, layout_gains, layout_shifts, layout_cotangent.T, first_t, first_l, text_dense, layout_dense,
         layout_widen, layout_narrow, layouts[1], layouts[3],
         mine, come[1], come[3], shard_weights[1], shard_weights[3], *arrays),
        (shape((own, width)), shape((own, width)), shape((groups, own, hid)),
         shape((4, width), F32), shape((groups, 1, hid), F32), shape((own, hid)),
         shape((width_l, own)), shape((4, width_l), F32), shape((groups, 1, hid_l), F32), shape((groups, 128, width)),
         shape((own, width), F32), shape((own, width)), shape((own, width)), shape((4, width), F32),
         shape((width_l, own), F32), shape((own, width_l)), shape((own, wide)), shape((4, width_l), F32)),
        scratch=(pltpu.VMEM((2, width, hid), BF), pltpu.VMEM((own, hid), F32), pltpu.VMEM((own, width), F32),
                 pltpu.VMEM((groups, own, hid_l), F32), pltpu.VMEM((groups, own, hid_l), BF),
                 pltpu.VMEM((groups, own, hid_l), BF), pltpu.VMEM((own, width_l), BF), pltpu.VMEM((own, width_l), BF),
                 pltpu.VMEM((own, width_l), F32), pltpu.VMEM((own, width_l), F32), pltpu.VMEM((width_l, 2 * wide), F32)),
    )
    result_t, dout_t, dhid_t, sums_t, hsums_t, actives[2] = outs[:6]
    result_lt, sums_l, hsums_l, pack = outs[6:10]
    dfirst_t, db_t, dc_t, low_sums_t, dfirst_lt, db_l, dc_l, low_sums_l, turned = outs[10:]

    def across_planes(value):
        bit = PIECES
        while bit < planes:
            value = add(value, across(value, bit))
            bit *= 2
        return value

    ffn_in = (*(actives[k] for k in range(4)), dout_t, low_t, dhid_t)
    send_a, send_b, ffn_sent = call(
        "ffn_send", ffn_send_kernel, (info, *ffn_in, pack),
        (shape((groups, 4 * rows_a, width)), shape((groups, 4 * piece, width))),
    )
    recv_a, recv_b = across(send_a, CORE), across(send_b, CORE)
    dq, dk, dv, dq_l, dk_l, dv_l, attended_back = call(
        "attend_back", attend_back_kernel,
        (info, qt, kt, vt, ql, kl, vl, dc_t, dc_l, lse),
        (shape((own, width)), shape((padded, width)), shape((padded, width)),
         shape((own, wide)), shape((padded, wide)), shape((padded, wide))),
        scratch=(pltpu.VMEM((window, width), F32), pltpu.VMEM((window, width), F32),
                 pltpu.VMEM((window, wide), F32), pltpu.VMEM((window, wide), F32), pltpu.VMEM((own, wide), F32)),
        after=(ffn_sent,),
    )
    next_a, next_b, keep_a, keep_b, kept = call(
        "ffn_keep", ffn_keep_kernel, (info, *ffn_in, recv_a, recv_b, pack),
        (shape((2, groups, rows_a, width)), shape((2, groups, piece, width))) * 2,
        scratch=(pltpu.VMEM((4 * rows_a, width), BF), pltpu.VMEM((4 * piece, width), BF)), after=(attended_back,),
    )
    recv_a, recv_b = across(next_a, X), across(next_b, Y)
    copied_in = (text_input, dq, dk, dv, ct, db_t)
    send, extra, sent = call(
        "copied_send", copied_send_kernel,
        (info,) + copied_in + (xlt, dq_l, dk_l, dv_l, cl, db_l, sums_t, low_sums_t, hsums_t, sums_l, low_sums_l, hsums_l),
        (shape((groups, 4 * rows_a, width)), shape((4 * 128, width))),
        scratch=(pltpu.VMEM((32, width), F32),), after=(kept,),
    )
    packed = shape((own + own // 4, width))
    left, right, sided = call(
        "sides", sides_kernel, (info, text_project, wl, dk, dv, dk_l, dv_l), (packed, packed), after=(sent,)
    )
    from_right = lax.ppermute(left, "tensor", [(i + 1, i) for i in range(groups - 1)])
    from_left = lax.ppermute(right, "tensor", [(i, i + 1) for i in range(groups - 1)])

    recv = across(send, CORE)
    copied_next_a, copied_keep_a, copied_next_b, copied_keep_b, copied_kept = call(
        "copied_keep", copied_keep_kernel, (info,) + copied_in + (extra, recv),
        (shape((2, 2, rows_a, width)),) * 4,
        scratch=(pltpu.VMEM((groups, 4 * rows_a, width), BF),), after=(sided,),
    )
    copied_recv_a, copied_recv_b = across(copied_next_a, X), across(copied_next_b, Y)
    own_sum, owned = call(
        "own", own_kernel,
        (info, text_project, wl, dq, dk, dv, dq_l, dk_l, dv_l, dfirst_t, dfirst_lt, from_right, from_left),
        (packed,), after=(copied_kept,),
    )
    step_right = lambda v, far: lax.ppermute(v, "tensor", [(i, i + 1) for i in range(far, groups - 1)])
    step_left = lambda v, far: lax.ppermute(v, "tensor", [(i, i - 1) for i in range(groups - 1 - far, 0, -1)])
    lefts, rights = [step_right(own_sum, 0)], [step_left(own_sum, 0)]
    for far in (1, 2):
        lefts.append(step_right(lefts[-1], far))
        rights.append(step_left(rights[-1], far))
    to_group = lambda v, k: lax.ppermute(v, "tensor", shift_to(k))
    copied_next_a, copied_keep_a = add_split(copied_keep_a, copied_recv_a, zero_of(recv_a))
    copied_next_b, copied_keep_b = add_split(copied_keep_b, copied_recv_b, zero_of(recv_b))
    copied_recv_a, copied_recv_b = across(copied_next_a, Y), across(copied_next_b, X)
    *parts, copied_spreaded = call(
        "copied_spread", copied_spread_kernel, (info, copied_keep_a, copied_recv_a, copied_keep_b, copied_recv_b),
        (shape((rows_a, width)),) * 4,
        after=(lefts[0], rights[0]),
    )
    parts = [parts[0]] + [to_group(parts[k], k) for k in (1, 2, 3)]
    summed = across_planes(add(*parts, zero_of(lefts[1]), zero_of(rights[1])))
    next_a, keep_a = add_split(keep_a, recv_a, zero_of(lefts[1]), zero_of(rights[1]))
    next_b, keep_b = add_split(keep_b, recv_b, zero_of(lefts[1]), zero_of(rights[1]))
    recv_a, recv_b = across(next_a, Y), across(next_b, X)
    every = [summed] + [from_group(summed, k) for k in (1, 2, 3)]
    ffn_parts, _ = call(
        "ffn_spread", ffn_spread_kernel, (info, keep_a, recv_a, keep_b, recv_b),
        (shape((groups, rows_a + piece, width)),), after=tuple(every[1:]),
    )
    ffn_grads = lax.psum_scatter(ffn_parts, "tensor", scatter_dimension=0, tiled=False)
    every = jnp.stack(every)
    arrays, plan = spread(every, planes)
    vectors = lambda w, h: (shape((4, w), F32), shape((2, w), F32), shape((2, w), F32), shape((1, h), F32))
    outs = call(
        "copied_final", functools.partial(copied_final_kernel, plan), (info, *arrays),
        (shape((width, 3 * width), F32), shape((width, width), F32),
         shape((width_l, 3 * width_l), F32), shape((width_l, width_l), F32)) + vectors(width, hid) + vectors(width_l, hid_l),
        scratch=(pltpu.VMEM((4 * 128, width), F32),), final=True,
    )
    text_grad, layout_grad_t, given = call(
        "input_final", input_final_kernel, (info, own_sum, *lefts, *rights),
        (shape((total, width), F32), shape((width_l, total), F32)), after=(outs[-1],), final=True,
    )
    ffn_grads = add(across_planes(ffn_grads), zero_of(outs[-1]))
    ffn_arrays, ffn_plan = spread(ffn_grads, planes, rows_a, given)
    g_narrow, g_widen, g_narrow_l, g_widen_l, _ = call(
        "ffn_final", functools.partial(ffn_final_kernel, ffn_plan), (info, *ffn_arrays),
        (shape((hid, width), F32), shape((width, hid), F32), shape((hid_l, width_l), F32), shape((width_l, hid_l), F32)),
        scratch=(pltpu.VMEM((128, width), F32),), final=True,
    )
    g_project, g_dense, g_project_l, g_dense_l = outs[:4]
    bias_t, gain_t, shift_t, hb_t, bias_l, gain_l, shift_l, hb_l = outs[4:12]
    return (
        result_t, result_lt.T, text_grad, layout_grad_t.T,
        g_project, bias_t, g_dense, gain_t, shift_t, g_widen, hb_t[0], g_narrow,
        g_project_l, bias_l, g_dense_l, gain_l, shift_l, g_widen_l, hb_l[0], g_narrow_l,
    )


def solution(mesh):
    rows = P(("dp", "tensor"), None)
    weights = (P(), P(), P(), P(), P(), P(None, "tensor"), P("tensor"), P("tensor", None))
    return jax.shard_map(
        per_device,
        mesh=mesh,
        in_specs=(P("dp", None), P("dp", None), P("dp"), P("dp", None), rows, rows) + weights + weights,
        out_specs=(rows, rows, P("dp", None), P("dp", None)) + weights + weights,
        check_vma=False,
    )
```

```python
import functools
import math

import jax
import jax.numpy as jnp
from jax import lax
from jax.experimental import pallas as pl
from jax.experimental.pallas import tpu as pltpu
from jax.sharding import PartitionSpec as P

HEADS = 12
DOC = 2048
LANES = 128
epsilon = 1e-05
masked_score = -1e30
F32 = jnp.float32
BF = jnp.bfloat16

OWN, WINDOW, SHIFT, LOCAL, LIMIT, FLAGGED, PLACE, GROUP, HALF, PIECE, SLOT = 0, 1, 2, 3, 6, 9, 12, 15, 16, 18, 22
PIECES = 8
MARGIN = 8
CORE, X, Y = 1, 2, 4
PER_MICROSECOND = 0.2e9
MICROSECONDS = {
    "pack": 1, "project": 5, "attend": 9, "first_norm": 3, "shard": 3, "turn": 12, "ffn_send": 4, "ffn_keep": 4, "ffn_spread": 1,
    "attend_back": 15, "copied_send": 4, "sides": 3, "copied_keep": 3, "own": 3, "input_final": 4,
    "ffn_final": 3, "copied_spread": 1, "copied_final": 6,
}


def nn(a, b):
    return lax.dot_general(a, b, (((1,), (0,)), ((), ())), preferred_element_type=F32)


def nt(a, b):
    return lax.dot_general(a, b, (((1,), (1,)), ((), ())), preferred_element_type=F32)


def tn(a, b):
    return lax.dot_general(a, b, (((0,), (0,)), ((), ())), preferred_element_type=F32)


def mean(values):
    return jnp.mean(values, axis=-1, keepdims=True)


def column_sum(values):
    return jnp.sum(values.astype(F32), axis=0, keepdims=True)


def normalised(values):
    centre = values - mean(values)
    scale = lax.rsqrt(mean(centre * centre) + epsilon)
    return centre * scale, scale


def norm_back(upstream, normal, scale, gain_row):
    u = upstream * gain_row
    return scale * (u - mean(u) - normal * mean(u * normal))


def lanes_of(start):
    return pl.ds(pl.multiple_of(start, LANES), LANES)


def head_masks(pair, text_scale, layout_scale):
    lane = lax.broadcasted_iota(jnp.int32, (1, LANES), 1)
    first = 32 * pair - LANES * (pair // 4)
    text_a = jnp.where(lane < 64, text_scale, 0.0)
    text_b = jnp.where(lane < 64, 0.0, text_scale)
    layout_a = jnp.where((lane >= first) & (lane < first + 16), layout_scale, 0.0)
    layout_b = jnp.where((lane >= first + 16) & (lane < first + 32), layout_scale, 0.0)
    return text_a, layout_a, text_b, layout_b


def stack_heads(text, layout, masks):
    text_a, layout_a, text_b, layout_b = (m.astype(BF) for m in masks)
    upper = jnp.concatenate([text * text_a, layout * layout_a], axis=1)
    lower = jnp.concatenate([text * text_b, layout * layout_b], axis=1)
    return jnp.concatenate([upper, lower], axis=0)


def unstack_heads(stacked, masks):
    text_a, layout_a, text_b, layout_b = masks
    upper, lower = stacked[:LANES], stacked[LANES:]
    text = upper[:, :LANES] * text_a + lower[:, :LANES] * text_b
    layout = upper[:, LANES:] * layout_a + lower[:, LANES:] * layout_b
    return text, layout


def pair_scores(stacked, keys, limit):
    scores = nt(stacked, keys)
    key = lax.broadcasted_iota(jnp.int32, (1, scores.shape[1]), 1)
    return jnp.where(key < limit, scores, masked_score)


def pack_kernel(place, weights, layout, bias, bias_l, mine, rest):
    mine[:192] = weights[...]
    both = layout[...].astype(F32)
    for i, (row, lane) in enumerate(((0, 0), (0, 384), (8, 0))):
        rest[row : row + 8, lane : lane + 192] = both[8 * i : 8 * i + 8]
        rest[row : row + 8, lane + 192 : lane + 384] = both[24 + 8 * i : 32 + 8 * i]

    def split(values):
        high = values.astype(BF).astype(F32)
        middle = (values - high).astype(BF).astype(F32)
        return high, middle, values - high - middle

    for i, part in enumerate(split(bias[...])):
        rest[8 + 2 * i : 9 + 2 * i, 384:] = part[:, :384]
        rest[9 + 2 * i : 10 + 2 * i, 384:] = part[:, 384:]
    high, middle, low = split(bias_l[...])
    rest[14:15, 384:576] = high
    rest[14:15, 576:] = middle
    rest[15:16, 384:576] = low
    rest[15:16, 576:] = jnp.zeros_like(low)
    mine[192:, :] = rest[...].astype(BF)


def biases_of(piece):
    split = piece[192:208, 384:768].astype(F32)[8:]
    text = [split[i : i + 1] + split[i + 2 : i + 3] + split[i + 4 : i + 5] for i in (0, 1)]
    left, right = piece[192:208, 384:576].astype(F32), piece[192:208, 576:768].astype(F32)
    return jnp.concatenate(text, axis=1), left[14:15] + right[14:15] + left[15:16]


def identity(size):
    row = lax.broadcasted_iota(jnp.int32, (size, size), 0)
    column = lax.broadcasted_iota(jnp.int32, (size, size), 1)
    return jnp.where(row == column, 1.0, 0.0).astype(BF)


def project_kernel(info, xt, xlt, wt, wl, bt, bl, qt, kt, vt, ql, kl, vl, xl_own, wide_l):
    own_rows, width = qt.shape
    wide = ql.shape[1]
    width_l = wl.shape[0]
    own = pl.multiple_of(info[OWN], LANES)
    start = pl.multiple_of(info[WINDOW], LANES)
    rows = pl.ds(own, own_rows)
    for i in range(3):
        wide_l[:, i * wide : i * wide + width_l] = wl[:, i * width_l : (i + 1) * width_l]
        wide_l[:, i * wide + width_l : (i + 1) * wide] = jnp.zeros((width_l, wide - width_l), BF)
    edge = jnp.zeros((1, wide - width_l), F32)
    bias = [jnp.concatenate([bl[i : i + 1, :], edge], axis=1) for i in (0, 1)]
    qt[...] = (nn(xt[rows, :], wt[:, :width]) + bt[0:1, :]).astype(BF)
    ql[...] = (tn(xlt[:, rows], wide_l[:, :wide]) + bias[0]).astype(BF)
    xl_own[...] = tn(xlt[:, rows], identity(width_l)).astype(BF)

    def part(i, carry):
        rows = pl.ds(pl.multiple_of(i * 256, 256), 256)
        from_rows = pl.ds(pl.multiple_of(start + i * 256, 256), 256)
        x = xt[from_rows, :]
        kt[rows, :] = nn(x, wt[:, width : 2 * width]).astype(BF)
        vt[rows, :] = (nn(x, wt[:, 2 * width :]) + bt[1:2, :]).astype(BF)
        x = xlt[:, from_rows]
        kl[rows, :] = tn(x, wide_l[:, wide : 2 * wide]).astype(BF)
        vl[rows, :] = (tn(x, wide_l[:, 2 * wide :]) + bias[1]).astype(BF)
        return carry

    lax.fori_loop(0, kt.shape[0] // 256, part, 0)


def attend_kernel(info, qt, kt, vt, ql, kl, vl, ct, cl, lse, cl_acc):
    own_rows, layout_width = cl.shape
    block = kt.shape[0] // 2
    cl_acc[...] = jnp.zeros_like(cl_acc)
    lse[...] = jnp.zeros_like(lse)
    lane = lax.broadcasted_iota(jnp.int32, (1, LANES), 1)

    def one_pair(pair, carry):
        text_lanes = lanes_of(pair * LANES)
        group_lanes = lanes_of((pair // 4) * LANES)
        scaled = head_masks(pair, 0.125, 0.25)
        plain = head_masks(pair, 1.0, 1.0)
        for j in range(own_rows // LANES):
            rows = pl.ds(j * LANES, LANES)
            keys_at = pl.ds(pl.multiple_of(info[LOCAL + j] * block, block), block)
            stacked = stack_heads(qt[rows, text_lanes], ql[rows, group_lanes], scaled)
            keys = jnp.concatenate([kt[keys_at, text_lanes], kl[keys_at, group_lanes]], axis=1)
            values = jnp.concatenate([vt[keys_at, text_lanes], vl[keys_at, group_lanes]], axis=1)
            scores = pair_scores(stacked, keys, info[LIMIT + j])
            highest = jnp.max(scores, axis=-1, keepdims=True)
            exponent = jnp.exp(scores - highest)
            totals = jnp.sum(exponent, axis=-1, keepdims=True)
            probs = (exponent * (1.0 / totals)).astype(BF)
            text, layout = unstack_heads(nn(probs, values), plain)
            ct[rows, text_lanes] = text.astype(BF)
            cl_acc[rows, group_lanes] += layout
            log_total = highest + jnp.log(totals)
            lse[rows, :] = (
                lse[rows, :]
                + jnp.where(lane == 2 * pair, log_total[:LANES], 0.0)
                + jnp.where(lane == 2 * pair + 1, log_total[LANES:], 0.0)
            )
        return carry

    lax.fori_loop(0, HEADS // 2, one_pair, 0, unroll=3)
    cl[...] = cl_acc[:, :layout_width].astype(BF)


def gelu_both(hidden):
    below = 0.5 * (1.0 + lax.erf(hidden * math.sqrt(0.5)))
    density = jnp.exp(-0.5 * hidden * hidden) * (1.0 / math.sqrt(2.0 * math.pi))
    return hidden * below, below + hidden * density


def shard_forward(low, widen, bias, narrow, active, slope, total):
    hid = widen.shape[1]
    step = 256 if hid % 256 == 0 else hid
    for n in range(hid // step):
        cols = slice(n * step, (n + 1) * step)
        value, gradient = gelu_both(nn(low[...], widen[:, cols]) + bias[:, cols])
        active[:, cols] = value.astype(BF)
        slope[:, cols] = gradient
    total[...] += nn(active[...], narrow[...])


def shard_backward(dout, narrow, slope, widen, dhid, sums, total):
    hid = widen.shape[1]
    step = 256 if hid % 256 == 0 else hid
    for n in range(hid // step):
        cols = slice(n * step, (n + 1) * step)
        dhidden = (nt(dout[...], narrow[cols, :]) * slope[:, cols]).astype(BF)
        dhid[:, cols] = dhidden
        sums[:, cols] = column_sum(dhidden)
    total[...] += nt(dhid[...], widen[...])


def first_norm_kernel(
    info, xt, xl_own, ct, cl, dense_t, dense_l, bt, bl, gt, st, gl, sl, widen, hidden, narrow,
    first_t, first_l, low_t, low_l, normed_l, active, slope, total,
):
    own_rows, width = first_t.shape
    rows = pl.ds(pl.multiple_of(info[OWN], LANES), own_rows)
    first = xt[rows, :].astype(F32) + (nn(ct[...], dense_t[...]) + bt[2:3, :])
    first_t[...] = first
    normed = normalised(first)[0] * gt[0:1, :] + st[0:1, :]
    low_t[...] = normed.astype(BF)
    total[...] = normed + bt[3:4, :]
    first = xl_own[...].astype(F32) + (nn(cl[...], dense_l[...]) + bl[2:3, :])
    first_l[...] = first
    normed = normalised(first)[0] * gl[0:1, :] + sl[0:1, :]
    low_l[...] = normed.astype(BF)
    normed_l[...] = normed + bl[3:4, :]
    shard_forward(low_t, widen, biases_of(hidden)[0], narrow, active, slope, total)


def piece_rows(info, rel):
    return pl.ds(pl.multiple_of(info[HALF + rel // 4] + info[PIECE + rel % 4], 32), 96)


def place_shard(info, plan, refs, weights):
    for ref, (rel, low, high) in zip(refs, plan):
        for part in (0, 1):
            if low <= 96 * part and high >= 96 * (part + 1):
                weights[part, piece_rows(info, rel), :] = ref[96 * part - low : 96 * (part + 1) - low, :]


def place_layout(info, plan, refs, both):
    for ref, (rel, low, high) in zip(refs, plan):
        if high == 208:
            at = (info[HALF + rel // 4] + info[PIECE + rel % 4]) // 4
            for i, (row, lane) in enumerate(((0, 0), (0, 384), (8, 0))):
                rows = pl.ds(pl.multiple_of(at + 8 * i, 8), 8)
                for half in (0, 1):
                    lanes = slice(lane + 192 * half, lane + 192 * half + 192)
                    got = ref[192 - low : 208 - low, lanes].astype(F32)
                    both[rows, 256 * half : 256 * half + 192] = got[row : row + 8]


def shard_kernel(plan, info, low, total_in, *refs):
    pieces = refs[: len(plan)]
    active, slope, total, weights, layout, both = refs[len(plan) :]
    place_shard(info, plan, pieces, weights)
    place_layout(info, plan, pieces, both)
    layout[...] = both[...].astype(BF)
    total[...] = total_in[...]
    bias = biases_of(pieces[0])[0]
    shard_forward(low, weights.at[0], bias, weights.at[1], active, slope, total)


def upper_back(total, gain, shift, cot, keep, result, dout, sums):
    normal, scale = normalised(total[...])
    result[...] = (normal * gain[1:2, :] + shift[1:2, :]).astype(BF)
    upstream = cot.astype(F32) * keep
    dsecond = norm_back(upstream, normal, scale, gain[1:2, :])
    dout[...] = dsecond.astype(BF)
    sums[0:1, :] = column_sum(upstream * normal)
    sums[1:2, :] = column_sum(upstream)
    sums[2:3, :] = column_sum(dout[...])
    sums[3:4, :] = jnp.zeros_like(sums[3:4, :])
    total[...] = dsecond


def turn_kernel(plan, info, *refs):
    refs = list(refs)
    take = lambda n: [refs.pop(0) for _ in range(n)]
    low, total_in, gain, shift, cot, widen_own, narrow_own = take(7)
    slopes_in, actives = take(3), take(3)
    low_l, normed_l, gain_l, shift_l, cot_lt = take(5)
    first, first_l, dense, dense_l = take(4)
    widen_own_l, narrow_own_l, layout_one, layout_three, mine, first_piece, third_piece = take(7)
    weights_one, weights_three = take(2)
    pieces = take(len(plan))
    result, dout, dhid, sums, hsums, active = take(6)
    result_lt, sums_l, hsums_l, pack = take(4)
    lower, lower_l = take(4), take(4)
    weights, slope, dnormed, slope_l, active_l, dhid_l, dout_l, result_l, dnormed_l, dfirst_l, both = take(11)
    shards = dhid.shape[0]
    width = low.shape[1]
    dnormed[...] = total_in[...]
    dnormed_l[...] = normed_l[...]
    row = lax.broadcasted_iota(jnp.int32, (LANES, 1), 0)
    keep = []
    for j in range(low.shape[0] // LANES):
        place = row + info[PLACE + j]
        keep.append(jnp.where((place >= info[FLAGGED + j]) & (place < info[LIMIT + j]), 1.0, 0.0))
    keep = jnp.concatenate(keep, axis=0)

    width_l = low_l.shape[1]
    hidden_bias = [biases_of(ref) for ref in (mine, first_piece, pieces[0], third_piece)]
    place_layout(info, plan, pieces, both)
    last_l = both[...].astype(BF)
    layouts = [(widen_own_l[...], narrow_own_l[...])]
    layouts += [(v[:, :width_l], v[:, 256 : 256 + width_l]) for v in (layout_one[...], last_l, layout_three[...])]
    for s in range(shards):
        widen, narrow = layouts[s]
        shard_forward(low_l, widen, hidden_bias[s][1], narrow, active_l.at[s], slope_l.at[s], dnormed_l)
    cot_l = tn(cot_lt[...], identity(width_l))
    upper_back(dnormed_l, gain_l, shift_l, cot_l, keep, result_l, dout_l, sums_l)
    result_lt[...] = nt(identity(width_l), result_l[...]).astype(BF)
    for s in range(shards):
        widen, narrow = layouts[s]
        shard_backward(dout_l, narrow, slope_l.at[s], widen, dhid_l.at[s], hsums_l.at[s], dnormed_l)
    for s in range(shards):
        pack[s] = jnp.zeros_like(pack[s])
        g = tn(active_l[s], dout_l[...]).astype(BF)
        pack[s, :128, :width_l] = g[:128]
        pack[s, :64, 512 : 512 + width_l] = g[128:]
        g = tn(low_l[...], dhid_l[s]).astype(BF)
        pack[s, :128, 256 : 256 + width_l] = g[:128]
        pack[s, 64:, 512 : 512 + width_l] = g[128:]

    place_shard(info, plan, pieces, weights)
    shard_forward(low, weights.at[0], hidden_bias[2][0], weights.at[1], active, slope, dnormed)
    upper_back(dnormed, gain, shift, cot[...], keep, result, dout, sums)
    shard_backward(dout, narrow_own, slopes_in[0], widen_own, dhid.at[0], hsums.at[0], dnormed)
    shard_backward(dout, weights_one.at[1], slopes_in[1], weights_one.at[0], dhid.at[1], hsums.at[1], dnormed)
    shard_backward(dout, weights.at[1], slope, weights.at[0], dhid.at[2], hsums.at[2], dnormed)
    shard_backward(dout, weights_three.at[1], slopes_in[2], weights_three.at[0], dhid.at[3], hsums.at[3], dnormed)

    lower_back(first, dnormed, gain, dense, *lower)
    dfirst_lt = lower_l[0]
    lower_back(first_l, dnormed_l, gain_l, dense_l, dfirst_l, *lower_l[1:])
    dfirst_lt[...] = jnp.transpose(dfirst_l[...])


def lower_back(first, dnormed, gain, dense, dfirst, dbranch, dcontext, sums):
    width = first.shape[1]
    wide = dcontext.shape[1]
    normal, scale = normalised(first[...])
    back = norm_back(dnormed[...], normal, scale, gain[0:1, :])
    sums[0:1, :] = column_sum(dnormed[...] * normal)
    sums[1:2, :] = column_sum(dnormed[...])
    dfirst[...] = back
    dbranch[...] = back.astype(BF)
    sums[2:3, :] = column_sum(dbranch[...])
    sums[3:4, :] = jnp.zeros_like(sums[3:4, :])
    dc = nt(dbranch[...], dense[...]).astype(BF)
    dcontext[:, :width] = dc
    if wide > width:
        dcontext[:, width:] = jnp.zeros((dc.shape[0], wide - width), BF)


EXTRA = 16


def ffn_send_kernel(info, a0, a1, a2, a3, dout, low, dhid, pack, send_a, send_b):
    half = pl.ds(pl.multiple_of(info[HALF + 1], LANES), 384)
    more = pl.ds(pl.multiple_of(info[HALF + 1] // 6, 64), 64)
    for s, active in enumerate((a0, a1, a2, a3)):
        send_a[s, :384] = tn(active[:, half], dout[...]).astype(BF)
        send_a[s, 384:] = pack[s, more, :]
        send_b[s] = tn(low[:, half], dhid[s]).astype(BF)


def ffn_keep_kernel(
    info, a0, a1, a2, a3, dout, low, dhid, recv_a, recv_b, pack, next_a, next_b, keep_a, keep_b, sum_a, sum_b,
):
    half = pl.ds(pl.multiple_of(info[HALF], LANES), 384)
    more = pl.ds(pl.multiple_of(info[HALF] // 6, 64), 64)
    for s, active in enumerate((a0, a1, a2, a3)):
        sum_a[:384] = (tn(active[:, half], dout[...]) + recv_a[s, :384].astype(F32)).astype(BF)
        sum_a[384:] = (pack[s, more, :].astype(F32) + recv_a[s, 384:].astype(F32)).astype(BF)
        sum_b[...] = (tn(low[:, half], dhid[s]) + recv_b[s].astype(F32)).astype(BF)
        for rel in range(4):
            rows = pl.ds(pl.multiple_of(info[PIECE + rel], 32), 96)
            rest = pl.ds(pl.multiple_of(384 + info[PIECE + rel] // 6, EXTRA), EXTRA)
            to = (next_a if rel % 2 else keep_a).at[rel // 2, s]
            to[:96] = sum_a[rows, :]
            to[96:] = sum_a[rest, :]
            (next_b if rel // 2 else keep_b)[rel % 2, s] = sum_b[rows, :]


def ffn_spread_kernel(info, keep_a, recv_a, keep_b, recv_b, out):
    rows = keep_a.shape[1]
    for s in range(4):
        group = lax.rem(info[GROUP] + s, 4)
        out[group, :rows] = (keep_a[s].astype(F32) + recv_a[s].astype(F32)).astype(BF)
        out[group, rows:] = (keep_b[s].astype(F32) + recv_b[s].astype(F32)).astype(BF)


def add(a, b, *more):
    total = a.astype(F32) + b.astype(F32)
    for value in more:
        total = total + value.astype(F32)
    return total.astype(BF)


def add_split(keep, recv, *zeros):
    return add(keep[1], recv[1], *zeros), add(keep[0], recv[0], *zeros)


def zero_of(value):
    return value[(0,) * value.ndim].astype(F32) * 0.0


def copied_spread_kernel(info, keep_a, recv_a, keep_b, recv_b, *outs):
    for k, out in enumerate(outs):
        keep, recv = (keep_a, recv_a) if k < 2 else (keep_b, recv_b)
        out[...] = (keep[k % 2].astype(F32) + recv[k % 2].astype(F32)).astype(out.dtype)


def ffn_final_kernel(plan, info, *refs):
    pieces, (narrow, widen, narrow_l, widen_l, pack) = refs[: len(plan)], refs[len(plan) :]
    for piece, (rel, low, high) in zip(pieces, plan):
        rows = piece_rows(info, rel)
        if low == 0:
            narrow[rows, :] = piece[:96].astype(F32)
            rest = pl.ds(pl.multiple_of((info[HALF + rel // 4] + info[PIECE + rel % 4]) // 6, EXTRA), EXTRA)
            pack[rest, :] = piece[96:112].astype(F32)
        if high > 112:
            widen[rows, :] = piece[112 - low :].astype(F32)
    width_l = narrow_l.shape[0]
    narrow_l[:128] = pack[:, :width_l]
    narrow_l[128:] = pack[:64, 512 : 512 + width_l]
    widen_l[:128] = pack[:, 256 : 256 + width_l]
    widen_l[128:] = pack[64:, 512 : 512 + width_l]


def copied_final_kernel(plan, info, *refs):
    pieces, refs = refs[: len(plan)], refs[len(plan) :]
    project, dense, project_l, dense_l = refs[:4]
    vectors, vectors_l, (extra,) = refs[4:8], refs[8:12], refs[12:]
    width = dense.shape[1]
    for piece, (rel, low, high) in zip(pieces, plan):
        rows = piece_rows(info, rel)
        for part in range(low, high):
            block = lax.rem(info[GROUP] + part, 4)
            at = pl.ds(pl.multiple_of(128 * block + (info[HALF + rel // 4] + info[PIECE + rel % 4]) // 6, EXTRA), EXTRA)
            extra[at, :] = piece[part - low, 96:].astype(F32)

            @pl.when(block < 3)
            def _():
                project[rows, pl.ds(pl.multiple_of(block * width, LANES), width)] = piece[part - low, :96].astype(F32)

            @pl.when(block == 3)
            def _():
                dense[rows, :] = piece[part - low, :96].astype(F32)

    width_l = dense_l.shape[0]
    for i in range(3):
        project_l[:, i * width_l : (i + 1) * width_l] = extra[:width_l, i * 256 : i * 256 + width_l]
    dense_l[...] = extra[width_l : 2 * width_l, :width_l]
    for at, (biases, gains, shifts, hidden), lanes in ((2 * width_l, vectors, width), (2 * width_l + 16, vectors_l, width_l)):
        rows = extra[at : at + 16, :lanes]
        for i, row in enumerate((8, 9, 6, 2)):
            biases[i : i + 1, :] = rows[row : row + 1]
        gains[0:1, :] = rows[4:5]
        gains[1:2, :] = rows[0:1]
        shifts[0:1, :] = rows[5:6]
        shifts[1:2, :] = rows[1:2]
        hidden[...] = extra[pl.ds(at + 12 + info[GROUP], 1), :lanes]


def attend_back_kernel(
    info, qt, kt, vt, ql, kl, vl, dct, dcl, lse,
    dq, dk, dv, dq_l, dk_l, dv_l,
    k_acc, v_acc, kl_acc, vl_acc, ql_acc,
):
    own_rows = qt.shape[0]
    window = kt.shape[0]
    block = window // 2
    pad = (dk.shape[0] - window) // 2
    for acc in (k_acc, v_acc, kl_acc, vl_acc, ql_acc):
        acc[...] = jnp.zeros_like(acc)
    for out in (dk, dv, dk_l, dv_l):
        edge = jnp.zeros((pad, out.shape[1]), BF)
        out[:pad, :] = edge
        out[pad + window :, :] = edge
    lane = lax.broadcasted_iota(jnp.int32, (1, LANES), 1)

    def one_pair(pair, carry):
        text_lanes = lanes_of(pair * LANES)
        group_lanes = lanes_of((pair // 4) * LANES)
        scaled = head_masks(pair, 0.125, 0.25)
        plain = head_masks(pair, 1.0, 1.0)
        for j in range(own_rows // LANES):
            rows = pl.ds(j * LANES, LANES)
            keys_at = pl.ds(pl.multiple_of(info[LOCAL + j] * block, block), block)
            stacked = stack_heads(qt[rows, text_lanes], ql[rows, group_lanes], scaled)
            keys = jnp.concatenate([kt[keys_at, text_lanes], kl[keys_at, group_lanes]], axis=1)
            values = jnp.concatenate([vt[keys_at, text_lanes], vl[keys_at, group_lanes]], axis=1)
            dcs = stack_heads(dct[rows, text_lanes], dcl[rows, group_lanes], plain)
            logs = lse[rows, :]
            log_total = jnp.concatenate(
                [
                    jnp.sum(jnp.where(lane == 2 * pair, logs, 0.0), axis=1, keepdims=True),
                    jnp.sum(jnp.where(lane == 2 * pair + 1, logs, 0.0), axis=1, keepdims=True),
                ],
                axis=0,
            )
            probs = jnp.exp(pair_scores(stacked, keys, info[LIMIT + j]) - log_total)
            dprobs = nt(dcs, values)
            inner = jnp.sum(probs * dprobs, axis=1, keepdims=True)
            dscores = (probs * (dprobs - inner)).astype(BF)
            text, layout = unstack_heads(nn(dscores, keys), scaled)
            dq[rows, text_lanes] = text.astype(BF)
            ql_acc[rows, group_lanes] += layout
            both = tn(dscores, stacked)
            k_acc[keys_at, text_lanes] += both[:, :LANES]
            kl_acc[keys_at, group_lanes] += both[:, LANES:]
            both = tn(probs.astype(BF), dcs)
            v_acc[keys_at, text_lanes] += both[:, :LANES]
            vl_acc[keys_at, group_lanes] += both[:, LANES:]
        return carry

    lax.fori_loop(0, HEADS // 2, one_pair, 0, unroll=3)
    middle = pl.ds(pad, window)
    dk[middle, :] = k_acc[...].astype(BF)
    dv[middle, :] = v_acc[...].astype(BF)
    dk_l[middle, :] = kl_acc[...].astype(BF)
    dv_l[middle, :] = vl_acc[...].astype(BF)
    dq_l[...] = ql_acc[...].astype(BF)


def key_value_grad(info, at, rows_out, wt, wl, dk, dv, dk_l, dv_l):
    width, wide = dk.shape[1], dk_l.shape[1]
    rows = pl.ds(pl.multiple_of(info[SHIFT] + at, LANES), rows_out)
    text = nt(dk[rows, :], wt[:, width : 2 * width]) + nt(dv[rows, :], wt[:, 2 * width :])
    layout = nt(wl[:, wide : 2 * wide], dk_l[rows, :]) + nt(wl[:, 2 * wide :], dv_l[rows, :])
    return text, layout


def store_packed(out, text, layout):
    own_rows = text.shape[0]
    half = layout.shape[0] // 2
    out[:own_rows, :] = text.astype(BF)
    out[own_rows:, :own_rows] = layout[:half].astype(BF)
    out[own_rows:, own_rows:] = layout[half:].astype(BF)


def sides_kernel(info, wt, wl, dk, dv, dk_l, dv_l, left, right):
    own_rows = left.shape[0] * 4 // 5
    for side, shift in ((left, 0), (right, 2 * own_rows)):
        store_packed(side, *key_value_grad(info, shift, own_rows, wt, wl, dk, dv, dk_l, dv_l))


def own_kernel(info, wt, wl, dq, dk, dv, dq_l, dk_l, dv_l, dfirst_t, dfirst_lt, left, right, out):
    own_rows, width = dq.shape
    wide = dq_l.shape[1]
    half = dfirst_lt.shape[0] // 2
    text, layout = key_value_grad(info, own_rows, own_rows, wt, wl, dk, dv, dk_l, dv_l)
    text = dfirst_t[...] + text + nt(dq[...], wt[:, :width])
    layout = dfirst_lt[...] + layout + nt(wl[:, :wide], dq_l[...])
    got = left[...].astype(F32) + right[...].astype(F32)
    text = text + got[:own_rows]
    layout = layout + jnp.concatenate([got[own_rows:, :own_rows], got[own_rows:, own_rows:]], axis=0)
    store_packed(out, text, layout)


def input_final_kernel(info, own, l1, l2, l3, r1, r2, r3, text, layout):
    own_rows, half = own.shape[0] * 4 // 5, layout.shape[0] // 2
    for distance, rows in ((0, own), (-1, l1), (-2, l2), (-3, l3), (1, r1), (2, r2), (3, r3)):
        group = info[GROUP] + distance

        @pl.when((group >= 0) & (group < 4))
        def _():
            at = pl.ds(pl.multiple_of(group * own_rows, LANES), own_rows)
            text[at, :] = rows[:own_rows, :].astype(F32)
            layout[:half, at] = rows[own_rows:, :own_rows].astype(F32)
            layout[half:, at] = rows[own_rows:, own_rows:].astype(F32)


def extras(
    info, xlt, dq, dv, dq_l, dk_l, dv_l, cl, db_l, sums_a, sums_b, hsums, sums_al, sums_bl, hsums_l, extra, small,
):
    own_rows = dq.shape[0]
    wide = dq_l.shape[1]
    width_l = xlt.shape[0]
    window = dk_l.shape[0] - 2 * own_rows
    own = pl.ds(pl.multiple_of(info[OWN], LANES), own_rows)
    seen = pl.ds(pl.multiple_of(info[WINDOW], LANES), window)
    middle = pl.ds(own_rows, window)
    extra[width_l:, :] = jnp.zeros((extra.shape[0] - width_l, extra.shape[1]), BF)
    extra[:width_l, :wide] = nn(xlt[:, own], dq_l[...]).astype(BF)
    extra[:width_l, wide : 2 * wide] = nn(xlt[:, seen], dk_l[middle, :]).astype(BF)
    extra[:width_l, 2 * wide : 3 * wide] = nn(xlt[:, seen], dv_l[middle, :]).astype(BF)
    extra[width_l : 2 * width_l, :width_l] = tn(cl[...], db_l[...]).astype(BF)
    small[...] = jnp.zeros_like(small)
    small[0:4, :] = sums_a[...]
    small[4:8, :] = sums_b[...]
    small[8:9, :] = column_sum(dq[...])
    small[9:10, :] = column_sum(dv[middle, :])
    small[16:20, :width_l] = sums_al[...]
    small[20:24, :width_l] = sums_bl[...]
    small[24:25, :wide] = column_sum(dq_l[...])
    small[25:26, :wide] = column_sum(dv_l[middle, :])
    for s in range(4):
        group = lax.rem(info[GROUP] + s, 4)
        small[pl.ds(12 + group, 1), :] = hsums[s]
        small[pl.ds(28 + group, 1), :width_l] = hsums_l[s]
    extra[2 * width_l : 2 * width_l + 32, :] = small[...].astype(BF)


def copied_grads(info, xt, dq, dk, dv, ct, db, half, store):
    own_rows = dq.shape[0]
    window = dk.shape[0] - 2 * own_rows
    own = pl.ds(pl.multiple_of(info[OWN], LANES), own_rows)
    seen = pl.ds(pl.multiple_of(info[WINDOW], LANES), window)
    middle = pl.ds(own_rows, window)
    for block in range(4):
        if block == 0:
            grad = tn(xt[own, half], dq[...])
        elif block == 1:
            grad = tn(xt[seen, half], dk[middle, :])
        elif block == 2:
            grad = tn(xt[seen, half], dv[middle, :])
        else:
            grad = tn(ct[:, half], db[...])
        store(block, info[SLOT + block], grad)


def copied_send_kernel(
    info, xt, dq, dk, dv, ct, db, xlt, dq_l, dk_l, dv_l, cl, db_l, sums_a, sums_b, hsums, sums_al, sums_bl, hsums_l,
    send, extra, small,
):
    half = pl.ds(pl.multiple_of(info[HALF + 1], LANES), 384)
    extras(info, xlt, dq, dv, dq_l, dk_l, dv_l, cl, db_l, sums_a, sums_b, hsums, sums_al, sums_bl, hsums_l, extra, small)

    def store(block, slot, grad):
        send[slot, :384] = grad.astype(BF)
        send[slot, 384:] = extra[pl.ds(pl.multiple_of(128 * block + info[HALF + 1] // 6, 64), 64), :]

    copied_grads(info, xt, dq, dk, dv, ct, db, half, store)


def copied_keep_kernel(info, xt, dq, dk, dv, ct, db, extra, recv, next_a, keep_a, next_b, keep_b, total):
    half = pl.ds(pl.multiple_of(info[HALF], LANES), 384)

    def store(block, slot, grad):
        more = pl.ds(pl.multiple_of(128 * block + info[HALF] // 6, 64), 64)
        total[slot, :384] = (grad + recv[slot, :384].astype(F32)).astype(BF)
        total[slot, 384:] = (extra[more, :].astype(F32) + recv[slot, 384:].astype(F32)).astype(BF)

    copied_grads(info, xt, dq, dk, dv, ct, db, half, store)
    for slot in range(4):
        for rel in range(4):
            x_part, y_part = rel % 2, rel // 2
            first, second = (x_part, y_part) if slot < 2 else (y_part, x_part)
            out = ((keep_a, next_a), (keep_b, next_b))[slot // 2][first].at[second, slot % 2]
            out[:96] = total[slot, pl.ds(pl.multiple_of(info[PIECE + rel], 32), 96), :]
            out[96:] = total[slot, pl.ds(pl.multiple_of(384 + info[PIECE + rel] // 6, EXTRA), EXTRA), :]


SM = pl.BlockSpec(memory_space=pltpu.SMEM)
VM = pl.BlockSpec(memory_space=pltpu.VMEM)
HB = pl.BlockSpec(memory_space=pl.ANY)


class InHbm:
    def __init__(self, dims, dtype=BF):
        self.shape, self.dtype = dims, dtype


def vmem_of(outs, scratch):
    held = list(outs) + [v for v in scratch if str(v.memory_space) == "vmem"]
    return int(1.1 * sum(math.prod(v.shape) * jnp.dtype(v.dtype).itemsize for v in held)) + (MARGIN << 20)


def call(name, kernel, operands, outs, scratch=(), after=(), in_hbm=0, final=False):
    operands = tuple(operands)
    outs = tuple(outs) + (shape((8, LANES), F32),)
    specs = [HB] * len(after) + [SM] + [VM] * (len(operands) - 1 - in_hbm) + [pl.BlockSpec(memory_space=pltpu.HBM)] * in_hbm
    limit = vmem_of(outs if final else (), scratch)
    operands = tuple(after) + operands
    at = len(operands) + len(outs) - 1

    def with_token(*refs):
        kernel(*refs[len(after) : at], *refs[at + 1 :])
        refs[at][...] = jnp.zeros_like(refs[at])

    return pl.pallas_call(
        with_token,
        out_shape=tuple(shape(o.shape, o.dtype) for o in outs),
        in_specs=specs,
        out_specs=[HB if isinstance(o, InHbm) else VM for o in outs],
        scratch_shapes=list(scratch),
        cost_estimate=pl.CostEstimate(flops=int(MICROSECONDS[name] * PER_MICROSECOND), bytes_accessed=0, transcendentals=0),
        compiler_params=pltpu.CompilerParams(vmem_limit_bytes=limit),
        name=name,
    )(*operands)


def shape(dims, dtype=BF):
    return jax.ShapeDtypeStruct(dims, dtype)


def flip(planes, bit):
    return [(i, i ^ bit) for i in range(planes)]


def gate(values, *tokens):
    outs = pl.pallas_call(
        lambda *refs: None,
        out_shape=tuple(shape(v.shape, v.dtype) for v in values),
        in_specs=[HB] * (len(values) + len(tokens)),
        out_specs=[HB] * len(values),
        input_output_aliases={i: i for i in range(len(values))},
        cost_estimate=pl.CostEstimate(flops=0, bytes_accessed=0, transcendentals=0),
        compiler_params=pltpu.CompilerParams(vmem_limit_bytes=1 << 20),
        name="gate",
    )(*values, *tokens)
    return list(outs)


def around(planes):
    return lambda v, bit: lax.ppermute(v, "dp", flip(planes, bit))


def forward(piece, by_x, by_y, planes, split, mid=None, token=None):
    across, parts = around(planes), piece.shape[0]
    if split == "x":
        return [(across(by_x, Y), 3, 0, parts)]
    if split == "y":
        return [(across(by_y, X), 3, 0, parts)]
    mid = mid or parts // 2
    low, high = across(by_x[:mid], Y), across(by_y[mid:], X)
    if token is not None:
        low, high = gate((low, high), token)
    return [(low, 3, 0, mid), (high, 3, mid, parts)]


def to_core(held, planes):
    across = around(planes)
    held = held + [(across(v, CORE), rel + 4, low, high) for v, rel, low, high in held]
    return [h[0] for h in held], tuple(h[1:] for h in held)


def spread(piece, planes, mid=None, token=None):
    across, parts = around(planes), piece.shape[0]
    by_x, by_y = across(piece, X), across(piece, Y)
    held = [(piece, 0, 0, parts), (by_x, 1, 0, parts), (by_y, 2, 0, parts)]
    return to_core(held + forward(piece, by_x, by_y, planes, "half", mid, token), planes)


def per_device(
    text_input, layout_input, block_starts, intersection_flags, text_cotangent, layout_cotangent,
    text_project, text_biases, text_dense, text_gains, text_shifts, text_widen, text_hidden_bias, text_narrow,
    layout_project, layout_biases, layout_dense, layout_gains, layout_shifts, layout_widen, layout_hidden_bias,
    layout_narrow,
):
    blocks, length = intersection_flags.shape
    total = blocks * length
    groups = lax.axis_size("tensor")
    planes = lax.axis_size("dp")
    own = total // groups
    tiles = own // LANES
    width = text_input.shape[1]
    width_l = layout_input.shape[1]
    wide = 2 * LANES
    window = 2 * length
    padded = window + 2 * own
    hid = text_narrow.shape[0]
    hid_l = layout_narrow.shape[0]
    piece = width // PIECES
    t = lax.axis_index("tensor").astype(jnp.int32)
    me = lax.axis_index("dp").astype(jnp.int32)
    core, x_bit, y_bit = me & 1, (me >> 1) & 1, (me >> 2) & 1

    def row_of(rc, rx, ry):
        return 4 * piece * (core ^ rc) + piece * ((x_bit ^ rx) + 2 * (y_bit ^ ry))

    flagged = jnp.sum(intersection_flags, axis=1, dtype=jnp.int32)
    base = jnp.minimum((t * own) // length, blocks - 2)
    tile_rows = t * own + LANES * jnp.arange(tiles, dtype=jnp.int32)
    tile_block = tile_rows // length
    pick = tile_block[:, None] == jnp.arange(blocks, dtype=jnp.int32)[None, :]
    limit = DOC - jnp.sum(jnp.where(pick, block_starts[None, :], 0), axis=1)
    flags_of = jnp.sum(jnp.where(pick, flagged[None, :], 0), axis=1)
    info = jnp.concatenate(
        [
            jnp.stack([t * own, base * length, t * own - base * length]),
            tile_block - base,
            limit,
            flags_of,
            tile_rows - tile_block * length,
            jnp.stack(
                [t, 4 * piece * core, 4 * piece * (1 - core)]
                + [row_of(0, rx, ry) - 4 * piece * core for ry in (0, 1) for rx in (0, 1)]
                + [(b - t) % groups for b in range(4)]
            ),
        ]
    ).astype(jnp.int32)

    shift_from = lambda k: [(i, (i - k) % groups) for i in range(groups)]
    shift_to = lambda k: [(i, (i + k) % groups) for i in range(groups)]
    across = around(planes)
    row = row_of(0, 0, 0)
    mine, packed_up = call(
        "pack", pack_kernel,
        (jnp.zeros((1,), jnp.int32),
         jnp.concatenate([lax.dynamic_slice_in_dim(v, row, piece, 0) for v in (text_widen, text_narrow)], axis=0),
         jnp.concatenate([lax.dynamic_slice_in_dim(v, row // 4, piece // 4, 0) for v in (layout_widen, layout_narrow)], axis=0),
         text_hidden_bias[None, :], layout_hidden_bias[None, :]),
        (shape((2 * piece + EXTRA, width)),),
        scratch=(pltpu.VMEM((EXTRA, width), F32),),
    )
    from_group = lambda v, k: lax.ppermute(v, "tensor", shift_from(k))
    come = {k: from_group(mine, k) for k in (1, 3)}

    xlt = layout_input.T
    qt, kt, vt, ql, kl, vl, xl_own, wl, projected = call(
        "project", project_kernel,
        (info, text_input, xlt, text_project, layout_project, text_biases, layout_biases),
        (shape((own, width)), shape((window, width)), shape((window, width)),
         shape((own, wide)), shape((window, wide)), shape((window, wide)),
         shape((own, width_l)), shape((width_l, 3 * wide))),
        after=(packed_up,),
    )
    mine_again, come[1], come[3] = gate((mine, come[1], come[3]), projected)
    come[2] = from_group(mine_again, 2)
    by_x, by_y = {}, {}
    for k in (1, 3):
        by_x[k], by_y[k] = across(come[k], X), across(come[k], Y)
    ct, cl, lse, attended = call(
        "attend", attend_kernel,
        (info, qt, kt, vt, ql, kl, vl),
        (shape((own, width)), shape((own, width_l)), shape((own, LANES), F32)),
        scratch=(pltpu.VMEM((own, wide), F32),),
    )
    by_x[1], by_y[1], by_x[3], by_y[3], *came = gate(
        (by_x[1], by_y[1], by_x[3], by_y[3], come[1], come[2], come[3]), attended
    )
    come = dict(zip((1, 2, 3), came))
    forwarded = {k: forward(come[k], by_x[k], by_y[k], planes, {1: "x", 3: "y"}[k]) for k in (1, 3)}
    first_t, first_l, low_t, low_l, normed_l, active0, slope0, total_t, first_done = call(
        "first_norm", first_norm_kernel,
        (info, text_input, xl_own, ct, cl, text_dense, layout_dense, text_biases, layout_biases,
         text_gains, text_shifts, layout_gains, layout_shifts, text_widen, mine, text_narrow),
        (shape((own, width), F32), shape((own, width_l), F32), shape((own, width)), shape((own, width_l)),
         shape((own, width_l), F32), shape((own, hid)), shape((own, hid), F32), shape((own, width), F32)),
    )
    last_x, last_y = across(come[2], X), across(come[2], Y)
    *both, come[1], come[3], by_x[1], by_y[1], by_x[3], by_y[3] = gate(
        (forwarded[1][0][0], forwarded[3][0][0], come[1], come[3], by_x[1], by_y[1], by_x[3], by_y[3]), first_done
    )
    shards = {}
    for k, array in zip((1, 3), both):
        parts = come[k].shape[0]
        held = [(come[k], 0, 0, parts), (by_x[k], 1, 0, parts), (by_y[k], 2, 0, parts), (array, 3, 0, parts)]
        shards[k] = to_core(held, planes)
    by_x[2], by_y[2] = last_x, last_y
    last = forward(come[2], by_x[2], by_y[2], planes, "half", 96)
    actives, slopes, shard_weights, layouts, shard_done = {0: active0}, {0: slope0}, {}, {}, {}
    for k in (1, 3):
        arrays, plan = shards[k]
        actives[k], slopes[k], total_t, shard_weights[k], layouts[k], shard_done[k] = call(
            "shard", functools.partial(shard_kernel, plan),
            (info, low_t, total_t, *arrays),
            (shape((own, hid)), shape((own, hid), F32), shape((own, width), F32), shape((2, width, hid)),
             shape((width_l, 2 * wide))),
            scratch=(pltpu.VMEM((width_l, 2 * wide), F32),),
        )
    last = [(v,) + f[1:] for v, f in zip(gate([f[0] for f in last], shard_done[3]), last)]
    parts = come[2].shape[0]
    shards[2] = to_core([(come[2], 0, 0, parts), (by_x[2], 1, 0, parts), (by_y[2], 2, 0, parts)] + last, planes)
    arrays, plan = shards[2]
    rows_a = piece + EXTRA
    outs = call(
        "turn", functools.partial(turn_kernel, plan),
        (info, low_t, total_t, text_gains, text_shifts, text_cotangent, text_widen, text_narrow,
         slopes[0], slopes[1], slopes[3], actives[0], actives[1], actives[3],
         low_l, normed_l, layout_gains, layout_shifts, layout_cotangent.T, first_t, first_l, text_dense, layout_dense,
         layout_widen, layout_narrow, layouts[1], layouts[3],
         mine, come[1], come[3], shard_weights[1], shard_weights[3], *arrays),
        (shape((own, width)), shape((own, width)), shape((groups, own, hid)),
         shape((4, width), F32), shape((groups, 1, hid), F32), shape((own, hid)),
         shape((width_l, own)), shape((4, width_l), F32), shape((groups, 1, hid_l), F32), shape((groups, 128, width)),
         shape((own, width), F32), shape((own, width)), shape((own, width)), shape((4, width), F32),
         shape((width_l, own), F32), shape((own, width_l)), shape((own, wide)), shape((4, width_l), F32)),
        scratch=(pltpu.VMEM((2, width, hid), BF), pltpu.VMEM((own, hid), F32), pltpu.VMEM((own, width), F32),
                 pltpu.VMEM((groups, own, hid_l), F32), pltpu.VMEM((groups, own, hid_l), BF),
                 pltpu.VMEM((groups, own, hid_l), BF), pltpu.VMEM((own, width_l), BF), pltpu.VMEM((own, width_l), BF),
                 pltpu.VMEM((own, width_l), F32), pltpu.VMEM((own, width_l), F32), pltpu.VMEM((width_l, 2 * wide), F32)),
    )
    result_t, dout_t, dhid_t, sums_t, hsums_t, actives[2] = outs[:6]
    result_lt, sums_l, hsums_l, pack = outs[6:10]
    dfirst_t, db_t, dc_t, low_sums_t, dfirst_lt, db_l, dc_l, low_sums_l, turned = outs[10:]

    def across_planes(value):
        bit = PIECES
        while bit < planes:
            value = add(value, across(value, bit))
            bit *= 2
        return value

    ffn_in = (*(actives[k] for k in range(4)), dout_t, low_t, dhid_t)
    send_a, send_b, ffn_sent = call(
        "ffn_send", ffn_send_kernel, (info, *ffn_in, pack),
        (shape((groups, 4 * rows_a, width)), shape((groups, 4 * piece, width))),
    )
    recv_a, recv_b = across(send_a, CORE), across(send_b, CORE)
    dq, dk, dv, dq_l, dk_l, dv_l, attended_back = call(
        "attend_back", attend_back_kernel,
        (info, qt, kt, vt, ql, kl, vl, dc_t, dc_l, lse),
        (shape((own, width)), shape((padded, width)), shape((padded, width)),
         shape((own, wide)), shape((padded, wide)), shape((padded, wide))),
        scratch=(pltpu.VMEM((window, width), F32), pltpu.VMEM((window, width), F32),
                 pltpu.VMEM((window, wide), F32), pltpu.VMEM((window, wide), F32), pltpu.VMEM((own, wide), F32)),
        after=(ffn_sent,),
    )
    next_a, next_b, keep_a, keep_b, kept = call(
        "ffn_keep", ffn_keep_kernel, (info, *ffn_in, recv_a, recv_b, pack),
        (shape((2, groups, rows_a, width)), shape((2, groups, piece, width))) * 2,
        scratch=(pltpu.VMEM((4 * rows_a, width), BF), pltpu.VMEM((4 * piece, width), BF)), after=(attended_back,),
    )
    recv_a, recv_b = across(next_a, X), across(next_b, Y)
    copied_in = (text_input, dq, dk, dv, ct, db_t)
    send, extra, sent = call(
        "copied_send", copied_send_kernel,
        (info,) + copied_in + (xlt, dq_l, dk_l, dv_l, cl, db_l, sums_t, low_sums_t, hsums_t, sums_l, low_sums_l, hsums_l),
        (shape((groups, 4 * rows_a, width)), shape((4 * 128, width))),
        scratch=(pltpu.VMEM((32, width), F32),), after=(kept,),
    )
    packed = shape((own + own // 4, width))
    left, right, sided = call(
        "sides", sides_kernel, (info, text_project, wl, dk, dv, dk_l, dv_l), (packed, packed), after=(sent,)
    )
    from_right = lax.ppermute(left, "tensor", [(i + 1, i) for i in range(groups - 1)])
    from_left = lax.ppermute(right, "tensor", [(i, i + 1) for i in range(groups - 1)])

    recv = across(send, CORE)
    copied_next_a, copied_keep_a, copied_next_b, copied_keep_b, copied_kept = call(
        "copied_keep", copied_keep_kernel, (info,) + copied_in + (extra, recv),
        (shape((2, 2, rows_a, width)),) * 4,
        scratch=(pltpu.VMEM((groups, 4 * rows_a, width), BF),), after=(sided,),
    )
    copied_recv_a, copied_recv_b = across(copied_next_a, X), across(copied_next_b, Y)
    own_sum, owned = call(
        "own", own_kernel,
        (info, text_project, wl, dq, dk, dv, dq_l, dk_l, dv_l, dfirst_t, dfirst_lt, from_right, from_left),
        (packed,), after=(copied_kept,),
    )
    step_right = lambda v, far: lax.ppermute(v, "tensor", [(i, i + 1) for i in range(far, groups - 1)])
    step_left = lambda v, far: lax.ppermute(v, "tensor", [(i, i - 1) for i in range(groups - 1 - far, 0, -1)])
    lefts, rights = [step_right(own_sum, 0)], [step_left(own_sum, 0)]
    for far in (1, 2):
        lefts.append(step_right(lefts[-1], far))
        rights.append(step_left(rights[-1], far))
    to_group = lambda v, k: lax.ppermute(v, "tensor", shift_to(k))
    copied_next_a, copied_keep_a = add_split(copied_keep_a, copied_recv_a, zero_of(recv_a))
    copied_next_b, copied_keep_b = add_split(copied_keep_b, copied_recv_b, zero_of(recv_b))
    copied_recv_a, copied_recv_b = across(copied_next_a, Y), across(copied_next_b, X)
    *parts, copied_spreaded = call(
        "copied_spread", copied_spread_kernel, (info, copied_keep_a, copied_recv_a, copied_keep_b, copied_recv_b),
        (shape((rows_a, width)),) * 4,
        after=(lefts[0], rights[0]),
    )
    parts = [parts[0]] + [to_group(parts[k], k) for k in (1, 2, 3)]
    summed = across_planes(add(*parts, zero_of(lefts[1]), zero_of(rights[1])))
    next_a, keep_a = add_split(keep_a, recv_a, zero_of(lefts[1]), zero_of(rights[1]))
    next_b, keep_b = add_split(keep_b, recv_b, zero_of(lefts[1]), zero_of(rights[1]))
    recv_a, recv_b = across(next_a, Y), across(next_b, X)
    every = [summed] + [from_group(summed, k) for k in (1, 2, 3)]
    ffn_parts, _ = call(
        "ffn_spread", ffn_spread_kernel, (info, keep_a, recv_a, keep_b, recv_b),
        (shape((groups, rows_a + piece, width)),), after=tuple(every[1:]),
    )
    ffn_grads = lax.psum_scatter(ffn_parts, "tensor", scatter_dimension=0, tiled=False)
    every = jnp.stack(every)
    arrays, plan = spread(every, planes)
    vectors = lambda w, h: (shape((4, w), F32), shape((2, w), F32), shape((2, w), F32), shape((1, h), F32))
    outs = call(
        "copied_final", functools.partial(copied_final_kernel, plan), (info, *arrays),
        (shape((width, 3 * width), F32), shape((width, width), F32),
         shape((width_l, 3 * width_l), F32), shape((width_l, width_l), F32)) + vectors(width, hid) + vectors(width_l, hid_l),
        scratch=(pltpu.VMEM((4 * 128, width), F32),), final=True,
    )
    text_grad, layout_grad_t, given = call(
        "input_final", input_final_kernel, (info, own_sum, *lefts, *rights),
        (shape((total, width), F32), shape((width_l, total), F32)), after=(outs[-1],), final=True,
    )
    ffn_grads = add(across_planes(ffn_grads), zero_of(outs[-1]))
    ffn_arrays, ffn_plan = spread(ffn_grads, planes, rows_a, given)
    g_narrow, g_widen, g_narrow_l, g_widen_l, _ = call(
        "ffn_final", functools.partial(ffn_final_kernel, ffn_plan), (info, *ffn_arrays),
        (shape((hid, width), F32), shape((width, hid), F32), shape((hid_l, width_l), F32), shape((width_l, hid_l), F32)),
        scratch=(pltpu.VMEM((128, width), F32),), final=True,
    )
    g_project, g_dense, g_project_l, g_dense_l = outs[:4]
    bias_t, gain_t, shift_t, hb_t, bias_l, gain_l, shift_l, hb_l = outs[4:12]
    return (
        result_t, result_lt.T, text_grad, layout_grad_t.T,
        g_project, bias_t, g_dense, gain_t, shift_t, g_widen, hb_t[0], g_narrow,
        g_project_l, bias_l, g_dense_l, gain_l, shift_l, g_widen_l, hb_l[0], g_narrow_l,
    )


def solution(mesh):
    rows = P(("dp", "tensor"), None)
    weights = (P(), P(), P(), P(), P(), P(None, "tensor"), P("tensor"), P("tensor", None))
    return jax.shard_map(
        per_device,
        mesh=mesh,
        in_specs=(P("dp", None), P("dp", None), P("dp"), P("dp", None), rows, rows) + weights + weights,
        out_specs=(rows, rows, P("dp", None), P("dp", None)) + weights + weights,
        check_vma=False,
    )
```
